128 devices in a mesh: cols: 8 (over y, core), rows: 16 (over z, x).
Axes of the slice: x: 4, y: 4, z: 4, core: 2. Of those that a mesh axis runs over, the one named last changes fastest.
Arguments:
- sensitivity: float32 [8, 6144, 2048], P('cols', 'rows'), may hold values from -470 to 470, as said below
Outputs:
- rotated: float32 [8, 6144, 2048], P(None, 'rows', 'cols')
- frame: float32 [2048, 2048], P('rows', 'cols')
- column_scale: float32 [2048], P('cols')
The draws below stay inside these ranges and needn't reach their ends.
Inputs may be any that keep to these rules, and one draw needn't show every extreme that they name: `sensitivity`: Real-valued sensitivities.
All inputs are finite; a program needn't handle non-finite values.
Results may differ from the reference program's by a relative error of at most 0.00018.
Values sent between devices are 32-bit elements; how exact they have to be, the bound alone decides.
No kernel may reach another device: no remote copies, remote signals or barrier semaphores. Data moves between devices by JAX's collectives and lax.ppermute only.
A program may use at most 64 MiB of HBM per device.

```python
import math
import jax
import jax.numpy as jnp
from jax import lax

N = 2048
SUB = 384
ROUNDS = 4
BLOCK = 128
PAIR = 256
N_COLS = 8
N_ROWS = 16


def draw_sensitivity(key, part):
    first_key, second_key, third_key = jax.random.split(key, 3)
    group_rows = SUB * N_ROWS
    shape = (N_COLS, group_rows, N)
    base = jnp.clip(jax.random.normal(first_key, shape, jnp.float32), -4.0, 4.0)
    position = (jnp.arange(group_rows).astype(jnp.float32) / group_rows)[None, :, None]
    rough = jnp.exp(jax.random.uniform(second_key, (N_COLS, group_rows, 1), jnp.float32, 0.0, math.log(4.0)))
    column_gain = jnp.exp(jax.random.uniform(third_key, (1, 1, N), jnp.float32, math.log(0.3), math.log(3.0)))
    row_gain = (1.0 + 2.0 * position) * rough
    coupling = -0.8 + 1.6 * position
    distant = 0.6 - 0.3 * position
    following = jnp.roll(base, -1, axis=2)
    partner_index = (jnp.arange(N) * 37 + 11) % N
    partner = jnp.take(base, partner_index, axis=2)
    return row_gain * column_gain * (base + coupling * following + distant * partner)


def setup_inputs(seed: int = 0) -> dict:
    splits = jax.random.split(jax.random.key(seed), 2)
    sensitivity = draw_sensitivity(jax.random.fold_in(splits[1], 71), 0)
    return {"sensitivity": sensitivity}


def product(left, right):
    return jnp.dot(left.astype(jnp.float32), right.astype(jnp.float32), precision=lax.Precision.HIGHEST, preferred_element_type=jnp.float32)

def inner_gram(left, right):
    return lax.dot_general(left.astype(jnp.float32), right.astype(jnp.float32), (((0,), (0,)), ((), ())), precision=lax.Precision.HIGHEST, preferred_element_type=jnp.float32)

def cayley_rotation(gram):
    order = gram.shape[0]
    diagonal = jnp.diagonal(gram)
    spread = diagonal[None, :] - diagonal[:, None]
    totals = diagonal[None, :] + diagonal[:, None]
    skew = gram * spread / (2.0 * spread * spread + 0.5 * totals * totals)
    identity = jnp.eye(order, dtype=jnp.float32)
    raised = identity + skew
    numerator = product(raised, raised)
    denominator = identity - product(skew, skew)
    factor = jnp.linalg.cholesky(denominator)
    partial_solve = lax.linalg.triangular_solve(factor, numerator.T, left_side=True, lower=True)
    solved = lax.linalg.triangular_solve(factor, partial_solve, left_side=True, lower=True, transpose_a=True)
    return solved.T

def rotate_pair(blocks):
    upper_part, lower_part, basis_up, basis_low = blocks
    paired = jnp.concatenate([upper_part, lower_part], axis=1)
    weights = cayley_rotation(inner_gram(paired, paired))
    turned = product(paired, weights)
    framed = product(jnp.concatenate([basis_up, basis_low], axis=1), weights)
    return (turned[:, :BLOCK], turned[:, BLOCK:], framed[:, :BLOCK], framed[:, BLOCK:])

def reference(sensitivity):
    total_rows = sensitivity.shape[0] * sensitivity.shape[1]
    matrix = sensitivity.reshape(total_rows, N_COLS, PAIR)
    slabs = jnp.transpose(matrix, (1, 0, 2))
    upper = slabs[:, :, :BLOCK]
    lower = slabs[:, :, BLOCK:]
    basis = jnp.transpose(jnp.eye(N, dtype=jnp.float32).reshape(N, N_COLS, PAIR), (1, 0, 2))
    basis_upper = basis[:, :, :BLOCK]
    basis_lower = basis[:, :, BLOCK:]
    for sweep_round in range(ROUNDS):
        if sweep_round > 0:
            lower = jnp.roll(lower, 1, axis=0)
            basis_lower = jnp.roll(basis_lower, 1, axis=0)
        upper, lower, basis_upper, basis_lower = lax.map(rotate_pair, (upper, lower, basis_upper, basis_lower))
    turned_all = jnp.concatenate([upper, lower], axis=2)
    squares = lax.optimization_barrier(jnp.sum(turned_all * turned_all, axis=1)).reshape(N)
    column_scale = jnp.sqrt(squares / total_rows)
    rotated = jnp.transpose(turned_all, (1, 0, 2)).reshape(N_COLS, total_rows // N_COLS, N)
    frame = jnp.transpose(jnp.concatenate([basis_upper, basis_lower], axis=2), (1, 0, 2)).reshape(N, N)
    return (rotated, frame, column_scale)
```

```python
import jax
import jax.numpy as jnp
from jax import lax
from jax.experimental import pallas as pl
from jax.experimental.pallas import tpu as pltpu
from jax.sharding import PartitionSpec as P

ROUNDS = 4
BLOCK = 128
PAIR = 256
SIDE = 4
ROWS = 16
COLS = 8
F32 = jnp.float32
VMEM_LIMIT = 48 * 1024 * 1024

TURN_CORE = [(c, c ^ 1) for c in range(COLS)]
NEXT_SLOT = [(c, (c + 1) % COLS) for c in range(COLS)]
NEXT_CHIP = [(c, (c + 2) % COLS) for c in range(COLS)]
ODD_TO_EVEN = [(c, (c + 1) % COLS) for c in range(1, COLS, 2)]
ODD_TO_ODD = [(c, (c + 2) % COLS) for c in range(1, COLS, 2)]
SAME_CORE = [[c for c in range(COLS) if c % 2 == k] for k in range(2)]
ALONG_X = [[(r, r - r % SIDE + (r + k) % SIDE) for r in range(ROWS)] for k in range(1, SIDE)]
ALONG_Z = [[(r, (r + SIDE * k) % ROWS) for r in range(ROWS)] for k in range(1, SIDE)]


def mm(left, right):
    return jnp.dot(left, right, precision=lax.Precision.HIGHEST, preferred_element_type=F32)


def mm_t(left, right):
    return lax.dot_general(
        left, right, (((0,), (0,)), ((), ())), precision=lax.Precision.HIGHEST, preferred_element_type=F32
    )


def call(kernel, grid, in_specs, out_specs, out_shape, scalars=0, scratch=(), flops=0, nbytes=0):
    return pl.pallas_call(
        kernel,
        grid_spec=pltpu.PrefetchScalarGridSpec(
            num_scalar_prefetch=scalars,
            grid=grid,
            in_specs=in_specs,
            out_specs=out_specs,
            scratch_shapes=list(scratch),
        ),
        out_shape=out_shape,
        compiler_params=pltpu.CompilerParams(vmem_limit_bytes=VMEM_LIMIT),
        cost_estimate=pl.CostEstimate(flops=flops, bytes_accessed=nbytes, transcendentals=0),
    )


def shape(*dims):
    return jax.ShapeDtypeStruct(dims, F32)


def whole(*dims):
    return pl.BlockSpec(dims, lambda *_: (0,) * len(dims))


def pack_kernel(x_ref, out_ref):
    out_ref[0, 0, 0] = x_ref[:, :BLOCK]
    out_ref[0, 0, 1] = x_ref[:, BLOCK:]


def pack(x):
    rows = x.shape[0]
    return call(
        pack_kernel,
        (SIDE, 3),
        [pl.BlockSpec((rows, PAIR), lambda y, j: (0, (2 * y + jnp.where(j == 2, COLS - 1, j)) % COLS))],
        pl.BlockSpec((1, 1, 2, rows, BLOCK), lambda y, j: (y, j, 0, 0, 0)),
        shape(SIDE, 3, 2, rows, BLOCK),
        nbytes=2 * 4 * SIDE * 3 * rows * PAIR,
    )(x)


def gram_kernel(core_ref, x_ref, keep_ref, send_ref):
    @pl.when(pl.program_id(0) == 0)
    def _():
        keep_ref[...] = jnp.zeros_like(keep_ref)
        send_ref[...] = jnp.zeros_like(send_ref)

    grams = []
    for slot in range(2):
        paired = jnp.concatenate([x_ref[0, slot, 0], x_ref[0, slot, 1]], axis=1)
        grams.append(mm_t(paired, paired))
    first = core_ref[0] == 0
    keep_ref[...] += jnp.where(first, grams[0], grams[1])
    send_ref[...] += jnp.where(first, grams[1], grams[0])


def first_grams(core, blocks):
    rows = blocks.shape[3]
    return call(
        gram_kernel,
        (SIDE,),
        [pl.BlockSpec((1, 2, 2, rows, BLOCK), lambda i, c: (i, 0, 0, 0, 0))],
        [whole(PAIR, PAIR)] * 2,
        [shape(PAIR, PAIR)] * 2,
        scalars=1,
        flops=2 * 6 * 2 * SIDE * rows * PAIR * PAIR,
        nbytes=4 * SIDE * rows * 2 * PAIR,
    )(core, blocks)


def rotation_of(gram, x_ref, r_ref):
    rows = lax.broadcasted_iota(jnp.int32, (PAIR, PAIR), 0)
    columns = lax.broadcasted_iota(jnp.int32, (PAIR, PAIR), 1)
    eye = (rows == columns).astype(F32)
    on_diagonal = gram * eye
    across = jnp.sum(on_diagonal, axis=0, keepdims=True)
    down = jnp.sum(on_diagonal, axis=1, keepdims=True)
    spread = across - down
    totals = across + down
    skew = gram * spread / (2.0 * spread * spread + 0.5 * totals * totals)
    square = mm(skew, skew)
    bound = jnp.max(jnp.sum(jnp.abs(square), axis=0))
    scale = 2.0 / (2.0 + bound)
    x_ref[...] = scale * (eye + skew)
    r_ref[...] = (1.0 - scale) * eye + scale * square

    def step(size):
        left = r_ref[...]
        x = x_ref[...]
        x_ref[...] = x + mm(x, left)
        r_ref[...] = mm(left, left)
        return size * size

    lax.while_loop(lambda size: size > 3e-4, step, bound / (2.0 + bound))
    x = x_ref[...]
    x = x + mm(x, eye - x + mm(skew, x))
    return 2.0 * x - eye


def first_cayley_kernel(gram_ref, weights_ref, x_ref, r_ref):
    weights_ref[...] = rotation_of(gram_ref[...], x_ref, r_ref)


def first_cayley(gram):
    return call(
        first_cayley_kernel,
        (1,),
        [whole(PAIR, PAIR)],
        whole(PAIR, PAIR),
        shape(PAIR, PAIR),
        scratch=[pltpu.VMEM((PAIR, PAIR), F32)] * 2,
        flops=2 * 6 * 8 * PAIR**3,
        nbytes=8 * PAIR * PAIR,
    )(gram)


def cayley_kernel(core_ref, up_ref, low_ref, z0_ref, z1_ref, z2_ref, z3_ref, wm_ref, wo_ref, weights_ref, gram_ref, x_ref, r_ref):
    mixed = (z0_ref[...] + z1_ref[...]) + (z2_ref[...] + z3_ref[...])
    before = jnp.where(core_ref[0] == 0, wm_ref[:, BLOCK:], wo_ref[:, BLOCK:])
    cross = mm(mixed, before)
    gram_ref[:BLOCK, :BLOCK] = up_ref[...]
    gram_ref[:BLOCK, BLOCK:] = cross
    gram_ref[BLOCK:, :BLOCK] = cross.T
    gram_ref[BLOCK:, BLOCK:] = low_ref[...]
    weights_ref[...] = rotation_of(gram_ref[...], x_ref, r_ref)


def cayley(core, up, low, parts, weights_m, weights_o):
    return call(
        cayley_kernel,
        (1,),
        [whole(BLOCK, BLOCK)] * 2 + [whole(BLOCK, PAIR)] * 4 + [whole(PAIR, PAIR)] * 2,
        [whole(PAIR, PAIR)] * 2,
        [shape(PAIR, PAIR)] * 2,
        scalars=1,
        scratch=[pltpu.VMEM((PAIR, PAIR), F32)] * 2,
        flops=2 * 6 * 8 * PAIR**3,
        nbytes=16 * PAIR * PAIR,
    )(core, up, low, *parts, weights_m, weights_o)


def project_kernel(gram_ref, weights_ref, up_ref, low_ref):
    weights = weights_ref[...]
    turned = mm(gram_ref[...], weights)
    up_ref[...] = mm_t(weights[:, :BLOCK], turned[:, :BLOCK])
    low_ref[...] = mm_t(weights[:, BLOCK:], turned[:, BLOCK:])


def project(gram, weights):
    return call(
        project_kernel,
        (1,),
        [whole(PAIR, PAIR)] * 2,
        [whole(BLOCK, BLOCK)] * 2,
        [shape(BLOCK, BLOCK)] * 2,
        flops=2 * 6 * 2 * PAIR**3,
        nbytes=12 * PAIR * PAIR,
    )(gram, weights)


def scale_kernel(rows, gram_ref, weights_ref, out_ref):
    weights = weights_ref[...]
    squares = jnp.sum(weights * mm(gram_ref[...], weights), axis=0, keepdims=True)
    out_ref[...] = jnp.sqrt(squares / rows)


def scale_of(gram, weights, rows):
    return call(
        lambda *refs: scale_kernel(rows, *refs),
        (1,),
        [whole(PAIR, PAIR)] * 2,
        whole(1, PAIR),
        shape(1, PAIR),
        flops=2 * 6 * PAIR**3,
        nbytes=8 * PAIR * PAIR,
    )(gram, weights)


def main_kernel(step, valid, swap, core_ref, own_ref, other_ref, u0_ref, l0_ref, u1_ref, l1_ref, um_ref, lm_ref,
                out0_ref, out1_ref, lown_ref, keep_ref, send_ref):
    index = pl.program_id(0)

    @pl.when(index == 0)
    def _():
        keep_ref[...] = jnp.zeros_like(keep_ref)
        send_ref[...] = jnp.zeros_like(send_ref)

    first = core_ref[0] == 0
    w0 = jnp.where(first, own_ref[...], other_ref[...])
    w1 = jnp.where(first, other_ref[:, :BLOCK], own_ref[:, :BLOCK])
    pair0 = jnp.concatenate([u0_ref[...], l0_ref[...]], axis=1)
    pair1 = jnp.concatenate([u1_ref[...], l1_ref[...]], axis=1)
    pair_m = jnp.concatenate([um_ref[...], lm_ref[...]], axis=1)
    turned = mm(pair0, w0)
    up0 = turned[:, :BLOCK]
    up1 = mm(pair1, w1)
    lown_ref[...] = turned[:, BLOCK:]
    if swap:
        out0_ref[...] = jnp.where(first, up0, up1)
        out1_ref[...] = jnp.where(first, up1, up0)
    else:
        out0_ref[...] = up0
        out1_ref[...] = up1
    inside = index * step + lax.broadcasted_iota(jnp.int32, up0.shape, 0) < valid
    z0 = mm_t(jnp.where(inside, up0, 0.0), pair_m)
    z1 = mm_t(jnp.where(inside, up1, 0.0), pair0)
    keep_ref[...] += jnp.where(first, z0, z1)
    send_ref[...] += jnp.where(first, z1, z0)


def rotate_main(core, own, other, state, valid, swap):
    rows = state[0].shape[0]
    step = rows // SIDE
    tile = pl.BlockSpec((step, BLOCK), lambda i, c: (i, 0))
    return call(
        lambda *refs: main_kernel(step, valid, swap, *refs),
        (SIDE,),
        [whole(PAIR, PAIR)] * 2 + [tile] * 6,
        [tile] * 3 + [whole(BLOCK, PAIR)] * 2,
        [shape(rows, BLOCK)] * 3 + [shape(BLOCK, PAIR)] * 2,
        scalars=1,
        flops=2 * 6 * rows * (PAIR * (PAIR + BLOCK) + 2 * BLOCK * PAIR),
        nbytes=4 * 9 * rows * BLOCK,
    )(core, own, other, *state)


def ahead_kernel(um_ref, lm_ref, weights_ref, up_ref, low_ref):
    turned = mm(jnp.concatenate([um_ref[...], lm_ref[...]], axis=1), weights_ref[...])
    up_ref[...] = turned[:, :BLOCK]
    low_ref[...] = turned[:, BLOCK:]


def rotate_ahead(upper, lower, weights):
    rows = upper.shape[0]
    tile = pl.BlockSpec((rows // SIDE, BLOCK), lambda i: (i, 0))
    return call(
        ahead_kernel,
        (SIDE,),
        [tile] * 2 + [whole(PAIR, PAIR)],
        [tile] * 2,
        [shape(rows, BLOCK)] * 2,
        flops=2 * 6 * rows * PAIR * PAIR,
        nbytes=4 * 4 * rows * BLOCK,
    )(upper, lower, weights)


def last_ahead_kernel(core_ref, um_ref, lm_ref, weights_ref, lown_ref, keep_ref, send_ref):
    low0 = mm(jnp.concatenate([um_ref[...], lm_ref[...]], axis=1), weights_ref[:, BLOCK:])
    low1 = lown_ref[...]
    first = core_ref[0] == 0
    keep_ref[...] = jnp.where(first, low0, low1)
    send_ref[...] = jnp.where(first, low1, low0)


def rotate_last_ahead(core, upper, lower, weights, lown):
    rows = upper.shape[0]
    tile = pl.BlockSpec((rows // SIDE, BLOCK), lambda i, c: (i, 0))
    return call(
        last_ahead_kernel,
        (SIDE,),
        [tile] * 2 + [whole(PAIR, PAIR)] + [tile],
        [tile] * 2,
        [shape(rows, BLOCK)] * 2,
        scalars=1,
        flops=2 * 6 * rows * PAIR * BLOCK,
        nbytes=4 * 5 * rows * BLOCK,
    )(core, upper, lower, weights, lown)


def final_kernel(core_ref, weights_ref, ku_ref, kl_ref, ru_ref, rl_ref, kub_ref, klb_ref, rub_ref, rlb_ref,
                 out_ref, frame_ref):
    weights = weights_ref[...]
    first = core_ref[0] == 0
    half = kub_ref.shape[0]

    def ordered(keep_up, keep_low, other_up, other_low):
        mine = mm(jnp.concatenate([keep_up[...], keep_low[...]], axis=1), weights)
        theirs = mm(jnp.concatenate([other_up[...], other_low[...]], axis=1), weights)
        return jnp.where(first, mine, theirs), jnp.where(first, theirs, mine)

    out_ref[0], out_ref[1] = ordered(ku_ref, kl_ref, ru_ref, rl_ref)

    @pl.when(pl.program_id(0) == 0)
    def _():
        frame_ref[:half], frame_ref[half:] = ordered(kub_ref, klb_ref, rub_ref, rlb_ref)


def rotate_final(core, weights, blocks, rows, basis_rows):
    tile = pl.BlockSpec((rows, BLOCK), lambda i, c: (i, 0))
    at = SIDE * rows // basis_rows
    basis = pl.BlockSpec((basis_rows, BLOCK), lambda i, c: (at, 0))
    return call(
        final_kernel,
        (SIDE,),
        [whole(PAIR, PAIR)] + [tile] * 4 + [basis] * 4,
        [pl.BlockSpec((2, rows, PAIR), lambda i, c: (i, 0, 0)), whole(2 * basis_rows, PAIR)],
        [shape(COLS, rows, PAIR), shape(2 * basis_rows, PAIR)],
        scalars=1,
        flops=2 * 6 * 2 * SIDE * rows * PAIR * PAIR,
        nbytes=4 * 4 * SIDE * rows * PAIR,
    )(core, weights, *blocks, *blocks)


def swap_core(value):
    return lax.ppermute(value, "cols", TURN_CORE)


def sum_over_rows(value):
    value = value + sum(lax.ppermute(value, "rows", pairs) for pairs in ALONG_X)
    return [value] + [lax.ppermute(value, "rows", pairs) for pairs in ALONG_Z]


def gram_over_rows(gram):
    parts = lax.all_to_all(gram.reshape(ROWS, PAIR // ROWS, PAIR), "rows", 0, 0, tiled=True)
    share = jnp.sum(parts, axis=0)
    spread = jnp.broadcast_to(share[None], (ROWS,) + share.shape)
    return lax.all_to_all(spread, "rows", 0, 0, tiled=True).reshape(PAIR, PAIR)


def body(sensitivity):
    rows = sensitivity.shape[1]
    column = lax.axis_index("cols")
    parity = column % 2
    core = parity.astype(jnp.int32).reshape(1)
    blocks = lax.all_to_all(pack(sensitivity[0]), "cols", 0, 0, axis_index_groups=SAME_CORE, tiled=True)

    keep, send = first_grams(core, blocks)
    gram = gram_over_rows(keep + swap_core(send))

    basis_rows = sensitivity.shape[2] // ROWS // 2
    basis_at = lax.axis_index("rows") * 2 * basis_rows + parity * basis_rows
    row_ids = basis_at + lax.broadcasted_iota(jnp.int32, (basis_rows, BLOCK), 0)
    state = []
    for j, slot in enumerate((column - parity, column - parity + 1, (column - parity + COLS - 1) % COLS)):
        for half in range(2):
            ids = slot * PAIR + half * BLOCK + lax.broadcasted_iota(jnp.int32, (basis_rows, BLOCK), 1)
            data = blocks[:, j, half].reshape(SIDE * rows, BLOCK)
            state.append(jnp.concatenate([data, (row_ids == ids).astype(F32)], axis=0))
    valid = SIDE * rows

    weights = first_cayley(gram)
    for sweep_round in range(ROUNDS - 1):
        last = sweep_round == ROUNDS - 2
        other = swap_core(weights)
        ahead = lax.ppermute(weights, "cols", ODD_TO_EVEN) + lax.ppermute(weights, "cols", ODD_TO_ODD)
        up, low = project(gram, weights)
        low = lax.ppermute(low, "cols", NEXT_SLOT)
        out0, out1, low_out, keep, send = rotate_main(core, weights, other, state, valid, last)
        parts = sum_over_rows(keep + swap_core(send))
        if last:
            keep_low, send_low = rotate_last_ahead(core, state[4], state[5], ahead, low_out)
            held = [out0, keep_low, swap_core(out1), swap_core(send_low)]
        else:
            up_m, low0 = rotate_ahead(state[4], state[5], ahead)
            low_m = lax.ppermute(low_out, "cols", NEXT_CHIP)
            state = [out0, low0, out1, low_out, up_m, low_m]
        weights, gram = cayley(core, up, low, parts, ahead, other)

    column_scale = scale_of(gram, weights, float(rows * COLS * ROWS)).reshape(PAIR)
    rotated, frame = rotate_final(core, weights, held, rows, basis_rows)
    return rotated, frame, column_scale


def solution(mesh):
    in_specs = (P("cols", "rows", None),)
    out_specs = (P(None, "rows", "cols"), P("rows", "cols"), P("cols"))
    return jax.shard_map(body, mesh=mesh, in_specs=in_specs, out_specs=out_specs, check_vma=False)
```

```python
import jax
import jax.numpy as jnp
from jax import lax
from jax.experimental import pallas as pl
from jax.experimental.pallas import tpu as pltpu
from jax.sharding import PartitionSpec as P

ROUNDS = 4
BLOCK = 128
PAIR = 256
SIDE = 4
ROWS = 16
COLS = 8
F32 = jnp.float32
VMEM_LIMIT = 48 * 1024 * 1024

TURN_CORE = [(c, c ^ 1) for c in range(COLS)]
NEXT_SLOT = [(c, (c + 1) % COLS) for c in range(COLS)]
CHIPS_ON = [[(c, (c + 2 * k) % COLS) for c in range(COLS)] for k in range(SIDE)]
ODD_TO_EVEN = [(c, (c + 1) % COLS) for c in range(1, COLS, 2)]
EVEN_TO_ODD = [(c, c + 1) for c in range(0, COLS, 2)]
ALONG_X = [[(r, r - r % SIDE + (r + k) % SIDE) for r in range(ROWS)] for k in range(1, SIDE)]
ALONG_Z = [[(r, (r + SIDE * k) % ROWS) for r in range(ROWS)] for k in range(1, SIDE)]


def mm(left, right):
    return jnp.dot(left, right, precision=lax.Precision.HIGHEST, preferred_element_type=F32)


def mm_t(left, right):
    return lax.dot_general(
        left, right, (((0,), (0,)), ((), ())), precision=lax.Precision.HIGHEST, preferred_element_type=F32
    )


def call(kernel, grid, in_specs, out_specs, out_shape, scalars=0, scratch=(), flops=0, nbytes=0):
    return pl.pallas_call(
        kernel,
        grid_spec=pltpu.PrefetchScalarGridSpec(
            num_scalar_prefetch=scalars,
            grid=grid,
            in_specs=in_specs,
            out_specs=out_specs,
            scratch_shapes=list(scratch),
        ),
        out_shape=out_shape,
        compiler_params=pltpu.CompilerParams(vmem_limit_bytes=VMEM_LIMIT),
        cost_estimate=pl.CostEstimate(flops=flops, bytes_accessed=nbytes, transcendentals=0),
    )


def shape(*dims):
    return jax.ShapeDtypeStruct(dims, F32)


def whole(*dims):
    return pl.BlockSpec(dims, lambda *_: (0,) * len(dims))


def pack_main_kernel(chip_ref, *refs):
    for x_ref, out_ref in zip(refs[:SIDE], refs[SIDE:]):
        out_ref[0, 0] = x_ref[:, :BLOCK]
        out_ref[0, 1] = x_ref[:, BLOCK:]


def pack_main(chip, x):
    rows = x.shape[0]

    def columns(k):
        return pl.BlockSpec((rows, PAIR), lambda j, c: (0, 2 * ((c[0] + k) % SIDE) + j))

    return call(
        pack_main_kernel,
        (2,),
        [columns(k) for k in range(SIDE)],
        [pl.BlockSpec((1, 2, rows, BLOCK), lambda j, c: (j, 0, 0, 0))] * SIDE,
        [shape(2, 2, rows, BLOCK)] * SIDE,
        scalars=1,
        nbytes=8 * SIDE * rows * 2 * PAIR,
    )(chip, *[x] * SIDE)


def pack_ahead_kernel(chip_ref, *refs):
    for x_ref, out_ref in zip(refs[:SIDE], refs[SIDE + 1:]):
        out_ref[0] = x_ref[:, :BLOCK]
        out_ref[1] = x_ref[:, BLOCK:]


def pack_ahead(chip, x, before):
    rows = x.shape[0]

    def columns(k):
        return pl.BlockSpec((rows, PAIR), lambda i, c: (0, (2 * ((c[0] + k) % SIDE) + COLS - 1) % COLS))

    return call(
        pack_ahead_kernel,
        (1,),
        [columns(k) for k in range(SIDE)] + [whole(*before.shape)],
        [whole(2, rows, BLOCK)] * SIDE,
        [shape(2, rows, BLOCK)] * SIDE,
        scalars=1,
        nbytes=8 * SIDE * rows * PAIR,
    )(chip, *[x] * SIDE, before)


def gram_kernel(x_ref, out_ref):
    paired = x_ref[...]
    out_ref[:, 0] = mm_t(paired, paired).reshape(ROWS, PAIR // ROWS, PAIR)


def row_grams(x):
    rows = x.shape[0]
    return call(
        gram_kernel,
        (COLS,),
        [pl.BlockSpec((rows, PAIR), lambda s: (0, s))],
        pl.BlockSpec((ROWS, 1, PAIR // ROWS, PAIR), lambda s: (0, s, 0, 0)),
        shape(ROWS, COLS, PAIR // ROWS, PAIR),
        flops=2 * 6 * COLS * rows * PAIR * PAIR,
        nbytes=4 * COLS * (rows * PAIR + PAIR * PAIR),
    )(x)


def rotation_of(gram, x_ref, r_ref):
    rows = lax.broadcasted_iota(jnp.int32, (PAIR, PAIR), 0)
    columns = lax.broadcasted_iota(jnp.int32, (PAIR, PAIR), 1)
    eye = (rows == columns).astype(F32)
    on_diagonal = gram * eye
    across = jnp.sum(on_diagonal, axis=0, keepdims=True)
    down = jnp.sum(on_diagonal, axis=1, keepdims=True)
    spread = across - down
    totals = across + down
    skew = gram * spread / (2.0 * spread * spread + 0.5 * totals * totals)
    square = mm(skew, skew)
    bound = jnp.max(jnp.sum(jnp.abs(square), axis=0))
    scale = 2.0 / (2.0 + bound)
    x_ref[...] = scale * (eye + skew)
    r_ref[...] = (1.0 - scale) * eye + scale * square

    def step(size):
        left = r_ref[...]
        x = x_ref[...]
        x_ref[...] = x + mm(x, left)
        r_ref[...] = mm(left, left)
        return size * size

    lax.while_loop(lambda size: size > 3e-4, step, bound / (2.0 + bound))
    x = x_ref[...]
    x = x + mm(x, eye - x + mm(skew, x))
    return 2.0 * x - eye


def first_cayley_kernel(gram_ref, weights_ref, x_ref, r_ref):
    weights_ref[...] = rotation_of(gram_ref[...], x_ref, r_ref)


def first_cayley(gram):
    return call(
        first_cayley_kernel,
        (1,),
        [whole(PAIR, PAIR)],
        whole(PAIR, PAIR),
        shape(PAIR, PAIR),
        scratch=[pltpu.VMEM((PAIR, PAIR), F32)] * 2,
        flops=2 * 6 * 8 * PAIR**3,
        nbytes=8 * PAIR * PAIR,
    )(gram)


def cayley_kernel(core_ref, up_ref, low_ref, z0_ref, z1_ref, z2_ref, z3_ref, wm_ref, wo_ref, weights_ref, gram_ref, x_ref, r_ref):
    mixed = (z0_ref[...] + z1_ref[...]) + (z2_ref[...] + z3_ref[...])
    before = jnp.where(core_ref[0] == 0, wm_ref[:, BLOCK:], wo_ref[:, BLOCK:])
    cross = mm(mixed, before)
    gram_ref[:BLOCK, :BLOCK] = up_ref[...]
    gram_ref[:BLOCK, BLOCK:] = cross
    gram_ref[BLOCK:, :BLOCK] = cross.T
    gram_ref[BLOCK:, BLOCK:] = low_ref[...]
    weights_ref[...] = rotation_of(gram_ref[...], x_ref, r_ref)


def cayley(core, up, low, parts, weights_m, weights_o):
    return call(
        cayley_kernel,
        (1,),
        [whole(BLOCK, BLOCK)] * 2 + [whole(BLOCK, PAIR)] * 4 + [whole(PAIR, PAIR)] * 2,
        [whole(PAIR, PAIR)] * 2,
        [shape(PAIR, PAIR)] * 2,
        scalars=1,
        scratch=[pltpu.VMEM((PAIR, PAIR), F32)] * 2,
        flops=2 * 6 * 8 * PAIR**3,
        nbytes=16 * PAIR * PAIR,
    )(core, up, low, *parts, weights_m, weights_o)


def project_kernel(gram_ref, weights_ref, up_ref, low_ref):
    weights = weights_ref[...]
    turned = mm(gram_ref[...], weights)
    up_ref[...] = mm_t(weights[:, :BLOCK], turned[:, :BLOCK])
    low_ref[...] = mm_t(weights[:, BLOCK:], turned[:, BLOCK:])


def project(gram, weights):
    return call(
        project_kernel,
        (1,),
        [whole(PAIR, PAIR)] * 2,
        [whole(BLOCK, BLOCK)] * 2,
        [shape(BLOCK, BLOCK)] * 2,
        flops=2 * 6 * 2 * PAIR**3,
        nbytes=12 * PAIR * PAIR,
    )(gram, weights)


def scale_kernel(rows, gram_ref, weights_ref, out_ref):
    weights = weights_ref[...]
    squares = jnp.sum(weights * mm(gram_ref[...], weights), axis=0, keepdims=True)
    out_ref[...] = jnp.sqrt(squares / rows)


def scale_of(gram, weights, rows):
    return call(
        lambda *refs: scale_kernel(rows, *refs),
        (1,),
        [whole(PAIR, PAIR)] * 2,
        whole(1, PAIR),
        shape(1, PAIR),
        flops=2 * 6 * PAIR**3,
        nbytes=8 * PAIR * PAIR,
    )(gram, weights)


def turn(core_ref, own_ref, other_ref, pair0, pair1, pair_m, rows, out0_ref, out1_ref, keep_ref, send_ref):
    @pl.when(pl.program_id(0) == 0)
    def _():
        keep_ref[...] = jnp.zeros_like(keep_ref)
        send_ref[...] = jnp.zeros_like(send_ref)

    first = core_ref[0] == 0
    up0 = mm(pair0, jnp.where(first, own_ref[:, :BLOCK], other_ref[:, :BLOCK]))
    up1 = mm(pair1, jnp.where(first, other_ref[:, :BLOCK], own_ref[:, :BLOCK]))
    out0_ref[0] = up0
    out1_ref[0] = up1
    z0 = mm_t(up0[:rows], pair_m[:rows])
    z1 = mm_t(up1[:rows], pair0[:rows])
    keep_ref[...] += jnp.where(first, z0, z1)
    send_ref[...] += jnp.where(first, z1, z0)


def halves(up_ref, low_ref):
    return jnp.concatenate([up_ref[0], low_ref[0]], axis=1)


def main_kernel(rows, core_ref, own_ref, other_ref, u0_ref, l0_ref, u1_ref, l1_ref, um_ref, lm_ref, *outs):
    turn(core_ref, own_ref, other_ref, halves(u0_ref, l0_ref), halves(u1_ref, l1_ref), halves(um_ref, lm_ref), rows, *outs)


def rotate_main(core, own, other, state, rows):
    step = state[0].shape[1]
    tile = pl.BlockSpec((1, step, BLOCK), lambda i, c: (i, 0, 0))
    return call(
        lambda *refs: main_kernel(rows, *refs),
        (SIDE,),
        [whole(PAIR, PAIR)] * 2 + [tile] * 6,
        [tile] * 2 + [whole(BLOCK, PAIR)] * 2,
        [shape(SIDE, step, BLOCK)] * 2 + [shape(BLOCK, PAIR)] * 2,
        scalars=1,
        flops=2 * 6 * SIDE * step * 4 * BLOCK * PAIR,
        nbytes=4 * 8 * SIDE * step * BLOCK,
    )(core, own, other, *state)


def start_pair(info_ref, step, slot, up, low):
    column = slot * PAIR - info_ref[2] - (step - up.shape[0]) * pl.program_id(0)
    rows = lax.broadcasted_iota(jnp.int32, (step - up.shape[0], PAIR), 0)
    columns = lax.broadcasted_iota(jnp.int32, (step - up.shape[0], PAIR), 1)
    basis = (rows == columns + column).astype(F32)
    return jnp.concatenate([jnp.concatenate([up, low], axis=1), basis], axis=0)


def start_main_kernel(step, info_ref, own_ref, other_ref, main_ref, ahead_ref, *outs):
    slot = 2 * info_ref[1]
    pair0 = start_pair(info_ref, step, slot, main_ref[0, 0, 0], main_ref[0, 0, 1])
    pair1 = start_pair(info_ref, step, slot + 1, main_ref[0, 1, 0], main_ref[0, 1, 1])
    pair_m = jnp.concatenate([ahead_ref[0, 0], ahead_ref[0, 1]], axis=1)
    turn(info_ref, own_ref, other_ref, pair0, pair1, pair_m, pair_m.shape[0], *outs)


def start_ahead_kernel(step, info_ref, weights_ref, other_ref, own_ref, low_in_ref, main_ref, ahead_ref, *outs):
    slot = 2 * info_ref[1]
    pair0 = start_pair(info_ref, step, slot, main_ref[0, 0, 0], main_ref[0, 0, 1])
    pair_m = start_pair(info_ref, step, (slot + COLS - 1) % COLS, ahead_ref[0, 0], ahead_ref[0, 1])
    turn_ahead(info_ref, weights_ref, other_ref, own_ref, pair0, pair_m, *outs)


def start_specs(rows, step):
    main = pl.BlockSpec((1, 2, 2, rows, BLOCK), lambda i, c: (lax.rem(c[1] + SIDE - i, SIDE), 0, 0, 0, 0))
    ahead = pl.BlockSpec((1, 2, rows, BLOCK), lambda i, c: (lax.rem(c[1] + SIDE - i, SIDE), 0, 0, 0))
    return main, ahead, pl.BlockSpec((1, step, BLOCK), lambda i, c: (i, 0, 0))


def start_main(info, own, other, main, ahead, step):
    rows = main.shape[3]
    main_spec, ahead_spec, tile = start_specs(rows, step)
    return call(
        lambda *refs: start_main_kernel(step, *refs),
        (SIDE,),
        [whole(PAIR, PAIR)] * 2 + [main_spec, ahead_spec],
        [tile] * 2 + [whole(BLOCK, PAIR)] * 2,
        [shape(SIDE, step, BLOCK)] * 2 + [shape(BLOCK, PAIR)] * 2,
        scalars=1,
        flops=2 * 6 * SIDE * step * 4 * BLOCK * PAIR,
        nbytes=4 * 8 * SIDE * step * BLOCK,
    )(info, own, other, main, ahead)


def turn_ahead(core_ref, weights_ref, other_ref, own_ref, pair0, pair_m, up_ref, low_ref, pass_ref):
    turned = mm(pair_m, weights_ref[...])
    up_ref[0] = turned[:, :BLOCK]
    low_ref[0] = turned[:, BLOCK:]
    pass_ref[0] = mm(pair0, jnp.where(core_ref[0] == 0, own_ref[:, BLOCK:], other_ref[:, BLOCK:]))


def ahead_kernel(core_ref, weights_ref, other_ref, own_ref, low_in_ref, u0_ref, l0_ref, um_ref, lm_ref, *outs):
    turn_ahead(core_ref, weights_ref, other_ref, own_ref, halves(u0_ref, l0_ref), halves(um_ref, lm_ref), *outs)


def ahead_call(kernel, step, specs, args):
    tile = pl.BlockSpec((1, step, BLOCK), lambda i, c: (i, 0, 0))
    return call(
        kernel,
        (SIDE,),
        [whole(PAIR, PAIR)] * 3 + [whole(BLOCK, BLOCK)] + specs,
        [tile] * 3,
        [shape(SIDE, step, BLOCK)] * 3,
        scalars=1,
        flops=2 * 6 * SIDE * step * 3 * BLOCK * PAIR,
        nbytes=4 * 7 * SIDE * step * BLOCK,
    )(*args)


def rotate_ahead(core, weights, other, own, low, blocks):
    step = blocks[0].shape[1]
    tile = pl.BlockSpec((1, step, BLOCK), lambda i, c: (i, 0, 0))
    return ahead_call(ahead_kernel, step, [tile] * 4, (core, weights, other, own, low, *blocks))


def start_ahead(info, weights, other, own, low, main, ahead, step):
    specs = list(start_specs(main.shape[3], step)[:2])
    kernel = lambda *refs: start_ahead_kernel(step, *refs)
    return ahead_call(kernel, step, specs, (info, weights, other, own, low, main, ahead))


def last_ahead_kernel(core_ref, weights_ref, other_ref, own_ref, before_ref, u0_ref, l0_ref, um_ref, lm_ref,
                      out0_ref, out1_ref, keep_up_ref, keep_low_ref, send_up_ref, send_low_ref):
    first = core_ref[0] == 0
    low0 = mm(halves(um_ref, lm_ref), weights_ref[:, BLOCK:])
    low1 = mm(halves(u0_ref, l0_ref), jnp.where(first, own_ref[:, BLOCK:], other_ref[:, BLOCK:]))
    up0 = out0_ref[0]
    up1 = out1_ref[0]
    keep_up_ref[0] = jnp.where(first, up0, up1)
    send_up_ref[0] = jnp.where(first, up1, up0)
    keep_low_ref[0] = jnp.where(first, low0, low1)
    send_low_ref[0] = jnp.where(first, low1, low0)


def rotate_last_ahead(core, weights, other, own, before, blocks):
    step = blocks[0].shape[1]
    tile = pl.BlockSpec((1, step, BLOCK), lambda i, c: (i, 0, 0))
    return call(
        last_ahead_kernel,
        (SIDE,),
        [whole(PAIR, PAIR)] * 3 + [whole(*before.shape)] + [tile] * 6,
        [tile] * 4,
        [shape(SIDE, step, BLOCK)] * 4,
        scalars=1,
        flops=2 * 6 * SIDE * step * 2 * PAIR * BLOCK,
        nbytes=4 * 10 * SIDE * step * BLOCK,
    )(core, weights, other, own, before, *blocks)


def final_kernel(rows, core_ref, weights_ref, ku_ref, kl_ref, ru_ref, rl_ref, out_ref, frame_ref):
    weights = weights_ref[...]
    first = core_ref[0] == 0
    mine = mm(halves(ku_ref, kl_ref), weights)
    theirs = mm(halves(ru_ref, rl_ref), weights)
    for k, turned in enumerate((jnp.where(first, mine, theirs), jnp.where(first, theirs, mine))):
        out_ref[k] = turned[:rows]
        frame_ref[k] = turned[rows:]


def rotate_final(core, weights, blocks, rows):
    step = blocks[0].shape[1]
    tile = pl.BlockSpec((1, step, BLOCK), lambda i, c: (i, 0, 0))
    share = step - rows
    return call(
        lambda *refs: final_kernel(rows, *refs),
        (SIDE,),
        [whole(PAIR, PAIR)] + [tile] * 4,
        [pl.BlockSpec((2, rows, PAIR), lambda i, c: (i, 0, 0)), pl.BlockSpec((2, share, PAIR), lambda i, c: (0, i, 0))],
        [shape(COLS, rows, PAIR), shape(2, SIDE * share, PAIR)],
        scalars=1,
        flops=2 * 6 * 2 * SIDE * step * PAIR * PAIR,
        nbytes=4 * 4 * SIDE * step * PAIR,
    )(core, weights, *blocks)


def swap_core(value):
    return lax.ppermute(value, "cols", TURN_CORE)


def sum_over_rows(value):
    value = value + sum(lax.ppermute(value, "rows", pairs) for pairs in ALONG_X)
    return [value] + [lax.ppermute(value, "rows", pairs) for pairs in ALONG_Z]


def spread_over_rows(share):
    copies = jnp.broadcast_to(share[None], (ROWS,) + share.shape)
    return lax.all_to_all(copies, "rows", 0, 0, tiled=True).reshape(PAIR, PAIR)


def body(sensitivity):
    x = sensitivity[0]
    rows = x.shape[0]
    column = lax.axis_index("cols")
    parity = column % 2
    basis_rows = x.shape[1] // ROWS // 2
    basis_at = (lax.axis_index("rows") * 2 + parity) * basis_rows
    core = parity.astype(jnp.int32).reshape(1)
    chip = (column // 2).astype(jnp.int32).reshape(1)
    info = jnp.stack([parity, column // 2, basis_at]).astype(jnp.int32)
    step = rows + basis_rows // SIDE

    packed = pack_main(chip, x)
    main = [packed[0]] + [lax.ppermute(packed[k], "cols", CHIPS_ON[k]) for k in range(1, SIDE)]

    parts = lax.all_to_all(row_grams(x), "rows", 0, 0, tiled=True)
    parts = lax.all_to_all(jnp.sum(parts, axis=0), "cols", 0, 0, tiled=True)
    share = jnp.sum(parts, axis=0)

    packed = pack_ahead(chip, x, share)
    ahead = [packed[0]] + [lax.ppermute(packed[k], "cols", CHIPS_ON[k]) for k in range(1, SIDE)]
    gram = spread_over_rows(share)
    weights = first_cayley(gram)

    main = jnp.stack(main)
    ahead = jnp.stack(ahead)
    state = None
    for sweep_round in range(ROUNDS - 1):
        other = swap_core(weights)
        weights_m = lax.ppermute(weights, "cols", ODD_TO_EVEN)
        weights_m = weights_m + lax.ppermute(weights_m, "cols", EVEN_TO_ODD)
        up, low = project(gram, weights)
        low = lax.ppermute(low, "cols", NEXT_SLOT)
        if state is None:
            up0, up1, keep, send = start_main(info, weights, other, main, ahead, step)
        else:
            up0, up1, keep, send = rotate_main(core, weights, other, state, rows)
        parts = sum_over_rows(keep + swap_core(send))
        if sweep_round == ROUNDS - 2:
            blocks = (state[0], state[1], state[4], state[5], up0, up1)
            held = rotate_last_ahead(core, weights_m, other, weights, parts[0], blocks)
            held = [held[0], held[1], swap_core(held[2]), swap_core(held[3])]
        else:
            if state is None:
                up_m, low0, low1 = start_ahead(info, weights_m, other, weights, low, main, ahead, step)
            else:
                blocks = (state[0], state[1], state[4], state[5])
                up_m, low0, low1 = rotate_ahead(core, weights_m, other, weights, low, blocks)
            state = [up0, low0, up1, low1, up_m, lax.ppermute(low1, "cols", CHIPS_ON[1])]
        weights, gram = cayley(core, up, low, parts, weights_m, other)

    column_scale = scale_of(gram, weights, float(rows * COLS * ROWS)).reshape(PAIR)
    rotated, frame = rotate_final(core, weights, held, rows)
    return rotated, frame.reshape(2 * basis_rows, PAIR), column_scale


def solution(mesh):
    in_specs = (P("cols", "rows", None),)
    out_specs = (P(None, "rows", "cols"), P("rows", "cols"), P("cols"))
    return jax.shard_map(body, mesh=mesh, in_specs=in_specs, out_specs=out_specs, check_vma=False)
```

```python
import functools

import jax
import jax.numpy as jnp
from jax import lax
from jax.experimental import pallas as pl
from jax.experimental.pallas import tpu as pltpu
from jax.sharding import PartitionSpec as P

ROUNDS = 4
BLOCK = 128
PAIR = 256
SIDE = 4
ROWS = 16
COLS = 8
F32 = jnp.float32
BF16 = jnp.bfloat16
VMEM_LIMIT = 48 * 1024 * 1024

TURN_CORE = [(c, c ^ 1) for c in range(COLS)]
NEXT_SLOT = [(c, (c + 1) % COLS) for c in range(COLS)]
CHIPS_ON = [[(c, (c + 2 * k) % COLS) for c in range(COLS)] for k in range(SIDE)]
ODD_TO_EVEN = [(c, (c + 1) % COLS) for c in range(1, COLS, 2)]
ODD_TO_ODD = [(c, (c + 2) % COLS) for c in range(1, COLS, 2)]
ALONG_X = [[(r, r - r % SIDE + (r + k) % SIDE) for r in range(ROWS)] for k in range(1, SIDE)]
ALONG_Z = [[(r, (r + SIDE * k) % ROWS) for r in range(ROWS)] for k in range(1, SIDE)]


def mm(left, right):
    return jnp.dot(left, right, precision=lax.Precision.HIGHEST, preferred_element_type=F32)


def mm_t(left, right):
    return lax.dot_general(
        left, right, (((0,), (0,)), ((), ())), precision=lax.Precision.HIGHEST, preferred_element_type=F32
    )


def parts_of(value):
    high = value.astype(BF16)
    return high, (value - high.astype(F32)).astype(BF16)


def dot(left, right, axis):
    return lax.dot_general(left, right, (((axis,), (0,)), ((), ())), preferred_element_type=F32)


def mm3(left, right, axis=1):
    high, low = parts_of(left)
    right_high, right_low = parts_of(right)
    width = right.shape[1]
    if width < PAIR:
        both = dot(high, jnp.concatenate([right_high, right_low], axis=1), axis)
        return both[:, :width] + (both[:, width:] + dot(low, right_high, axis))
    return dot(high, right_high, axis) + (dot(high, right_low, axis) + dot(low, right_high, axis))


def call(kernel, grid, in_specs, out_specs, out_shape, scalars=0, scratch=(), flops=0, nbytes=0):
    return pl.pallas_call(
        kernel,
        grid_spec=pltpu.PrefetchScalarGridSpec(
            num_scalar_prefetch=scalars,
            grid=grid,
            in_specs=in_specs,
            out_specs=out_specs,
            scratch_shapes=list(scratch),
        ),
        out_shape=out_shape,
        compiler_params=pltpu.CompilerParams(vmem_limit_bytes=VMEM_LIMIT),
        cost_estimate=pl.CostEstimate(flops=flops, bytes_accessed=nbytes, transcendentals=0),
    )


def shape(*dims):
    return jax.ShapeDtypeStruct(dims, F32)


def whole(*dims):
    return pl.BlockSpec(dims, lambda *_: (0,) * len(dims))


def pack_main_kernel(info_ref, *refs):
    for x_ref, out_ref in zip(refs[:SIDE], refs[SIDE:]):
        out_ref[0, 0] = x_ref[:, :BLOCK]
        out_ref[0, 1] = x_ref[:, BLOCK:]


def pack_main(info, x):
    rows = x.shape[0]

    def columns(k):
        return pl.BlockSpec((rows, PAIR), lambda j, c: (0, 2 * ((c[1] + k) % SIDE) + j))

    return call(
        pack_main_kernel,
        (2,),
        [columns(k) for k in range(SIDE)],
        [pl.BlockSpec((1, 2, rows, BLOCK), lambda j, c: (j, 0, 0, 0))] * SIDE,
        [shape(2, 2, rows, BLOCK)] * SIDE,
        scalars=1,
        nbytes=8 * SIDE * rows * 2 * PAIR,
    )(info, *[x] * SIDE)


def pack_ahead_kernel(info_ref, *refs):
    for x_ref, out_ref in zip(refs[:SIDE], refs[SIDE + 1:]):
        out_ref[0] = x_ref[:, :BLOCK]
        out_ref[1] = x_ref[:, BLOCK:]


def pack_ahead(info, x, before):
    rows = x.shape[0]

    def columns(k):
        return pl.BlockSpec((rows, PAIR), lambda i, c: (0, (2 * ((c[1] + k) % SIDE) + COLS - 1) % COLS))

    return call(
        pack_ahead_kernel,
        (1,),
        [columns(k) for k in range(SIDE)] + [pl.BlockSpec(memory_space=pl.ANY)],
        [whole(2, rows, BLOCK)] * SIDE,
        [shape(2, rows, BLOCK)] * SIDE,
        scalars=1,
        nbytes=8 * SIDE * rows * PAIR,
    )(info, *[x] * SIDE, before)


def gram_kernel(x_ref, before_ref, out_ref):
    high, low = parts_of(x_ref[...])
    mixed = dot(high, low, 0)
    gram = dot(high, high, 0) + (mixed + mixed.T)
    for k, block in enumerate((gram[:BLOCK, :BLOCK], gram[:BLOCK, BLOCK:], gram[BLOCK:, BLOCK:])):
        out_ref[:, 0, k] = block.reshape(ROWS, BLOCK // ROWS, BLOCK)


def row_grams(x, before):
    rows = x.shape[0]
    return call(
        gram_kernel,
        (COLS,),
        [pl.BlockSpec((rows, PAIR), lambda s: (0, s)), pl.BlockSpec(memory_space=pl.ANY)],
        pl.BlockSpec((ROWS, 1, 3, BLOCK // ROWS, BLOCK), lambda s: (0, s, 0, 0, 0)),
        shape(ROWS, COLS, 3, BLOCK // ROWS, BLOCK),
        flops=2 * 2 * COLS * rows * PAIR * PAIR,
        nbytes=4 * COLS * (rows * PAIR + PAIR * PAIR),
    )(x, before)


def rotation_of(gram, x_ref, r_ref):
    rows = lax.broadcasted_iota(jnp.int32, (PAIR, PAIR), 0)
    columns = lax.broadcasted_iota(jnp.int32, (PAIR, PAIR), 1)
    eye = (rows == columns).astype(F32)
    on_diagonal = gram * eye
    across = jnp.sum(on_diagonal, axis=0, keepdims=True)
    down = jnp.sum(on_diagonal, axis=1, keepdims=True)
    spread = across - down
    totals = across + down
    skew = gram * spread / (2.0 * spread * spread + 0.5 * totals * totals)
    square = mm(skew, skew)
    bound = jnp.max(jnp.sum(jnp.abs(square), axis=0))
    scale = 2.0 / (2.0 + bound)
    x_ref[...] = scale * (eye + skew)
    r_ref[...] = (1.0 - scale) * eye + scale * square

    def step(size):
        left = r_ref[...]
        x = x_ref[...]
        x_ref[...] = x + mm(x, left)
        r_ref[...] = mm(left, left)
        return size * size

    lax.while_loop(lambda size: size > 3e-4, step, bound / (2.0 + bound))
    x = x_ref[...]
    x = x + mm(x, eye - x + mm(skew, x))
    return 2.0 * x - eye


def cayley_kernel(fill, *refs):
    weights_ref, up_ref, low_ref, gram_ref, x_ref, r_ref = refs[-6:]
    up, cross, low = fill(*refs[:-6])
    gram_ref[:BLOCK, :BLOCK] = up
    gram_ref[:BLOCK, BLOCK:] = cross
    gram_ref[BLOCK:, :BLOCK] = cross.T
    gram_ref[BLOCK:, BLOCK:] = low
    weights = rotation_of(gram_ref[...], x_ref, r_ref)
    weights_ref[...] = weights
    up_ref[...] = weights[:, :BLOCK]
    low_ref[...] = weights[:, BLOCK:]


def cayley_call(fill, args):
    return call(
        lambda *refs: cayley_kernel(fill, *refs),
        (1,),
        [whole(*arg.shape) for arg in args],
        [whole(PAIR, PAIR), whole(PAIR, BLOCK), whole(PAIR, BLOCK), whole(PAIR, PAIR)],
        [shape(PAIR, PAIR), shape(PAIR, BLOCK), shape(PAIR, BLOCK), shape(PAIR, PAIR)],
        scratch=[pltpu.VMEM((PAIR, PAIR), F32)] * 2,
        flops=2 * 6 * 8 * PAIR**3,
        nbytes=20 * PAIR * PAIR,
    )(*args)


def first_cayley(blocks):
    return cayley_call(lambda ref: [ref[:, k].reshape(BLOCK, BLOCK) for k in range(3)], (blocks,))


def cayley(up, low, parts):
    def fill(up_ref, low_ref, *part_refs):
        first, second, third, fourth = (ref[...] for ref in part_refs)
        return up_ref[...], (first + second) + (third + fourth), low_ref[...]

    return cayley_call(fill, (up, low, *parts))


def project_kernel(gram_ref, weights_ref, up_ref, low_ref):
    weights = weights_ref[...]
    turned = mm(gram_ref[...], weights)
    up_ref[...] = mm_t(weights[:, :BLOCK], turned[:, :BLOCK])
    low_ref[...] = mm_t(weights[:, BLOCK:], turned[:, BLOCK:])


def project(gram, weights):
    return call(
        project_kernel,
        (1,),
        [whole(PAIR, PAIR)] * 2,
        [whole(BLOCK, BLOCK)] * 2,
        [shape(BLOCK, BLOCK)] * 2,
        flops=2 * 6 * 2 * PAIR**3,
        nbytes=12 * PAIR * PAIR,
    )(gram, weights)


def halves(up_ref, low_ref):
    return jnp.concatenate([up_ref[0], low_ref[0]], axis=1)


def own_turn(info_ref, own_ref, other_ref, pair0, pair1, rows, up0_ref, up1_ref, low1_ref, cross_ref):
    @pl.when(pl.program_id(0) == 0)
    def _():
        cross_ref[...] = jnp.zeros_like(cross_ref)

    first = info_ref[0] == 0
    turned = mm3(pair0, jnp.where(first, own_ref[...], other_ref[...]))
    up1 = mm3(pair1, jnp.where(first, other_ref[:, :BLOCK], own_ref[:, :BLOCK]))
    up0_ref[0] = turned[:, :BLOCK]
    low1_ref[0] = turned[:, BLOCK:]
    up1_ref[0] = up1
    cross_ref[...] += mm3(up1[:rows], turned[:rows, BLOCK:], 0)


def ahead_turn(info_ref, even_ref, odd_ref, cross_ref, up0_ref, pair_m, rows, low0_ref, keep_ref, send_ref, sum_ref):
    @pl.when(pl.program_id(0) == 0)
    def _():
        sum_ref[...] = jnp.zeros_like(sum_ref)

    low0 = mm3(pair_m, even_ref[...] + odd_ref[...])
    low0_ref[0] = low0
    sum_ref[...] += mm3(up0_ref[0, :rows], low0[:rows], 0)

    @pl.when(pl.program_id(0) == SIDE - 1)
    def _():
        first = info_ref[0] == 0
        keep_ref[...] = jnp.where(first, sum_ref[...], cross_ref[...])
        send_ref[...] = jnp.where(first, cross_ref[...], sum_ref[...])


def up_turn(even_ref, odd_ref, pair_m, low1_ref, up_m_ref, pass_ref):
    up_m_ref[0] = mm3(pair_m, even_ref[...] + odd_ref[...])
    pass_ref[0] = low1_ref[0]


def own_kernel(rows, info_ref, own_ref, other_ref, u0_ref, l0_ref, u1_ref, l1_ref, *outs):
    own_turn(info_ref, own_ref, other_ref, halves(u0_ref, l0_ref), halves(u1_ref, l1_ref), rows, *outs)


def ahead_kernel(rows, info_ref, even_ref, odd_ref, cross_ref, up0_ref, um_ref, lm_ref, *outs):
    ahead_turn(info_ref, even_ref, odd_ref, cross_ref, up0_ref, halves(um_ref, lm_ref), rows, *outs)


def up_kernel(info_ref, even_ref, odd_ref, before_ref, low1_ref, um_ref, lm_ref, *outs):
    up_turn(even_ref, odd_ref, halves(um_ref, lm_ref), low1_ref, *outs)


def start_pair(info_ref, step, slot, up, low):
    column = slot * PAIR - info_ref[2] - (step - up.shape[0]) * pl.program_id(0)
    rows = lax.broadcasted_iota(jnp.int32, (step - up.shape[0], PAIR), 0)
    columns = lax.broadcasted_iota(jnp.int32, (step - up.shape[0], PAIR), 1)
    basis = (rows == columns + column).astype(F32)
    return jnp.concatenate([jnp.concatenate([up, low], axis=1), basis], axis=0)


def start_ahead_pair(info_ref, step, ahead_ref):
    slot = (2 * info_ref[1] + COLS - 1) % COLS
    return start_pair(info_ref, step, slot, ahead_ref[0, 0], ahead_ref[0, 1])


def start_own_kernel(step, rows, info_ref, own_ref, other_ref, main_ref, *outs):
    slot = 2 * info_ref[1]
    pair0 = start_pair(info_ref, step, slot, main_ref[0, 0, 0], main_ref[0, 0, 1])
    pair1 = start_pair(info_ref, step, slot + 1, main_ref[0, 1, 0], main_ref[0, 1, 1])
    own_turn(info_ref, own_ref, other_ref, pair0, pair1, rows, *outs)


def start_ahead_kernel(step, rows, info_ref, even_ref, odd_ref, cross_ref, up0_ref, ahead_ref, *outs):
    pair_m = start_ahead_pair(info_ref, step, ahead_ref)
    ahead_turn(info_ref, even_ref, odd_ref, cross_ref, up0_ref, pair_m, rows, *outs)


def start_up_kernel(step, info_ref, even_ref, odd_ref, before_ref, low1_ref, ahead_ref, *outs):
    up_turn(even_ref, odd_ref, start_ahead_pair(info_ref, step, ahead_ref), low1_ref, *outs)


def group_tile(step):
    return pl.BlockSpec((1, step, BLOCK), lambda i, c: (i, 0, 0))


def arrived(value):
    rest = value.shape[1:]
    return pl.BlockSpec((1,) + rest, lambda i, c: (lax.rem(c[1] + SIDE - i, SIDE),) + (0,) * len(rest))


def rotate_own(info, own, other, blocks, rows, step):
    starting = len(blocks) == 1
    kernel = functools.partial(start_own_kernel, step, rows) if starting else functools.partial(own_kernel, rows)
    tile = group_tile(step)
    return call(
        kernel,
        (SIDE,),
        [whole(PAIR, PAIR)] * 2 + ([arrived(blocks[0])] if starting else [tile] * 4),
        [tile] * 3 + [whole(BLOCK, BLOCK)],
        [shape(SIDE, step, BLOCK)] * 3 + [shape(BLOCK, BLOCK)],
        scalars=1,
        flops=2 * 3 * SIDE * step * 4 * BLOCK * PAIR,
        nbytes=4 * 7 * SIDE * step * BLOCK,
    )(info, own, other, *blocks)


def rotate_ahead(info, lower, cross, up0, blocks, rows, step):
    starting = len(blocks) == 1
    kernel = functools.partial(start_ahead_kernel, step, rows) if starting else functools.partial(ahead_kernel, rows)
    tile = group_tile(step)
    return call(
        kernel,
        (SIDE,),
        [whole(PAIR, BLOCK)] * 2 + [whole(BLOCK, BLOCK), tile] + ([arrived(blocks[0])] if starting else [tile] * 2),
        [tile] + [whole(BLOCK, BLOCK)] * 2,
        [shape(SIDE, step, BLOCK)] + [shape(BLOCK, BLOCK)] * 2,
        scalars=1,
        scratch=[pltpu.VMEM((BLOCK, BLOCK), F32)],
        flops=2 * 3 * SIDE * step * 2 * BLOCK * PAIR,
        nbytes=4 * 4 * SIDE * step * BLOCK,
    )(info, *lower, cross, up0, *blocks)


def rotate_up(info, upper, before, low1, blocks, step):
    starting = len(blocks) == 1
    kernel = functools.partial(start_up_kernel, step) if starting else up_kernel
    tile = group_tile(step)
    return call(
        kernel,
        (SIDE,),
        [whole(PAIR, BLOCK)] * 2
        + [pl.BlockSpec(memory_space=pl.ANY), tile]
        + ([arrived(blocks[0])] if starting else [tile] * 2),
        [tile] * 2,
        [shape(SIDE, step, BLOCK)] * 2,
        scalars=1,
        flops=2 * 3 * SIDE * step * BLOCK * PAIR,
        nbytes=4 * 5 * SIDE * step * BLOCK,
    )(info, *upper, before, low1, *blocks)


def other_slot_kernel(info_ref, before_ref, up0_ref, low0_ref, up1_ref, low1_ref, up_ref, low_ref):
    first = info_ref[0] == 0
    up_ref[0] = jnp.where(first, up1_ref[0], up0_ref[0])
    low_ref[0] = jnp.where(first, low1_ref[0], low0_ref[0])


def other_slot(info, before, blocks, step):
    tile = group_tile(step)
    return call(
        other_slot_kernel,
        (SIDE,),
        [pl.BlockSpec(memory_space=pl.ANY)] + [tile] * 4,
        [tile] * 2,
        [shape(SIDE, step, BLOCK)] * 2,
        scalars=1,
        nbytes=4 * 6 * SIDE * step * BLOCK,
    )(info, before, *blocks)


def final_kernel(rows, total, info_ref, weights_ref, gram_ref, up0_ref, low0_ref, up1_ref, low1_ref, ru_ref, rl_ref,
                 out_ref, frame_ref, scale_ref):
    weights = weights_ref[...]
    first = info_ref[0] == 0
    mine = mm3(jnp.where(first, halves(up0_ref, low0_ref), halves(up1_ref, low1_ref)), weights)
    theirs = mm3(halves(ru_ref, rl_ref), weights)
    for k, turned in enumerate((jnp.where(first, mine, theirs), jnp.where(first, theirs, mine))):
        out_ref[k] = turned[:rows]
        frame_ref[k] = turned[rows:]

    @pl.when(pl.program_id(0) == 0)
    def _():
        squares = jnp.sum(weights * mm(gram_ref[...], weights), axis=0, keepdims=True)
        scale_ref[...] = jnp.sqrt(squares / total)


def rotate_final(info, weights, gram, blocks, rows, step):
    tile = group_tile(step)
    share = step - rows
    return call(
        functools.partial(final_kernel, rows, float(rows * COLS * ROWS)),
        (SIDE,),
        [whole(PAIR, PAIR)] * 2 + [tile] * 6,
        [
            pl.BlockSpec((2, rows, PAIR), lambda i, c: (i, 0, 0)),
            pl.BlockSpec((2, share, PAIR), lambda i, c: (0, i, 0)),
            whole(1, PAIR),
        ],
        [shape(COLS, rows, PAIR), shape(2, SIDE * share, PAIR), shape(1, PAIR)],
        scalars=1,
        flops=2 * 3 * 2 * SIDE * step * PAIR * PAIR,
        nbytes=4 * 4 * SIDE * step * PAIR,
    )(info, weights, gram, *blocks)


def swap_core(value):
    return lax.ppermute(value, "cols", TURN_CORE)


def sum_over_rows(value):
    value = value + sum(lax.ppermute(value, "rows", pairs) for pairs in ALONG_X)
    return [value] + [lax.ppermute(value, "rows", pairs) for pairs in ALONG_Z]


def spread_over_rows(share):
    copies = jnp.broadcast_to(share[None], (ROWS,) + share.shape)
    return lax.all_to_all(copies, "rows", 0, 0, tiled=True)


def to_next_chip(value):
    return [lax.ppermute(value, "cols", pairs) for pairs in (ODD_TO_EVEN, ODD_TO_ODD)]


def body(sensitivity):
    x = sensitivity[0]
    rows = x.shape[0]
    column = lax.axis_index("cols")
    parity = column % 2
    basis_rows = x.shape[1] // ROWS // 2
    basis_at = (lax.axis_index("rows") * 2 + parity) * basis_rows
    info = jnp.stack([parity, column // 2, basis_at]).astype(jnp.int32)
    step = rows + basis_rows // SIDE

    packed = pack_main(info, x)
    main = [packed[0]] + [lax.ppermute(packed[k], "cols", CHIPS_ON[k]) for k in range(1, SIDE)]

    parts = lax.all_to_all(row_grams(x, packed[0]), "rows", 0, 0, tiled=True)
    parts = lax.all_to_all(jnp.sum(parts, axis=0), "cols", 0, 0, tiled=True)
    share = jnp.sum(parts, axis=0)

    packed = pack_ahead(info, x, share)
    ahead = [packed[0]] + [lax.ppermute(packed[k], "cols", CHIPS_ON[k]) for k in range(1, SIDE)]
    weights, upper, lower, gram = first_cayley(spread_over_rows(share))

    own_blocks = [jnp.stack(main)]
    ahead_blocks = [jnp.stack(ahead)]
    for sweep_round in range(ROUNDS - 1):
        lower = to_next_chip(lower)
        other = swap_core(weights)
        up, low = project(gram, weights)
        low = lax.ppermute(low, "cols", NEXT_SLOT)
        up0, up1, low1, cross = rotate_own(info, weights, other, own_blocks, rows, step)
        low0, keep, send = rotate_ahead(info, lower, cross, up0, ahead_blocks, rows, step)
        parts = sum_over_rows(keep + swap_core(send))
        own_blocks = [up0, low0, up1, low1]
        if sweep_round < ROUNDS - 2:
            up_m, passed = rotate_up(info, to_next_chip(upper), low, low1, ahead_blocks, step)
            ahead_blocks = [up_m, lax.ppermute(passed, "cols", CHIPS_ON[1])]
        else:
            received = [swap_core(value) for value in other_slot(info, parts[0], own_blocks, step)]
        weights, upper, lower, gram = cayley(up, low, parts)

    rotated, frame, column_scale = rotate_final(info, weights, gram, own_blocks + received, rows, step)
    return rotated, frame.reshape(2 * basis_rows, PAIR), column_scale.reshape(PAIR)


def solution(mesh):
    in_specs = (P("cols", "rows", None),)
    out_specs = (P(None, "rows", "cols"), P("rows", "cols"), P("cols"))
    return jax.shard_map(body, mesh=mesh, in_specs=in_specs, out_specs=out_specs, check_vma=False)
```

```python
import functools

import jax
import jax.numpy as jnp
from jax import lax
from jax.experimental import pallas as pl
from jax.experimental.pallas import tpu as pltpu
from jax.sharding import PartitionSpec as P

ROUNDS = 4
BLOCK = 128
PAIR = 256
SIDE = 4
ROWS = 16
COLS = 8
F32 = jnp.float32
BF16 = jnp.bfloat16
VMEM_LIMIT = 16 * 1024 * 1024

TURN_CORE = [(c, c ^ 1) for c in range(COLS)]
NEXT_SLOT = [(c, (c + 1) % COLS) for c in range(COLS)]
CHIPS_ON = [[(c, (c + 2 * k) % COLS) for c in range(COLS)] for k in range(SIDE)]
ODD_TO_EVEN = [(c, (c + 1) % COLS) for c in range(1, COLS, 2)]
ODD_TO_ODD = [(c, (c + 2) % COLS) for c in range(1, COLS, 2)]
ALONG_X = [[(r, r - r % SIDE + (r + k) % SIDE) for r in range(ROWS)] for k in range(1, SIDE)]
ALONG_Z = [[(r, (r + SIDE * k) % ROWS) for r in range(ROWS)] for k in range(1, SIDE)]


def mm(left, right):
    return jnp.dot(left, right, precision=lax.Precision.HIGHEST, preferred_element_type=F32)


def mm_t(left, right):
    return lax.dot_general(
        left, right, (((0,), (0,)), ((), ())), precision=lax.Precision.HIGHEST, preferred_element_type=F32
    )


def parts_of(value):
    high = value.astype(BF16)
    return high, (value - high.astype(F32)).astype(BF16)


def dot(left, right, axis):
    return lax.dot_general(left, right, (((axis,), (0,)), ((), ())), preferred_element_type=F32)


def mm3(left, right, axis=1):
    high, low = parts_of(left)
    right_high, right_low = parts_of(right)
    width = right.shape[1]
    if width < PAIR:
        both = dot(high, jnp.concatenate([right_high, right_low], axis=1), axis)
        return both[:, :width] + (both[:, width:] + dot(low, right_high, axis))
    return dot(high, right_high, axis) + (dot(high, right_low, axis) + dot(low, right_high, axis))


def call(kernel, grid, in_specs, out_specs, out_shape, scalars=0, scratch=(), flops=0, nbytes=0):
    return pl.pallas_call(
        kernel,
        grid_spec=pltpu.PrefetchScalarGridSpec(
            num_scalar_prefetch=scalars,
            grid=grid,
            in_specs=in_specs,
            out_specs=out_specs,
            scratch_shapes=list(scratch),
        ),
        out_shape=out_shape,
        compiler_params=pltpu.CompilerParams(vmem_limit_bytes=VMEM_LIMIT),
        cost_estimate=pl.CostEstimate(flops=flops, bytes_accessed=nbytes, transcendentals=0),
    )


def call_whole(kernel, args, out_shape, before=(), scratch=(), flops=0, nbytes=0):
    inner = kernel
    if before:
        inner = lambda *refs: kernel(*refs[: len(args)], *refs[len(args) + len(before):])
    return pl.pallas_call(
        inner,
        in_specs=[pl.BlockSpec(memory_space=pltpu.SMEM)]
        + [pl.BlockSpec(memory_space=pltpu.VMEM)] * (len(args) - 1)
        + [pl.BlockSpec(memory_space=pl.ANY)] * len(before),
        out_specs=[pl.BlockSpec(memory_space=pltpu.VMEM)] * len(out_shape),
        out_shape=out_shape,
        scratch_shapes=list(scratch),
        compiler_params=pltpu.CompilerParams(vmem_limit_bytes=VMEM_LIMIT),
        cost_estimate=pl.CostEstimate(flops=flops, bytes_accessed=nbytes, transcendentals=0),
    )(*args, *before)


def shape(*dims):
    return jax.ShapeDtypeStruct(dims, F32)


def whole(*dims):
    return pl.BlockSpec(dims, lambda *_: (0,) * len(dims))


def pack_main_kernel(info_ref, *refs):
    for x_ref, out_ref in zip(refs[:SIDE], refs[SIDE:]):
        out_ref[0, 0] = x_ref[:, :BLOCK]
        out_ref[0, 1] = x_ref[:, BLOCK:]


def pack_main(info, x):
    rows = x.shape[0]

    def columns(k):
        return pl.BlockSpec((rows, PAIR), lambda j, c: (0, 2 * ((c[1] + k) % SIDE) + j))

    return call(
        pack_main_kernel,
        (2,),
        [columns(k) for k in range(SIDE)],
        [pl.BlockSpec((1, 2, rows, BLOCK), lambda j, c: (j, 0, 0, 0))] * SIDE,
        [shape(2, 2, rows, BLOCK)] * SIDE,
        scalars=1,
        nbytes=8 * SIDE * rows * 2 * PAIR,
    )(info, *[x] * SIDE)


def pack_ahead_kernel(info_ref, *refs):
    parts_ref, shares_ref = refs[SIDE], refs[-1]
    shares_ref[...] = jnp.broadcast_to(jnp.sum(parts_ref[...], axis=0)[None], shares_ref.shape)
    for x_ref, out_ref in zip(refs[:SIDE], refs[SIDE + 1:]):
        out_ref[0] = x_ref[:, :BLOCK]
        out_ref[1] = x_ref[:, BLOCK:]


def pack_ahead(info, x, parts):
    rows = x.shape[0]
    shares = (ROWS,) + parts.shape[1:]

    def columns(k):
        return pl.BlockSpec((rows, PAIR), lambda i, c: (0, (2 * ((c[1] + k) % SIDE) + COLS - 1) % COLS))

    return call(
        pack_ahead_kernel,
        (1,),
        [columns(k) for k in range(SIDE)] + [whole(*parts.shape)],
        [whole(2, rows, BLOCK)] * SIDE + [whole(*shares)],
        [shape(2, rows, BLOCK)] * SIDE + [shape(*shares)],
        scalars=1,
        nbytes=8 * SIDE * rows * PAIR,
    )(info, *[x] * SIDE, parts)


def gram_kernel(x_ref, before_ref, out_ref):
    high, low = parts_of(x_ref[...])
    mixed = dot(high, low, 0)
    gram = dot(high, high, 0) + (mixed + mixed.T)
    for k, block in enumerate((gram[:BLOCK, :BLOCK], gram[:BLOCK, BLOCK:], gram[BLOCK:, BLOCK:])):
        out_ref[:, 0, k] = block.reshape(ROWS, BLOCK // ROWS, BLOCK)


def row_grams(x, before):
    rows = x.shape[0]
    return call(
        gram_kernel,
        (COLS,),
        [pl.BlockSpec((rows, PAIR), lambda s: (0, s)), pl.BlockSpec(memory_space=pl.ANY)],
        pl.BlockSpec((ROWS, 1, 3, BLOCK // ROWS, BLOCK), lambda s: (0, s, 0, 0, 0)),
        shape(ROWS, COLS, 3, BLOCK // ROWS, BLOCK),
        flops=2 * 2 * COLS * rows * PAIR * PAIR,
        nbytes=4 * COLS * (rows * PAIR + PAIR * PAIR),
    )(x, before)


def sum_kernel(info_ref, parts_ref, out_ref):
    out_ref[...] = jnp.sum(parts_ref[...], axis=0)


def sum_parts(info, parts, before):
    return call_whole(sum_kernel, (info, parts), [shape(*parts.shape[1:])], before, nbytes=4 * parts.size)[0]


def rotation_of(gram, x_ref, r_ref):
    rows = lax.broadcasted_iota(jnp.int32, (PAIR, PAIR), 0)
    columns = lax.broadcasted_iota(jnp.int32, (PAIR, PAIR), 1)
    eye = (rows == columns).astype(F32)
    on_diagonal = gram * eye
    across = jnp.sum(on_diagonal, axis=0, keepdims=True)
    down = jnp.sum(on_diagonal, axis=1, keepdims=True)
    spread = across - down
    totals = across + down
    skew = gram * spread / (2.0 * spread * spread + 0.5 * totals * totals)
    square = mm3(skew, skew)
    bound = jnp.max(jnp.sum(jnp.abs(square), axis=0))
    scale = 2.0 / (2.0 + bound)
    x_ref[...] = scale * (eye + skew)
    r_ref[...] = (1.0 - scale) * eye + scale * square

    def step(size):
        left = r_ref[...]
        x = x_ref[...]
        x_ref[...] = x + mm3(x, left)
        r_ref[...] = mm3(left, left)
        return size * size

    lax.while_loop(lambda size: size > 3e-4, step, bound / (2.0 + bound))
    x = x_ref[...]
    x = x + mm3(x, eye - x + mm3(skew, x))
    return 2.0 * x - eye


def cayley_kernel(fill, info_ref, *refs):
    weights_ref, up_ref, low_ref, gram_ref, x_ref, r_ref = refs[-6:]
    up, cross, low = fill(*refs[:-6])
    gram_ref[:BLOCK, :BLOCK] = up
    gram_ref[:BLOCK, BLOCK:] = cross
    gram_ref[BLOCK:, :BLOCK] = cross.T
    gram_ref[BLOCK:, BLOCK:] = low
    weights = rotation_of(gram_ref[...], x_ref, r_ref)
    weights_ref[...] = weights
    up_ref[...] = weights[:, :BLOCK]
    low_ref[...] = weights[:, BLOCK:]


def cayley_call(fill, args):
    return call_whole(
        functools.partial(cayley_kernel, fill),
        args,
        [shape(PAIR, PAIR), shape(PAIR, BLOCK), shape(PAIR, BLOCK), shape(PAIR, PAIR)],
        scratch=[pltpu.VMEM((PAIR, PAIR), F32)] * 2,
        flops=2 * 3 * 8 * PAIR**3,
        nbytes=20 * PAIR * PAIR,
    )


def first_cayley(info, blocks):
    return cayley_call(lambda ref: [ref[:, k].reshape(BLOCK, BLOCK) for k in range(3)], (info, blocks))


def cayley(info, up, low, parts):
    def fill(up_ref, low_ref, *part_refs):
        first, second, third, fourth = (ref[...] for ref in part_refs)
        return up_ref[...], (first + second) + (third + fourth), low_ref[...]

    return cayley_call(fill, (info, up, low, *parts))


def project_kernel(info_ref, gram_ref, weights_ref, up_ref, low_ref):
    weights = weights_ref[...]
    turned = mm3(gram_ref[...], weights)
    up_ref[...] = mm3(weights[:, :BLOCK], turned[:, :BLOCK], 0)
    low_ref[...] = mm3(weights[:, BLOCK:], turned[:, BLOCK:], 0)


def project(info, gram, weights):
    out = [shape(BLOCK, BLOCK)] * 2
    return call_whole(project_kernel, (info, gram, weights), out, flops=2 * 3 * 2 * PAIR**3, nbytes=12 * PAIR * PAIR)


def start_pair(info_ref, step, group, slot, up, low):
    share = step - up.shape[0]
    column = slot * PAIR - info_ref[2] - share * group
    rows = lax.broadcasted_iota(jnp.int32, (share, PAIR), 0)
    columns = lax.broadcasted_iota(jnp.int32, (share, PAIR), 1)
    basis = (rows == columns + column).astype(F32)
    return jnp.concatenate([jnp.concatenate([up, low], axis=1), basis], axis=0)


def groups_of(info_ref, step, refs, slots):
    if refs[0].shape[0] == SIDE:
        for group in range(SIDE):
            pairs = [(refs[2 * j][group], refs[2 * j + 1][group]) for j in range(len(slots))]
            yield group, [jnp.concatenate(pair, axis=1) for pair in pairs]
    else:
        for k, ref in enumerate(refs):
            group = lax.rem(info_ref[1] + SIDE - k, SIDE)
            yield group, [start_pair(info_ref, step, group, slot, ref[j, 0], ref[j, 1]) for j, slot in enumerate(slots)]


def own_kernel(rows, step, info_ref, own_ref, other_ref, *refs):
    up0_ref, up1_ref, low1_ref, cross_ref = refs[-4:]
    first = info_ref[0] == 0
    weights0 = jnp.where(first, own_ref[...], other_ref[...])
    weights1 = jnp.where(first, other_ref[:, :BLOCK], own_ref[:, :BLOCK])
    slot = 2 * info_ref[1]
    cross = jnp.zeros((BLOCK, BLOCK), F32)
    for group, (pair0, pair1) in groups_of(info_ref, step, refs[:-4], (slot, slot + 1)):
        turned = mm3(pair0, weights0)
        up1 = mm3(pair1, weights1)
        up0_ref[group] = turned[:, :BLOCK]
        low1_ref[group] = turned[:, BLOCK:]
        up1_ref[group] = up1
        cross = cross + mm3(up1[:rows], turned[:rows, BLOCK:], 0)
    cross_ref[...] = cross


def rotate_own(info, own, other, blocks, before, rows, step):
    return call_whole(
        functools.partial(own_kernel, rows, step),
        (info, own, other, *blocks),
        [shape(SIDE, step, BLOCK)] * 3 + [shape(BLOCK, BLOCK)],
        before,
        flops=2 * 3 * SIDE * step * 4 * BLOCK * PAIR,
        nbytes=4 * 7 * SIDE * step * BLOCK,
    )


def ahead_kernel(rows, step, info_ref, even_ref, odd_ref, upper_ref, cross_ref, up0_ref, *refs):
    low0_ref, keep_ref, send_ref, upper_out_ref = refs[-4:]
    upper_out_ref[...] = upper_ref[...]
    weights = even_ref[...] + odd_ref[...]
    slot = (2 * info_ref[1] + COLS - 1) % COLS
    total = jnp.zeros((BLOCK, BLOCK), F32)
    for group, (pair,) in groups_of(info_ref, step, refs[:-4], (slot,)):
        low0 = mm3(pair, weights)
        low0_ref[group] = low0
        total = total + mm3(up0_ref[group, :rows], low0[:rows], 0)
    first = info_ref[0] == 0
    keep_ref[...] = jnp.where(first, total, cross_ref[...])
    send_ref[...] = jnp.where(first, cross_ref[...], total)


def rotate_ahead(info, lower, upper, cross, up0, blocks, rows, step):
    return call_whole(
        functools.partial(ahead_kernel, rows, step),
        (info, *lower, upper, cross, up0, *blocks),
        [shape(SIDE, step, BLOCK)] + [shape(BLOCK, BLOCK)] * 2 + [shape(PAIR, BLOCK)],
        flops=2 * 3 * SIDE * step * 2 * BLOCK * PAIR,
        nbytes=4 * 4 * SIDE * step * BLOCK,
    )


def up_kernel(step, info_ref, even_ref, odd_ref, low1_ref, *refs):
    up_ref, pass_ref = refs[-2:]
    weights = even_ref[...] + odd_ref[...]
    slot = (2 * info_ref[1] + COLS - 1) % COLS
    for group, (pair,) in groups_of(info_ref, step, refs[:-2], (slot,)):
        up_ref[group] = mm3(pair, weights)
    pass_ref[...] = low1_ref[...]


def rotate_up(info, upper, low1, blocks, before, step):
    return call_whole(
        functools.partial(up_kernel, step),
        (info, *upper, low1, *blocks),
        [shape(SIDE, step, BLOCK)] * 2,
        before,
        flops=2 * 3 * SIDE * step * BLOCK * PAIR,
        nbytes=4 * 5 * SIDE * step * BLOCK,
    )


def other_slot_kernel(info_ref, up0_ref, low0_ref, up1_ref, low1_ref, up_ref, low_ref):
    first = info_ref[0] == 0
    up_ref[...] = jnp.where(first, up1_ref[...], up0_ref[...])
    low_ref[...] = jnp.where(first, low1_ref[...], low0_ref[...])


def other_slot(info, blocks, before):
    return call_whole(other_slot_kernel, (info, *blocks), [shape(*blocks[0].shape)] * 2, before, nbytes=24 * blocks[0].size)


def final_kernel(rows, total, info_ref, weights_ref, gram_ref, up0_ref, low0_ref, up1_ref, low1_ref, ru_ref, rl_ref,
                 out_ref, frame_ref, scale_ref):
    weights = weights_ref[...]
    first = info_ref[0] == 0
    i = pl.program_id(0)
    up = jnp.where(first, up0_ref[i], up1_ref[i])
    low = jnp.where(first, low0_ref[i], low1_ref[i])
    mine = mm3(jnp.concatenate([up, low], axis=1), weights)
    theirs = mm3(jnp.concatenate([ru_ref[i], rl_ref[i]], axis=1), weights)
    for k, turned in enumerate((jnp.where(first, mine, theirs), jnp.where(first, theirs, mine))):
        out_ref[k] = turned[:rows]
        frame_ref[k] = turned[rows:]

    @pl.when(i == 0)
    def _():
        squares = jnp.sum(weights * mm3(gram_ref[...], weights), axis=0, keepdims=True)
        scale_ref[...] = jnp.sqrt(squares / total)


def rotate_final(info, weights, gram, blocks, rows, step):
    share = step - rows
    return call(
        functools.partial(final_kernel, rows, float(rows * COLS * ROWS)),
        (SIDE,),
        [pl.BlockSpec(memory_space=pltpu.VMEM)] * 8,
        [
            pl.BlockSpec((2, rows, PAIR), lambda i, c: (i, 0, 0)),
            pl.BlockSpec((2, share, PAIR), lambda i, c: (0, i, 0)),
            whole(1, PAIR),
        ],
        [shape(COLS, rows, PAIR), shape(2, SIDE * share, PAIR), shape(1, PAIR)],
        scalars=1,
        flops=2 * 3 * 2 * SIDE * step * PAIR * PAIR,
        nbytes=4 * 4 * SIDE * step * PAIR,
    )(info, weights, gram, *blocks)


def swap_core(value):
    return lax.ppermute(value, "cols", TURN_CORE)


def sum_over_rows(value):
    value = value + sum(lax.ppermute(value, "rows", pairs) for pairs in ALONG_X)
    return [value] + [lax.ppermute(value, "rows", pairs) for pairs in ALONG_Z]


def to_next_chip(value):
    return [lax.ppermute(value, "cols", pairs) for pairs in (ODD_TO_EVEN, ODD_TO_ODD)]


def body(sensitivity):
    x = sensitivity[0]
    rows = x.shape[0]
    column = lax.axis_index("cols")
    parity = column % 2
    basis_rows = x.shape[1] // ROWS // 2
    basis_at = (lax.axis_index("rows") * 2 + parity) * basis_rows
    info = jnp.stack([parity, column // 2, basis_at]).astype(jnp.int32)
    step = rows + basis_rows // SIDE

    packed = pack_main(info, x)
    main = [packed[0]] + [lax.ppermute(packed[k], "cols", CHIPS_ON[k]) for k in range(1, SIDE)]

    parts = lax.all_to_all(row_grams(x, packed[0]), "rows", 0, 0, tiled=True)
    parts = lax.all_to_all(sum_parts(info, parts, main[1:]), "cols", 0, 0, tiled=True)
    *packed, shares = pack_ahead(info, x, parts)
    ahead = [packed[0]] + [lax.ppermute(packed[k], "cols", CHIPS_ON[k]) for k in range(1, SIDE)]
    weights, upper, lower, gram = first_cayley(info, lax.all_to_all(shares, "rows", 0, 0, tiled=True))

    own_blocks = main
    ahead_blocks = [value[None] for value in ahead]
    for sweep_round in range(ROUNDS - 1):
        lower = to_next_chip(lower)
        other = swap_core(weights)
        up, low = project(info, gram, weights)
        up0, up1, low1, cross = rotate_own(info, weights, other, own_blocks, [up], rows, step)
        low = lax.ppermute(low, "cols", NEXT_SLOT)
        low0, keep, send, upper = rotate_ahead(info, lower, upper, cross, up0, ahead_blocks, rows, step)
        parts = sum_over_rows(keep + swap_core(send))
        own_blocks = [up0, low0, up1, low1]
        if sweep_round < ROUNDS - 2:
            up_m, passed = rotate_up(info, to_next_chip(upper), low1, ahead_blocks, [low], step)
            ahead_blocks = [up_m, lax.ppermute(passed, "cols", CHIPS_ON[1])]
        else:
            received = [swap_core(value) for value in other_slot(info, own_blocks, [parts[0]])]
        weights, upper, lower, gram = cayley(info, up, low, parts)

    rotated, frame, column_scale = rotate_final(info, weights, gram, own_blocks + received, rows, step)
    return rotated, frame.reshape(2 * basis_rows, PAIR), column_scale.reshape(PAIR)


def solution(mesh):
    in_specs = (P("cols", "rows", None),)
    out_specs = (P(None, "rows", "cols"), P("rows", "cols"), P("cols"))
    return jax.shard_map(body, mesh=mesh, in_specs=in_specs, out_specs=out_specs, check_vma=False)
```

```python
import functools

import jax
import jax.numpy as jnp
from jax import lax
from jax.experimental import pallas as pl
from jax.experimental.pallas import tpu as pltpu
from jax.sharding import PartitionSpec as P

ROUNDS = 4
BLOCK = 128
PAIR = 256
SIDE = 4
ROWS = 16
COLS = 8
F32 = jnp.float32
BF16 = jnp.bfloat16
VMEM_LIMIT = 16 * 1024 * 1024

TURN_CORE = [(c, c ^ 1) for c in range(COLS)]
NEXT_SLOT = [(c, (c + 1) % COLS) for c in range(COLS)]
CHIPS_ON = [[(c, (c + 2 * k) % COLS) for c in range(COLS)] for k in range(SIDE)]
ODD_TO_EVEN = [(c, (c + 1) % COLS) for c in range(1, COLS, 2)]
ODD_TO_ODD = [(c, (c + 2) % COLS) for c in range(1, COLS, 2)]
ALONG_X = [[(r, r - r % SIDE + (r + k) % SIDE) for r in range(ROWS)] for k in range(1, SIDE)]
ALONG_Z = [[(r, (r + SIDE * k) % ROWS) for r in range(ROWS)] for k in range(1, SIDE)]


def mm(left, right):
    return jnp.dot(left, right, precision=lax.Precision.HIGHEST, preferred_element_type=F32)


def mm_t(left, right):
    return lax.dot_general(
        left, right, (((0,), (0,)), ((), ())), precision=lax.Precision.HIGHEST, preferred_element_type=F32
    )


def parts_of(value):
    high = value.astype(BF16)
    return high, (value - high.astype(F32)).astype(BF16)


def dot(left, right, axis):
    return lax.dot_general(left, right, (((axis,), (0,)), ((), ())), preferred_element_type=F32)


def mm3(left, right, axis=1):
    high, low = parts_of(left)
    right_high, right_low = parts_of(right)
    width = right.shape[1]
    if width < PAIR:
        both = dot(high, jnp.concatenate([right_high, right_low], axis=1), axis)
        return both[:, :width] + (both[:, width:] + dot(low, right_high, axis))
    return dot(high, right_high, axis) + (dot(high, right_low, axis) + dot(low, right_high, axis))


def call(kernel, grid, in_specs, out_specs, out_shape, scalars=0, scratch=(), flops=0, nbytes=0):
    return pl.pallas_call(
        kernel,
        grid_spec=pltpu.PrefetchScalarGridSpec(
            num_scalar_prefetch=scalars,
            grid=grid,
            in_specs=in_specs,
            out_specs=out_specs,
            scratch_shapes=list(scratch),
        ),
        out_shape=out_shape,
        compiler_params=pltpu.CompilerParams(vmem_limit_bytes=VMEM_LIMIT),
        cost_estimate=pl.CostEstimate(flops=flops, bytes_accessed=nbytes, transcendentals=0),
    )


def call_whole(kernel, args, out_shape, before=(), scratch=(), flops=0, nbytes=0):
    inner = kernel
    if before:
        inner = lambda *refs: kernel(*refs[: len(args)], *refs[len(args) + len(before):])
    return pl.pallas_call(
        inner,
        in_specs=[pl.BlockSpec(memory_space=pltpu.SMEM)]
        + [pl.BlockSpec(memory_space=pltpu.VMEM)] * (len(args) - 1)
        + [pl.BlockSpec(memory_space=pl.ANY)] * len(before),
        out_specs=[pl.BlockSpec(memory_space=pltpu.VMEM)] * len(out_shape),
        out_shape=out_shape,
        scratch_shapes=list(scratch),
        compiler_params=pltpu.CompilerParams(vmem_limit_bytes=VMEM_LIMIT),
        cost_estimate=pl.CostEstimate(flops=flops, bytes_accessed=nbytes, transcendentals=0),
    )(*args, *before)


def shape(*dims):
    return jax.ShapeDtypeStruct(dims, F32)


def whole(*dims):
    return pl.BlockSpec(dims, lambda *_: (0,) * len(dims))


def pack_main_kernel(info_ref, *refs):
    for x_ref, out_ref in zip(refs[:SIDE], refs[SIDE:]):
        out_ref[0, 0] = x_ref[:, :BLOCK]
        out_ref[0, 1] = x_ref[:, BLOCK:]


def pack_main(info, x):
    rows = x.shape[0]

    def columns(k):
        return pl.BlockSpec((rows, PAIR), lambda j, c: (0, 2 * ((c[1] + k) % SIDE) + j))

    return call(
        pack_main_kernel,
        (2,),
        [columns(k) for k in range(SIDE)],
        [pl.BlockSpec((1, 2, rows, BLOCK), lambda j, c: (j, 0, 0, 0))] * SIDE,
        [shape(2, 2, rows, BLOCK)] * SIDE,
        scalars=1,
        nbytes=8 * SIDE * rows * 2 * PAIR,
    )(info, *[x] * SIDE)


def pack_ahead_kernel(info_ref, *refs):
    for x_ref, out_ref in zip(refs[:SIDE], refs[-SIDE:]):
        out_ref[0] = x_ref[:, :BLOCK]
        out_ref[1] = x_ref[:, BLOCK:]


def pack_ahead(info, x, before):
    rows = x.shape[0]

    def columns(k):
        return pl.BlockSpec((rows, PAIR), lambda i, c: (0, (2 * ((c[1] + k) % SIDE) + COLS - 1) % COLS))

    return call(
        pack_ahead_kernel,
        (1,),
        [columns(k) for k in range(SIDE)] + [pl.BlockSpec(memory_space=pl.ANY)] * len(before),
        [whole(2, rows, BLOCK)] * SIDE,
        [shape(2, rows, BLOCK)] * SIDE,
        scalars=1,
        nbytes=8 * SIDE * rows * PAIR,
    )(info, *[x] * SIDE, *before)


def gram_kernel(info_ref, *refs):
    keep_ref, send_ref = refs[-2:]
    first = info_ref[0] == 0
    grams = []
    for slot in range(2):
        squares = jnp.zeros((PAIR, PAIR), F32)
        mixed = jnp.zeros((PAIR, PAIR), F32)
        for ref in refs[:-2]:
            high, low = parts_of(jnp.concatenate([ref[slot, 0], ref[slot, 1]], axis=1))
            squares = squares + dot(high, high, 0)
            mixed = mixed + dot(high, low, 0)
        grams.append(squares + (mixed + mixed.T))
    for ref, gram in ((keep_ref, jnp.where(first, grams[0], grams[1])), (send_ref, jnp.where(first, grams[1], grams[0]))):
        for k, block in enumerate((gram[:BLOCK, :BLOCK], gram[:BLOCK, BLOCK:], gram[BLOCK:, BLOCK:])):
            ref[:, k] = block.reshape(ROWS, BLOCK // ROWS, BLOCK)


def first_grams(info, main):
    out = shape(ROWS, 3, BLOCK // ROWS, BLOCK)
    return call_whole(
        gram_kernel, (info, *main), [out, out], flops=2 * 2 * 4 * main[0].size * PAIR, nbytes=16 * main[0].size
    )


def spread_kernel(info_ref, parts_ref, out_ref):
    out_ref[...] = jnp.broadcast_to(jnp.sum(parts_ref[...], axis=0)[None], out_ref.shape)


def spread_parts(info, parts, before):
    return call_whole(spread_kernel, (info, parts), [shape(*parts.shape)], before, nbytes=8 * parts.size)[0]


def rotation_of(gram, x_ref, r_ref):
    rows = lax.broadcasted_iota(jnp.int32, (PAIR, PAIR), 0)
    columns = lax.broadcasted_iota(jnp.int32, (PAIR, PAIR), 1)
    eye = (rows == columns).astype(F32)
    on_diagonal = gram * eye
    across = jnp.sum(on_diagonal, axis=0, keepdims=True)
    down = jnp.sum(on_diagonal, axis=1, keepdims=True)
    spread = across - down
    totals = across + down
    skew = gram * spread / (2.0 * spread * spread + 0.5 * totals * totals)
    square = mm3(skew, skew)
    bound = jnp.max(jnp.sum(jnp.abs(square), axis=0))
    scale = 2.0 / (2.0 + bound)
    x_ref[...] = scale * (eye + skew)
    r_ref[...] = (1.0 - scale) * eye + scale * square

    def step(size):
        left = r_ref[...]
        x = x_ref[...]
        x_ref[...] = x + mm3(x, left)
        r_ref[...] = mm3(left, left)
        return size * size

    lax.while_loop(lambda size: size > 3e-4, step, bound / (2.0 + bound))
    x = x_ref[...]
    x = x + mm3(x, eye - x + mm3(skew, x))
    return 2.0 * x - eye


def cayley_kernel(fill, info_ref, *refs):
    weights_ref, up_ref, low_ref, gram_ref, x_ref, r_ref = refs[-6:]
    up, cross, low = fill(info_ref, *refs[:-6])
    gram_ref[:BLOCK, :BLOCK] = up
    gram_ref[:BLOCK, BLOCK:] = cross
    gram_ref[BLOCK:, :BLOCK] = cross.T
    gram_ref[BLOCK:, BLOCK:] = low
    weights = rotation_of(gram_ref[...], x_ref, r_ref)
    weights_ref[...] = weights
    up_ref[...] = weights[:, :BLOCK]
    low_ref[...] = weights[:, BLOCK:]


def cayley_call(fill, args, before=()):
    return call_whole(
        functools.partial(cayley_kernel, fill),
        args,
        [shape(PAIR, PAIR), shape(PAIR, BLOCK), shape(PAIR, BLOCK), shape(PAIR, PAIR)],
        before,
        scratch=[pltpu.VMEM((PAIR, PAIR), F32)] * 2,
        flops=2 * 3 * 8 * PAIR**3,
        nbytes=20 * PAIR * PAIR,
    )


def first_cayley(info, blocks, before):
    return cayley_call(lambda _, ref: [ref[:, k].reshape(BLOCK, BLOCK) for k in range(3)], (info, blocks), before)


def cayley(info, up, across_chips, across_cores, parts):
    def fill(info_ref, up_ref, chips_ref, cores_ref, *part_refs):
        first, second, third, fourth = (ref[...] for ref in part_refs)
        low = jnp.where(info_ref[0] == 0, chips_ref[-BLOCK:], cores_ref[-BLOCK:])
        return up_ref[...], (first + second) + (third + fourth), low

    return cayley_call(fill, (info, up, across_chips, across_cores, *parts))


def project_kernel(info_ref, gram_ref, weights_ref, up_ref, low_ref):
    weights = weights_ref[...]
    turned = mm3(gram_ref[...], weights)
    up_ref[...] = mm3(weights[:, :BLOCK], turned[:, :BLOCK], 0)
    low_ref[...] = mm3(weights[:, BLOCK:], turned[:, BLOCK:], 0)


def project(info, gram, weights):
    out = [shape(BLOCK, BLOCK)] * 2
    return call_whole(project_kernel, (info, gram, weights), out, flops=2 * 3 * 2 * PAIR**3, nbytes=12 * PAIR * PAIR)


def start_pair(info_ref, step, group, slot, up, low):
    share = step - up.shape[0]
    column = slot * PAIR - info_ref[2] - share * group
    rows = lax.broadcasted_iota(jnp.int32, (share, PAIR), 0)
    columns = lax.broadcasted_iota(jnp.int32, (share, PAIR), 1)
    basis = (rows == columns + column).astype(F32)
    return jnp.concatenate([jnp.concatenate([up, low], axis=1), basis], axis=0)


def groups_of(info_ref, step, refs, slots):
    if refs[0].shape[0] == SIDE:
        for group in range(SIDE):
            pairs = [(refs[2 * j][group], refs[2 * j + 1][group]) for j in range(len(slots))]
            yield group, [jnp.concatenate(pair, axis=1) for pair in pairs]
    else:
        for k, ref in enumerate(refs):
            group = lax.rem(info_ref[1] + SIDE - k, SIDE)
            yield group, [start_pair(info_ref, step, group, slot, ref[j, 0], ref[j, 1]) for j, slot in enumerate(slots)]


def own_kernel(rows, step, info_ref, own_ref, other_ref, *refs):
    up0_ref, up1_ref, low1_ref, cross_ref = refs[-4:]
    first = info_ref[0] == 0
    weights0 = jnp.where(first, own_ref[...], other_ref[...])
    weights1 = jnp.where(first, other_ref[:, :BLOCK], own_ref[:, :BLOCK])
    slot = 2 * info_ref[1]
    cross = jnp.zeros((BLOCK, BLOCK), F32)
    for group, (pair0, pair1) in groups_of(info_ref, step, refs[:-4], (slot, slot + 1)):
        turned = mm3(pair0, weights0)
        up1 = mm3(pair1, weights1)
        up0_ref[group] = turned[:, :BLOCK]
        low1_ref[group] = turned[:, BLOCK:]
        up1_ref[group] = up1
        cross = cross + mm3(up1[:rows], turned[:rows, BLOCK:], 0)
    cross_ref[...] = cross


def rotate_own(info, own, other, blocks, rows, step):
    return call_whole(
        functools.partial(own_kernel, rows, step),
        (info, own, other, *blocks),
        [shape(SIDE, step, BLOCK)] * 3 + [shape(BLOCK, BLOCK)],
        flops=2 * 3 * SIDE * step * 4 * BLOCK * PAIR,
        nbytes=4 * 7 * SIDE * step * BLOCK,
    )


def ahead_kernel(rows, step, info_ref, even_ref, odd_ref, upper_ref, low_ref, cross_ref, up0_ref, *refs):
    low0_ref, keep_ref, send_ref, bundle_ref = refs[-4:]
    low = low_ref[...]
    if bundle_ref.shape[0] > BLOCK:
        bundle_ref[:PAIR] = upper_ref[...]
    bundle_ref[-BLOCK:] = low
    send_ref[BLOCK:] = low
    weights = even_ref[...] + odd_ref[...]
    slot = (2 * info_ref[1] + COLS - 1) % COLS
    total = jnp.zeros((BLOCK, BLOCK), F32)
    for group, (pair,) in groups_of(info_ref, step, refs[:-4], (slot,)):
        low0 = mm3(pair, weights)
        low0_ref[group] = low0
        total = total + mm3(up0_ref[group, :rows], low0[:rows], 0)
    first = info_ref[0] == 0
    keep_ref[...] = jnp.where(first, total, cross_ref[...])
    send_ref[:BLOCK] = jnp.where(first, cross_ref[...], total)


def rotate_ahead(info, lower, upper, low, cross, up0, blocks, last, rows, step):
    return call_whole(
        functools.partial(ahead_kernel, rows, step),
        (info, *lower, upper, low, cross, up0, *blocks),
        [shape(SIDE, step, BLOCK), shape(BLOCK, BLOCK), shape(2 * BLOCK, BLOCK), shape(BLOCK if last else 3 * BLOCK, BLOCK)],
        flops=2 * 3 * SIDE * step * 2 * BLOCK * PAIR,
        nbytes=4 * 4 * SIDE * step * BLOCK,
    )


def up_kernel(step, info_ref, even_ref, odd_ref, low1_ref, *refs):
    up_ref, pass_ref = refs[-2:]
    weights = even_ref[:PAIR] + odd_ref[:PAIR]
    slot = (2 * info_ref[1] + COLS - 1) % COLS
    for group, (pair,) in groups_of(info_ref, step, refs[:-2], (slot,)):
        up_ref[group] = mm3(pair, weights)
    pass_ref[...] = low1_ref[...]


def rotate_up(info, upper, low1, blocks, step):
    return call_whole(
        functools.partial(up_kernel, step),
        (info, *upper, low1, *blocks),
        [shape(SIDE, step, BLOCK)] * 2,
        flops=2 * 3 * SIDE * step * BLOCK * PAIR,
        nbytes=4 * 5 * SIDE * step * BLOCK,
    )


def other_slot_kernel(info_ref, up0_ref, low0_ref, up1_ref, low1_ref, up_ref, low_ref):
    first = info_ref[0] == 0
    up_ref[...] = jnp.where(first, up1_ref[...], up0_ref[...])
    low_ref[...] = jnp.where(first, low1_ref[...], low0_ref[...])


def other_slot(info, blocks, before):
    return call_whole(other_slot_kernel, (info, *blocks), [shape(*blocks[0].shape)] * 2, before, nbytes=24 * blocks[0].size)


def final_kernel(rows, total, info_ref, weights_ref, gram_ref, up0_ref, low0_ref, up1_ref, low1_ref, ru_ref, rl_ref,
                 out_ref, frame_ref, scale_ref):
    weights = weights_ref[...]
    first = info_ref[0] == 0
    i = pl.program_id(0)
    up = jnp.where(first, up0_ref[i], up1_ref[i])
    low = jnp.where(first, low0_ref[i], low1_ref[i])
    mine = mm3(jnp.concatenate([up, low], axis=1), weights)
    theirs = mm3(jnp.concatenate([ru_ref[i], rl_ref[i]], axis=1), weights)
    for k, turned in enumerate((jnp.where(first, mine, theirs), jnp.where(first, theirs, mine))):
        out_ref[k] = turned[:rows]
        frame_ref[k] = turned[rows:]

    @pl.when(i == 0)
    def _():
        squares = jnp.sum(weights * mm3(gram_ref[...], weights), axis=0, keepdims=True)
        scale_ref[...] = jnp.sqrt(squares / total)


def rotate_final(info, weights, gram, blocks, rows, step):
    share = step - rows
    return call(
        functools.partial(final_kernel, rows, float(rows * COLS * ROWS)),
        (SIDE,),
        [pl.BlockSpec(memory_space=pltpu.VMEM)] * 8,
        [
            pl.BlockSpec((2, rows, PAIR), lambda i, c: (i, 0, 0)),
            pl.BlockSpec((2, share, PAIR), lambda i, c: (0, i, 0)),
            whole(1, PAIR),
        ],
        [shape(COLS, rows, PAIR), shape(2, SIDE * share, PAIR), shape(1, PAIR)],
        scalars=1,
        flops=2 * 3 * 2 * SIDE * step * PAIR * PAIR,
        nbytes=4 * 4 * SIDE * step * PAIR,
    )(info, weights, gram, *blocks)


def swap_core(value):
    return lax.ppermute(value, "cols", TURN_CORE)


def sum_over_rows(value):
    value = value + sum(lax.ppermute(value, "rows", pairs) for pairs in ALONG_X)
    return [value] + [lax.ppermute(value, "rows", pairs) for pairs in ALONG_Z]


def to_next_chip(value):
    return [lax.ppermute(value, "cols", pairs) for pairs in (ODD_TO_EVEN, ODD_TO_ODD)]


def body(sensitivity):
    x = sensitivity[0]
    rows = x.shape[0]
    column = lax.axis_index("cols")
    parity = column % 2
    basis_rows = x.shape[1] // ROWS // 2
    basis_at = (lax.axis_index("rows") * 2 + parity) * basis_rows
    info = jnp.stack([parity, column // 2, basis_at]).astype(jnp.int32)
    step = rows + basis_rows // SIDE

    packed = pack_main(info, x)
    main = [packed[0]] + [lax.ppermute(packed[k], "cols", CHIPS_ON[k]) for k in range(1, SIDE)]

    keep, send = first_grams(info, main)
    packed = pack_ahead(info, x, main[1:])
    ahead = [packed[0]] + [lax.ppermute(packed[k], "cols", CHIPS_ON[k]) for k in range(1, SIDE)]
    parts = lax.all_to_all(keep + swap_core(send), "rows", 0, 0, tiled=True)
    parts = lax.all_to_all(spread_parts(info, parts, [ahead[1], ahead[3]]), "rows", 0, 0, tiled=True)
    weights, upper, lower, gram = first_cayley(info, parts, [ahead[2]])

    own_blocks = main
    ahead_blocks = [value[None] for value in ahead]
    for sweep_round in range(ROUNDS - 1):
        last = sweep_round == ROUNDS - 2
        lower = to_next_chip(lower)
        up, low = project(info, gram, weights)
        up0, up1, low1, cross = rotate_own(info, weights, swap_core(weights), own_blocks, rows, step)
        low0, keep, send, bundle = rotate_ahead(info, lower, upper, low, cross, up0, ahead_blocks, last, rows, step)
        received = swap_core(send)
        parts = sum_over_rows(keep + received[:BLOCK])
        own_blocks = [up0, low0, up1, low1]
        bundles = to_next_chip(bundle)
        if last:
            other_blocks = [swap_core(value) for value in other_slot(info, own_blocks, [parts[0]])]
        else:
            up_m, passed = rotate_up(info, bundles, low1, ahead_blocks, step)
            ahead_blocks = [up_m, lax.ppermute(passed, "cols", CHIPS_ON[1])]
        weights, upper, lower, gram = cayley(info, up, bundles[0], received, parts)

    rotated, frame, column_scale = rotate_final(info, weights, gram, own_blocks + other_blocks, rows, step)
    return rotated, frame.reshape(2 * basis_rows, PAIR), column_scale.reshape(PAIR)


def solution(mesh):
    in_specs = (P("cols", "rows", None),)
    out_specs = (P(None, "rows", "cols"), P("rows", "cols"), P("cols"))
    return jax.shard_map(body, mesh=mesh, in_specs=in_specs, out_specs=out_specs, check_vma=False)
```

```python
import functools

import jax
import jax.numpy as jnp
from jax import lax
from jax.experimental import pallas as pl
from jax.experimental.pallas import tpu as pltpu
from jax.sharding import PartitionSpec as P

ROUNDS = 4
BLOCK = 128
PAIR = 256
SIDE = 4
ROWS = 16
COLS = 8
F32 = jnp.float32
BF16 = jnp.bfloat16
VMEM_LIMIT = 16 * 1024 * 1024

TURN_CORE = [(c, c ^ 1) for c in range(COLS)]
NEXT_SLOT = [(c, (c + 1) % COLS) for c in range(COLS)]
CHIPS_ON = [[(c, (c + 2 * k) % COLS) for c in range(COLS)] for k in range(SIDE)]
ODD_TO_EVEN = [(c, (c + 1) % COLS) for c in range(1, COLS, 2)]
EVEN_TO_ODD = [(c, c + 1) for c in range(0, COLS, 2)]
ALONG_X = [[(r, r - r % SIDE + (r + k) % SIDE) for r in range(ROWS)] for k in range(1, SIDE)]
ALONG_Z = [[(r, (r + SIDE * k) % ROWS) for r in range(ROWS)] for k in range(1, SIDE)]


def mm(left, right):
    return jnp.dot(left, right, precision=lax.Precision.HIGHEST, preferred_element_type=F32)


def mm_t(left, right):
    return lax.dot_general(
        left, right, (((0,), (0,)), ((), ())), precision=lax.Precision.HIGHEST, preferred_element_type=F32
    )


def parts_of(value):
    high = value.astype(BF16)
    return high, (value - high.astype(F32)).astype(BF16)


def dot(left, right, axis):
    return lax.dot_general(left, right, (((axis,), (0,)), ((), ())), preferred_element_type=F32)


def mm3(left, right, axis=1):
    high, low = parts_of(left)
    right_high, right_low = parts_of(right)
    width = right.shape[1]
    if width < PAIR:
        both = dot(high, jnp.concatenate([right_high, right_low], axis=1), axis)
        return both[:, :width] + (both[:, width:] + dot(low, right_high, axis))
    return dot(high, right_high, axis) + (dot(high, right_low, axis) + dot(low, right_high, axis))


def call(kernel, grid, in_specs, out_specs, out_shape, scalars=0, scratch=(), flops=0, nbytes=0):
    return pl.pallas_call(
        kernel,
        grid_spec=pltpu.PrefetchScalarGridSpec(
            num_scalar_prefetch=scalars,
            grid=grid,
            in_specs=in_specs,
            out_specs=out_specs,
            scratch_shapes=list(scratch),
        ),
        out_shape=out_shape,
        compiler_params=pltpu.CompilerParams(vmem_limit_bytes=VMEM_LIMIT),
        cost_estimate=pl.CostEstimate(flops=flops, bytes_accessed=nbytes, transcendentals=0),
    )


def call_whole(kernel, args, out_shape, before=(), scratch=(), flops=0, nbytes=0):
    inner = kernel
    if before:
        inner = lambda *refs: kernel(*refs[: len(args)], *refs[len(args) + len(before):])
    return pl.pallas_call(
        inner,
        in_specs=[pl.BlockSpec(memory_space=pltpu.SMEM)]
        + [pl.BlockSpec(memory_space=pltpu.VMEM)] * (len(args) - 1)
        + [pl.BlockSpec(memory_space=pl.ANY)] * len(before),
        out_specs=[pl.BlockSpec(memory_space=pltpu.VMEM)] * len(out_shape),
        out_shape=out_shape,
        scratch_shapes=list(scratch),
        compiler_params=pltpu.CompilerParams(vmem_limit_bytes=VMEM_LIMIT),
        cost_estimate=pl.CostEstimate(flops=flops, bytes_accessed=nbytes, transcendentals=0),
    )(*args, *before)


def shape(*dims):
    return jax.ShapeDtypeStruct(dims, F32)


def whole(*dims):
    return pl.BlockSpec(dims, lambda *_: (0,) * len(dims))


def pack_main_kernel(info_ref, *refs):
    for x_ref, out_ref in zip(refs[:SIDE], refs[SIDE:]):
        out_ref[0, 0] = x_ref[:, :BLOCK]
        out_ref[0, 1] = x_ref[:, BLOCK:]


def pack_main(info, x):
    rows = x.shape[0]

    def columns(k):
        return pl.BlockSpec((rows, PAIR), lambda j, c: (0, 2 * ((c[1] + k) % SIDE) + j))

    return call(
        pack_main_kernel,
        (2,),
        [columns(k) for k in range(SIDE)],
        [pl.BlockSpec((1, 2, rows, BLOCK), lambda j, c: (j, 0, 0, 0))] * SIDE,
        [shape(2, 2, rows, BLOCK)] * SIDE,
        scalars=1,
        nbytes=8 * SIDE * rows * 2 * PAIR,
    )(info, *[x] * SIDE)


def pack_ahead_kernel(info_ref, *refs):
    for x_ref, out_ref in zip(refs[:SIDE], refs[-SIDE:]):
        out_ref[0] = x_ref[:, :BLOCK]
        out_ref[1] = x_ref[:, BLOCK:]


def pack_ahead(info, x, before):
    rows = x.shape[0]

    def columns(k):
        return pl.BlockSpec((rows, PAIR), lambda i, c: (0, (2 * ((c[1] + k) % SIDE) + COLS - 1) % COLS))

    return call(
        pack_ahead_kernel,
        (1,),
        [columns(k) for k in range(SIDE)] + [pl.BlockSpec(memory_space=pl.ANY)] * len(before),
        [whole(2, rows, BLOCK)] * SIDE,
        [shape(2, rows, BLOCK)] * SIDE,
        scalars=1,
        nbytes=8 * SIDE * rows * PAIR,
    )(info, *[x] * SIDE, *before)


def gram_kernel(info_ref, *refs):
    keep_ref, send_ref = refs[-2:]
    first = info_ref[0] == 0
    grams = []
    for slot in range(2):
        squares = jnp.zeros((PAIR, PAIR), F32)
        mixed = jnp.zeros((PAIR, PAIR), F32)
        for ref in refs[:-2]:
            high, low = parts_of(jnp.concatenate([ref[slot, 0], ref[slot, 1]], axis=1))
            squares = squares + dot(high, high, 0)
            mixed = mixed + dot(high, low, 0)
        grams.append(squares + (mixed + mixed.T))
    rows = lax.broadcasted_iota(jnp.int32, (BLOCK, BLOCK), 0)
    columns = lax.broadcasted_iota(jnp.int32, (BLOCK, BLOCK), 1)
    for ref, gram in ((keep_ref, jnp.where(first, grams[0], grams[1])), (send_ref, jnp.where(first, grams[1], grams[0]))):
        low = gram[BLOCK:, BLOCK:]
        diagonal = jnp.sum(jnp.where(rows == columns, low, 0.0), axis=0, keepdims=True)
        ref[:BLOCK] = gram[:BLOCK, BLOCK:]
        ref[BLOCK:PAIR] = jnp.where(rows <= columns, gram[:BLOCK, :BLOCK], low)
        ref[PAIR:] = jnp.broadcast_to(diagonal, (8, BLOCK))


def unpacked(packed):
    rows = lax.broadcasted_iota(jnp.int32, (BLOCK, BLOCK), 0)
    columns = lax.broadcasted_iota(jnp.int32, (BLOCK, BLOCK), 1)
    triangles = packed[BLOCK:PAIR]
    turned = triangles.T
    up = jnp.where(rows <= columns, triangles, turned)
    low = jnp.where(rows > columns, triangles, jnp.where(rows < columns, turned, packed[PAIR : PAIR + 1]))
    return up, packed[:BLOCK], low


def first_grams(info, main):
    out = shape(PAIR + 8, BLOCK)
    return call_whole(
        gram_kernel, (info, *main), [out, out], flops=2 * 2 * 4 * main[0].size * PAIR, nbytes=16 * main[0].size
    )


def sum_kernel(info_ref, *refs):
    refs[-1][...] = (refs[0][...] + refs[1][...]) + (refs[2][...] + refs[3][...])


def sum_parts(info, parts, before):
    return call_whole(sum_kernel, (info, *parts), [shape(*parts[0].shape)], before, nbytes=20 * parts[0].size)[0]


def rotation_of(gram, x_ref, r_ref):
    rows = lax.broadcasted_iota(jnp.int32, (PAIR, PAIR), 0)
    columns = lax.broadcasted_iota(jnp.int32, (PAIR, PAIR), 1)
    eye = (rows == columns).astype(F32)
    on_diagonal = gram * eye
    across = jnp.sum(on_diagonal, axis=0, keepdims=True)
    down = jnp.sum(on_diagonal, axis=1, keepdims=True)
    spread = across - down
    totals = across + down
    skew = gram * spread / (2.0 * spread * spread + 0.5 * totals * totals)
    square = mm3(skew, skew)
    bound = jnp.max(jnp.sum(jnp.abs(square), axis=0))
    scale = 2.0 / (2.0 + bound)
    x_ref[...] = scale * (eye + skew)
    r_ref[...] = (1.0 - scale) * eye + scale * square

    def step(size):
        left = r_ref[...]
        x = x_ref[...]
        x_ref[...] = x + mm3(x, left)
        r_ref[...] = mm3(left, left)
        return size * size

    lax.while_loop(lambda size: size > 3e-4, step, bound / (2.0 + bound))
    x = x_ref[...]
    x = x + mm3(x, eye - x + mm3(skew, x))
    return 2.0 * x - eye


def cayley_kernel(fill, info_ref, *refs):
    weights_ref, gram_ref, x_ref, r_ref = refs[-4:]
    up, cross, low = fill(info_ref, *refs[:-4])
    gram_ref[:BLOCK, :BLOCK] = up
    gram_ref[:BLOCK, BLOCK:] = cross
    gram_ref[BLOCK:, :BLOCK] = cross.T
    gram_ref[BLOCK:, BLOCK:] = low
    weights = rotation_of(gram_ref[...], x_ref, r_ref)
    weights_ref[:PAIR] = weights
    if weights_ref.shape[0] > PAIR:
        turned = mm3(weights[:, BLOCK:], mm3(gram_ref[...], weights[:, BLOCK:]), 0)
        weights_ref[PAIR:, :BLOCK] = turned[: BLOCK // 2]
        weights_ref[PAIR:, BLOCK:] = turned[BLOCK // 2 :]


def cayley_call(fill, args, before=(), last=False):
    return call_whole(
        functools.partial(cayley_kernel, fill),
        args,
        [shape(PAIR if last else PAIR + BLOCK // 2, PAIR), shape(PAIR, PAIR)],
        before,
        scratch=[pltpu.VMEM((PAIR, PAIR), F32)] * 2,
        flops=2 * 3 * 8 * PAIR**3,
        nbytes=16 * PAIR * PAIR,
    )


def total_of(part_refs):
    first, second, third, fourth = (ref[...] for ref in part_refs)
    return (first + second) + (third + fourth)


def first_cayley(info, parts, before):
    return cayley_call(lambda _, *part_refs: unpacked(total_of(part_refs)), (info, *parts), before)


def cayley(info, up, even, other, parts, before, last):
    def fill(info_ref, up_ref, even_ref, other_ref, *part_refs):
        folded = jnp.where(info_ref[0] == 0, even_ref[PAIR:], other_ref[PAIR:])
        low = jnp.concatenate([folded[:, :BLOCK], folded[:, BLOCK:]], axis=0)
        return up_ref[...], total_of(part_refs), low

    return cayley_call(fill, (info, up, even, other, *parts), before, last)


def project_kernel(info_ref, gram_ref, weights_ref, up_ref):
    weights = weights_ref[:PAIR, :BLOCK]
    up_ref[...] = mm3(weights, mm3(gram_ref[...], weights), 0)


def project(info, gram, weights):
    out = [shape(BLOCK, BLOCK)]
    return call_whole(project_kernel, (info, gram, weights), out, flops=2 * 3 * PAIR**3, nbytes=12 * PAIR * PAIR)[0]


def start_pair(info_ref, step, group, slot, up, low):
    share = step - up.shape[0]
    column = slot * PAIR - info_ref[2] - share * group
    rows = lax.broadcasted_iota(jnp.int32, (share, PAIR), 0)
    columns = lax.broadcasted_iota(jnp.int32, (share, PAIR), 1)
    basis = (rows == columns + column).astype(F32)
    return jnp.concatenate([jnp.concatenate([up, low], axis=1), basis], axis=0)


def groups_of(info_ref, step, refs, slots):
    if refs[0].shape[0] == SIDE:
        for group in range(SIDE):
            pairs = [(refs[2 * j][group], refs[2 * j + 1][group]) for j in range(len(slots))]
            yield group, [jnp.concatenate(pair, axis=1) for pair in pairs]
    else:
        for k, ref in enumerate(refs):
            group = lax.rem(info_ref[1] + SIDE - k, SIDE)
            yield group, [start_pair(info_ref, step, group, slot, ref[j, 0], ref[j, 1]) for j, slot in enumerate(slots)]


def own_kernel(rows, step, info_ref, own_ref, other_ref, *refs):
    up0_ref, up1_ref, low1_ref, cross_ref = refs[-4:]
    first = info_ref[0] == 0
    weights0 = jnp.where(first, own_ref[:PAIR], other_ref[:PAIR])
    weights1 = jnp.where(first, other_ref[:PAIR, :BLOCK], own_ref[:PAIR, :BLOCK])
    slot = 2 * info_ref[1]
    cross = jnp.zeros((BLOCK, BLOCK), F32)
    for group, (pair0, pair1) in groups_of(info_ref, step, refs[:-4], (slot, slot + 1)):
        turned = mm3(pair0, weights0)
        up1 = mm3(pair1, weights1)
        up0_ref[group] = turned[:, :BLOCK]
        low1_ref[group] = turned[:, BLOCK:]
        up1_ref[group] = up1
        cross = cross + mm3(up1[:rows], turned[:rows, BLOCK:], 0)
    cross_ref[...] = cross


def rotate_own(info, own, other, blocks, before, rows, step):
    return call_whole(
        functools.partial(own_kernel, rows, step),
        (info, own, other, *blocks),
        [shape(SIDE, step, BLOCK)] * 3 + [shape(BLOCK, BLOCK)],
        before,
        flops=2 * 3 * SIDE * step * 4 * BLOCK * PAIR,
        nbytes=4 * 7 * SIDE * step * BLOCK,
    )


def ahead_kernel(rows, step, info_ref, even_ref, odd_ref, cross_ref, up0_ref, *refs):
    low0_ref, keep_ref, send_ref = refs[-3:]
    weights = even_ref[:PAIR, BLOCK:] + odd_ref[:, BLOCK:]
    slot = (2 * info_ref[1] + COLS - 1) % COLS
    total = jnp.zeros((BLOCK, BLOCK), F32)
    for group, (pair,) in groups_of(info_ref, step, refs[:-3], (slot,)):
        low0 = mm3(pair, weights)
        low0_ref[group] = low0
        total = total + mm3(up0_ref[group, :rows], low0[:rows], 0)
    first = info_ref[0] == 0
    keep_ref[...] = jnp.where(first, total, cross_ref[...])
    send_ref[...] = jnp.where(first, cross_ref[...], total)


def rotate_ahead(info, ahead, cross, up0, blocks, rows, step):
    return call_whole(
        functools.partial(ahead_kernel, rows, step),
        (info, *ahead, cross, up0, *blocks),
        [shape(SIDE, step, BLOCK), shape(BLOCK, BLOCK), shape(BLOCK, BLOCK)],
        flops=2 * 3 * SIDE * step * 2 * BLOCK * PAIR,
        nbytes=4 * 4 * SIDE * step * BLOCK,
    )


def up_kernel(step, info_ref, even_ref, odd_ref, *refs):
    up_ref = refs[-1]
    weights = even_ref[:PAIR, :BLOCK] + odd_ref[:, :BLOCK]
    slot = (2 * info_ref[1] + COLS - 1) % COLS
    for group, (pair,) in groups_of(info_ref, step, refs[:-1], (slot,)):
        up_ref[group] = mm3(pair, weights)


def rotate_up(info, ahead, blocks, step):
    return call_whole(
        functools.partial(up_kernel, step),
        (info, *ahead, *blocks),
        [shape(SIDE, step, BLOCK)],
        flops=2 * 3 * SIDE * step * BLOCK * PAIR,
        nbytes=4 * 3 * SIDE * step * BLOCK,
    )[0]


def other_slot_kernel(info_ref, up0_ref, low0_ref, up1_ref, low1_ref, up_ref, low_ref):
    first = info_ref[0] == 0
    up_ref[...] = jnp.where(first, up1_ref[...], up0_ref[...])
    low_ref[...] = jnp.where(first, low1_ref[...], low0_ref[...])


def other_slot(info, blocks, before):
    return call_whole(other_slot_kernel, (info, *blocks), [shape(*blocks[0].shape)] * 2, before, nbytes=24 * blocks[0].size)


def final_kernel(rows, total, info_ref, weights_ref, gram_ref, up0_ref, low0_ref, up1_ref, low1_ref, ru_ref, rl_ref,
                 out_ref, frame_ref, scale_ref):
    weights = weights_ref[...]
    first = info_ref[0] == 0
    i = pl.program_id(0)
    up = jnp.where(first, up0_ref[i], up1_ref[i])
    low = jnp.where(first, low0_ref[i], low1_ref[i])
    mine = mm3(jnp.concatenate([up, low], axis=1), weights)
    theirs = mm3(jnp.concatenate([ru_ref[i], rl_ref[i]], axis=1), weights)
    for k, turned in enumerate((jnp.where(first, mine, theirs), jnp.where(first, theirs, mine))):
        out_ref[k] = turned[:rows]
        frame_ref[k] = turned[rows:]

    @pl.when(i == 0)
    def _():
        squares = jnp.sum(weights * mm3(gram_ref[...], weights), axis=0, keepdims=True)
        scale_ref[...] = jnp.sqrt(squares / total)


def rotate_final(info, weights, gram, blocks, rows, step):
    share = step - rows
    return call(
        functools.partial(final_kernel, rows, float(rows * COLS * ROWS)),
        (SIDE,),
        [pl.BlockSpec(memory_space=pltpu.VMEM)] * 8,
        [
            pl.BlockSpec((2, rows, PAIR), lambda i, c: (i, 0, 0)),
            pl.BlockSpec((2, share, PAIR), lambda i, c: (0, i, 0)),
            whole(1, PAIR),
        ],
        [shape(COLS, rows, PAIR), shape(2, SIDE * share, PAIR), shape(1, PAIR)],
        scalars=1,
        flops=2 * 3 * 2 * SIDE * step * PAIR * PAIR,
        nbytes=4 * 4 * SIDE * step * PAIR,
    )(info, weights, gram, *blocks)


def swap_core(value):
    return lax.ppermute(value, "cols", TURN_CORE)


def along(value, shifts):
    return [lax.ppermute(value, "rows", pairs) for pairs in shifts]


def same_kernel(info_ref, value_ref, out_ref):
    out_ref[...] = value_ref[: out_ref.shape[0]]


def odd_slot_before(info, weights, before):
    even = lax.ppermute(weights, "cols", ODD_TO_EVEN)
    copy = call_whole(same_kernel, (info, even), [shape(PAIR, PAIR)], before, nbytes=8 * PAIR * PAIR)[0]
    return [even, lax.ppermute(copy, "cols", EVEN_TO_ODD)]


def body(sensitivity):
    x = sensitivity[0]
    rows = x.shape[0]
    column = lax.axis_index("cols")
    parity = column % 2
    basis_rows = x.shape[1] // ROWS // 2
    basis_at = (lax.axis_index("rows") * 2 + parity) * basis_rows
    info = jnp.stack([parity, column // 2, basis_at]).astype(jnp.int32)
    step = rows + basis_rows // SIDE

    packed = pack_main(info, x)
    main = [packed[0]] + [lax.ppermute(packed[k], "cols", CHIPS_ON[k]) for k in range(1, SIDE)]

    keep, send = first_grams(info, main)
    packed = pack_ahead(info, x, main[1:])
    ahead = [packed[0]] + [lax.ppermute(packed[k], "cols", CHIPS_ON[k]) for k in range(1, SIDE)]
    value = keep + swap_core(send)
    value = sum_parts(info, [value] + along(value, ALONG_X), [ahead[1], ahead[3]])
    weights, gram = first_cayley(info, [value] + along(value, ALONG_Z), [ahead[2]])

    own_blocks = main
    ahead_blocks = [value[None] for value in ahead]
    for sweep_round in range(ROUNDS - 1):
        last = sweep_round == ROUNDS - 2
        other = swap_core(weights)
        up = project(info, gram, weights)
        before = [up] + ([ahead_blocks[0]] if sweep_round else [])
        up0, up1, low1, cross = rotate_own(info, weights, other, own_blocks, before, rows, step)
        weights_m = odd_slot_before(info, weights, [cross])
        low0, keep, send = rotate_ahead(info, weights_m, cross, up0, ahead_blocks, rows, step)
        value = keep + swap_core(send)
        value = value + sum(along(value, ALONG_X))
        own_blocks = [up0, low0, up1, low1]
        if last:
            other_blocks = [swap_core(block) for block in other_slot(info, own_blocks, [value])]
        else:
            up_m = rotate_up(info, weights_m, ahead_blocks, step)
            ahead_blocks = [up_m, lax.ppermute(low1, "cols", CHIPS_ON[1])]
        before = [] if last else [ahead_blocks[1]]
        weights, gram = cayley(info, up, weights_m[0], other, [value] + along(value, ALONG_Z), before, last)

    rotated, frame, column_scale = rotate_final(info, weights, gram, own_blocks + other_blocks, rows, step)
    return rotated, frame.reshape(2 * basis_rows, PAIR), column_scale.reshape(PAIR)


def solution(mesh):
    in_specs = (P("cols", "rows", None),)
    out_specs = (P(None, "rows", "cols"), P("rows", "cols"), P("cols"))
    return jax.shard_map(body, mesh=mesh, in_specs=in_specs, out_specs=out_specs, check_vma=False)
```

```python
import functools

import jax
import jax.numpy as jnp
from jax import lax
from jax.experimental import pallas as pl
from jax.experimental.pallas import tpu as pltpu
from jax.sharding import PartitionSpec as P

ROUNDS = 4
BLOCK = 128
PAIR = 256
SIDE = 4
ROWS = 16
COLS = 8
F32 = jnp.float32
BF16 = jnp.bfloat16
VMEM_LIMIT = 16 * 1024 * 1024

TURN_CORE = [(c, c ^ 1) for c in range(COLS)]
NEXT_SLOT = [(c, (c + 1) % COLS) for c in range(COLS)]
CHIPS_ON = [[(c, (c + 2 * k) % COLS) for c in range(COLS)] for k in range(SIDE)]
ODD_TO_EVEN = [(c, (c + 1) % COLS) for c in range(1, COLS, 2)]
ODD_TO_ODD = [(c, (c + 2) % COLS) for c in range(1, COLS, 2)]
EVEN_TO_ODD = [(c, c + 1) for c in range(0, COLS, 2)]
ALONG_X = [[(r, r - r % SIDE + (r + k) % SIDE) for r in range(ROWS)] for k in range(1, SIDE)]
ALONG_Z = [[(r, (r + SIDE * k) % ROWS) for r in range(ROWS)] for k in range(1, SIDE)]


def mm(left, right):
    return jnp.dot(left, right, precision=lax.Precision.HIGHEST, preferred_element_type=F32)


def mm_t(left, right):
    return lax.dot_general(
        left, right, (((0,), (0,)), ((), ())), precision=lax.Precision.HIGHEST, preferred_element_type=F32
    )


def parts_of(value):
    high = value.astype(BF16)
    return high, (value - high.astype(F32)).astype(BF16)


def dot(left, right, axis):
    return lax.dot_general(left, right, (((axis,), (0,)), ((), ())), preferred_element_type=F32)


def mm3(left, right, axis=1):
    high, low = parts_of(left)
    right_high, right_low = parts_of(right)
    width = right.shape[1]
    if width < PAIR:
        both = dot(high, jnp.concatenate([right_high, right_low], axis=1), axis)
        return both[:, :width] + (both[:, width:] + dot(low, right_high, axis))
    return dot(high, right_high, axis) + (dot(high, right_low, axis) + dot(low, right_high, axis))


def call(kernel, grid, in_specs, out_specs, out_shape, scalars=0, scratch=(), flops=0, nbytes=0):
    return pl.pallas_call(
        kernel,
        grid_spec=pltpu.PrefetchScalarGridSpec(
            num_scalar_prefetch=scalars,
            grid=grid,
            in_specs=in_specs,
            out_specs=out_specs,
            scratch_shapes=list(scratch),
        ),
        out_shape=out_shape,
        compiler_params=pltpu.CompilerParams(vmem_limit_bytes=VMEM_LIMIT),
        cost_estimate=pl.CostEstimate(flops=flops, bytes_accessed=nbytes, transcendentals=0),
    )


def call_whole(kernel, args, out_shape, before=(), scratch=(), flops=0, nbytes=0):
    inner = kernel
    if before:
        inner = lambda *refs: kernel(*refs[: len(args)], *refs[len(args) + len(before):])
    return pl.pallas_call(
        inner,
        in_specs=[pl.BlockSpec(memory_space=pltpu.SMEM)]
        + [pl.BlockSpec(memory_space=pltpu.VMEM)] * (len(args) - 1)
        + [pl.BlockSpec(memory_space=pl.ANY)] * len(before),
        out_specs=[pl.BlockSpec(memory_space=pltpu.VMEM)] * len(out_shape),
        out_shape=out_shape,
        scratch_shapes=list(scratch),
        compiler_params=pltpu.CompilerParams(vmem_limit_bytes=VMEM_LIMIT),
        cost_estimate=pl.CostEstimate(flops=flops, bytes_accessed=nbytes, transcendentals=0),
    )(*args, *before)


def shape(*dims):
    return jax.ShapeDtypeStruct(dims, F32)


def whole(*dims):
    return pl.BlockSpec(dims, lambda *_: (0,) * len(dims))


def pack_main_kernel(info_ref, *refs):
    for x_ref, out_ref in zip(refs[:SIDE], refs[SIDE:]):
        out_ref[0, 0] = x_ref[:, :BLOCK]
        out_ref[0, 1] = x_ref[:, BLOCK:]


def pack_main(info, x):
    rows = x.shape[0]

    def columns(k):
        return pl.BlockSpec((rows, PAIR), lambda j, c: (0, 2 * ((c[1] + k) % SIDE) + j))

    return call(
        pack_main_kernel,
        (2,),
        [columns(k) for k in range(SIDE)],
        [pl.BlockSpec((1, 2, rows, BLOCK), lambda j, c: (j, 0, 0, 0))] * SIDE,
        [shape(2, 2, rows, BLOCK)] * SIDE,
        scalars=1,
        nbytes=8 * SIDE * rows * 2 * PAIR,
    )(info, *[x] * SIDE)


def pack_ahead_kernel(info_ref, *refs):
    for x_ref, out_ref in zip(refs[:SIDE], refs[-SIDE:]):
        out_ref[0] = x_ref[:, :BLOCK]
        out_ref[1] = x_ref[:, BLOCK:]


def pack_ahead(info, x, before):
    rows = x.shape[0]

    def columns(k):
        return pl.BlockSpec((rows, PAIR), lambda i, c: (0, (2 * ((c[1] + k) % SIDE) + COLS - 1) % COLS))

    return call(
        pack_ahead_kernel,
        (1,),
        [columns(k) for k in range(SIDE)] + [pl.BlockSpec(memory_space=pl.ANY)] * len(before),
        [whole(2, rows, BLOCK)] * SIDE,
        [shape(2, rows, BLOCK)] * SIDE,
        scalars=1,
        nbytes=8 * SIDE * rows * PAIR,
    )(info, *[x] * SIDE, *before)


def gram_kernel(info_ref, *refs):
    keep_ref, send_ref = refs[-2:]
    first = info_ref[0] == 0
    grams = []
    for slot in range(2):
        squares = jnp.zeros((PAIR, PAIR), F32)
        mixed = jnp.zeros((PAIR, PAIR), F32)
        for ref in refs[:-2]:
            high, low = parts_of(jnp.concatenate([ref[slot, 0], ref[slot, 1]], axis=1))
            squares = squares + dot(high, high, 0)
            mixed = mixed + dot(high, low, 0)
        grams.append(squares + (mixed + mixed.T))
    rows = lax.broadcasted_iota(jnp.int32, (BLOCK, BLOCK), 0)
    columns = lax.broadcasted_iota(jnp.int32, (BLOCK, BLOCK), 1)
    for ref, gram in ((keep_ref, jnp.where(first, grams[0], grams[1])), (send_ref, jnp.where(first, grams[1], grams[0]))):
        low = gram[BLOCK:, BLOCK:]
        diagonal = jnp.sum(jnp.where(rows == columns, low, 0.0), axis=0, keepdims=True)
        ref[:BLOCK] = gram[:BLOCK, BLOCK:]
        ref[BLOCK:PAIR] = jnp.where(rows <= columns, gram[:BLOCK, :BLOCK], low)
        ref[PAIR:] = jnp.broadcast_to(diagonal, (8, BLOCK))


def unpacked(packed):
    rows = lax.broadcasted_iota(jnp.int32, (BLOCK, BLOCK), 0)
    columns = lax.broadcasted_iota(jnp.int32, (BLOCK, BLOCK), 1)
    triangles = packed[BLOCK:PAIR]
    turned = triangles.T
    up = jnp.where(rows <= columns, triangles, turned)
    low = jnp.where(rows > columns, triangles, jnp.where(rows < columns, turned, packed[PAIR : PAIR + 1]))
    return up, packed[:BLOCK], low


def first_grams(info, main):
    out = shape(PAIR + 8, BLOCK)
    return call_whole(
        gram_kernel, (info, *main), [out, out], flops=2 * 2 * 4 * main[0].size * PAIR, nbytes=16 * main[0].size
    )


def sum_kernel(info_ref, *refs):
    refs[-1][...] = (refs[0][...] + refs[1][...]) + (refs[2][...] + refs[3][...])


def sum_parts(info, parts, before):
    return call_whole(sum_kernel, (info, *parts), [shape(*parts[0].shape)], before, nbytes=20 * parts[0].size)[0]


def rotation_of(gram, x_ref, r_ref):
    rows = lax.broadcasted_iota(jnp.int32, (PAIR, PAIR), 0)
    columns = lax.broadcasted_iota(jnp.int32, (PAIR, PAIR), 1)
    eye = (rows == columns).astype(F32)
    on_diagonal = gram * eye
    across = jnp.sum(on_diagonal, axis=0, keepdims=True)
    down = jnp.sum(on_diagonal, axis=1, keepdims=True)
    spread = across - down
    totals = across + down
    skew = gram * spread / (2.0 * spread * spread + 0.5 * totals * totals)
    square = mm3(skew, skew)
    bound = jnp.max(jnp.sum(jnp.abs(square), axis=0))
    scale = 2.0 / (2.0 + bound)
    x_ref[...] = scale * (eye + skew)
    r_ref[...] = (1.0 - scale) * eye + scale * square

    def step(size):
        left = r_ref[...]
        x = x_ref[...]
        x_ref[...] = x + mm3(x, left)
        r_ref[...] = mm3(left, left)
        return size * size

    lax.while_loop(lambda size: size > 3e-4, step, bound / (2.0 + bound))
    x = x_ref[...]
    x = x + mm3(x, eye - x + mm3(skew, x))
    return 2.0 * x - eye


def cayley_kernel(fill, info_ref, *refs):
    weights_ref, lower_ref, gram_ref, x_ref, r_ref = refs[-5:]
    up, cross, low = fill(info_ref, *refs[:-5])
    gram_ref[:BLOCK, :BLOCK] = up
    gram_ref[:BLOCK, BLOCK:] = cross
    gram_ref[BLOCK:, :BLOCK] = cross.T
    gram_ref[BLOCK:, BLOCK:] = low
    weights = rotation_of(gram_ref[...], x_ref, r_ref)
    weights_ref[:PAIR] = weights
    lower_ref[...] = weights[:, BLOCK:]
    if weights_ref.shape[0] > PAIR:
        turned = mm3(weights[:, BLOCK:], mm3(gram_ref[...], weights[:, BLOCK:]), 0)
        weights_ref[PAIR:, :BLOCK] = turned[: BLOCK // 2]
        weights_ref[PAIR:, BLOCK:] = turned[BLOCK // 2 :]


def cayley_call(fill, args, before=(), last=False):
    return call_whole(
        functools.partial(cayley_kernel, fill),
        args,
        [shape(PAIR if last else PAIR + BLOCK // 2, PAIR), shape(PAIR, BLOCK), shape(PAIR, PAIR)],
        before,
        scratch=[pltpu.VMEM((PAIR, PAIR), F32)] * 2,
        flops=2 * 3 * 8 * PAIR**3,
        nbytes=16 * PAIR * PAIR,
    )


def total_of(part_refs):
    first, second, third, fourth = (ref[...] for ref in part_refs)
    return (first + second) + (third + fourth)


def first_cayley(info, parts, before):
    return cayley_call(lambda _, *part_refs: unpacked(total_of(part_refs)), (info, *parts), before)


def cayley(info, up, even, other, parts, before, last):
    def fill(info_ref, up_ref, even_ref, other_ref, *part_refs):
        folded = jnp.where(info_ref[0] == 0, even_ref[PAIR:], other_ref[PAIR:])
        low = jnp.concatenate([folded[:, :BLOCK], folded[:, BLOCK:]], axis=0)
        return up_ref[...], total_of(part_refs), low

    return cayley_call(fill, (info, up, even, other, *parts), before, last)


def project_kernel(info_ref, gram_ref, weights_ref, up_ref):
    weights = weights_ref[:PAIR, :BLOCK]
    up_ref[...] = mm3(weights, mm3(gram_ref[...], weights), 0)


def project(info, gram, weights):
    out = [shape(BLOCK, BLOCK)]
    return call_whole(project_kernel, (info, gram, weights), out, flops=2 * 3 * PAIR**3, nbytes=12 * PAIR * PAIR)[0]


def start_pair(info_ref, step, group, slot, up, low):
    share = step - up.shape[0]
    column = slot * PAIR - info_ref[2] - share * group
    rows = lax.broadcasted_iota(jnp.int32, (share, PAIR), 0)
    columns = lax.broadcasted_iota(jnp.int32, (share, PAIR), 1)
    basis = (rows == columns + column).astype(F32)
    return jnp.concatenate([jnp.concatenate([up, low], axis=1), basis], axis=0)


def groups_of(info_ref, step, refs, slots):
    if refs[0].shape[0] == SIDE:
        for group in range(SIDE):
            pairs = [(refs[2 * j][group], refs[2 * j + 1][group]) for j in range(len(slots))]
            yield group, [jnp.concatenate(pair, axis=1) for pair in pairs]
    else:
        for k, ref in enumerate(refs):
            group = lax.rem(info_ref[1] + SIDE - k, SIDE)
            yield group, [start_pair(info_ref, step, group, slot, ref[j, 0], ref[j, 1]) for j, slot in enumerate(slots)]


def own_kernel(rows, step, info_ref, own_ref, other_ref, *refs):
    up0_ref, up1_ref, low1_ref, cross_ref = refs[-4:]
    first = info_ref[0] == 0
    weights0 = jnp.where(first, own_ref[:PAIR], other_ref[:PAIR])
    weights1 = jnp.where(first, other_ref[:PAIR, :BLOCK], own_ref[:PAIR, :BLOCK])
    slot = 2 * info_ref[1]
    cross = jnp.zeros((BLOCK, BLOCK), F32)
    for group, (pair0, pair1) in groups_of(info_ref, step, refs[:-4], (slot, slot + 1)):
        turned = mm3(pair0, weights0)
        up1 = mm3(pair1, weights1)
        up0_ref[group] = turned[:, :BLOCK]
        low1_ref[group] = turned[:, BLOCK:]
        up1_ref[group] = up1
        cross = cross + mm3(up1[:rows], turned[:rows, BLOCK:], 0)
    cross_ref[...] = cross


def rotate_own(info, own, other, blocks, before, rows, step):
    return call_whole(
        functools.partial(own_kernel, rows, step),
        (info, own, other, *blocks),
        [shape(SIDE, step, BLOCK)] * 3 + [shape(BLOCK, BLOCK)],
        before,
        flops=2 * 3 * SIDE * step * 4 * BLOCK * PAIR,
        nbytes=4 * 7 * SIDE * step * BLOCK,
    )


def ahead_kernel(rows, step, info_ref, lower_ref, cross_ref, up0_ref, *refs):
    low0_ref, keep_ref, send_ref = refs[-3:]
    weights = lower_ref[...]
    slot = (2 * info_ref[1] + COLS - 1) % COLS
    total = jnp.zeros((BLOCK, BLOCK), F32)
    for group, (pair,) in groups_of(info_ref, step, refs[:-3], (slot,)):
        low0 = mm3(pair, weights)
        low0_ref[group] = low0
        total = total + mm3(up0_ref[group, :rows], low0[:rows], 0)
    first = info_ref[0] == 0
    keep_ref[...] = jnp.where(first, total, cross_ref[...])
    send_ref[...] = jnp.where(first, cross_ref[...], total)


def rotate_ahead(info, lower, cross, up0, blocks, rows, step):
    return call_whole(
        functools.partial(ahead_kernel, rows, step),
        (info, lower, cross, up0, *blocks),
        [shape(SIDE, step, BLOCK), shape(BLOCK, BLOCK), shape(BLOCK, BLOCK)],
        flops=2 * 3 * SIDE * step * 2 * BLOCK * PAIR,
        nbytes=4 * 4 * SIDE * step * BLOCK,
    )


def up_kernel(step, info_ref, even_ref, odd_ref, *refs):
    up_ref = refs[-1]
    weights = even_ref[:PAIR, :BLOCK] + odd_ref[...]
    slot = (2 * info_ref[1] + COLS - 1) % COLS
    for group, (pair,) in groups_of(info_ref, step, refs[:-1], (slot,)):
        up_ref[group] = mm3(pair, weights)


def rotate_up(info, ahead, blocks, step):
    return call_whole(
        functools.partial(up_kernel, step),
        (info, *ahead, *blocks),
        [shape(SIDE, step, BLOCK)],
        flops=2 * 3 * SIDE * step * BLOCK * PAIR,
        nbytes=4 * 3 * SIDE * step * BLOCK,
    )[0]


def other_slot_kernel(info_ref, up0_ref, low0_ref, up1_ref, low1_ref, up_ref, low_ref):
    first = info_ref[0] == 0
    up_ref[...] = jnp.where(first, up1_ref[...], up0_ref[...])
    low_ref[...] = jnp.where(first, low1_ref[...], low0_ref[...])


def other_slot(info, blocks, before):
    return call_whole(other_slot_kernel, (info, *blocks), [shape(*blocks[0].shape)] * 2, before, nbytes=24 * blocks[0].size)


def final_kernel(rows, total, info_ref, weights_ref, gram_ref, up0_ref, low0_ref, up1_ref, low1_ref, ru_ref, rl_ref,
                 out_ref, frame_ref, scale_ref):
    weights = weights_ref[...]
    first = info_ref[0] == 0
    i = pl.program_id(0)
    up = jnp.where(first, up0_ref[i], up1_ref[i])
    low = jnp.where(first, low0_ref[i], low1_ref[i])
    mine = mm3(jnp.concatenate([up, low], axis=1), weights)
    theirs = mm3(jnp.concatenate([ru_ref[i], rl_ref[i]], axis=1), weights)
    for k, turned in enumerate((jnp.where(first, mine, theirs), jnp.where(first, theirs, mine))):
        out_ref[k] = turned[:rows]
        frame_ref[k] = turned[rows:]

    @pl.when(i == 0)
    def _():
        squares = jnp.sum(weights * mm3(gram_ref[...], weights), axis=0, keepdims=True)
        scale_ref[...] = jnp.sqrt(squares / total)


def rotate_final(info, weights, gram, blocks, rows, step):
    share = step - rows
    return call(
        functools.partial(final_kernel, rows, float(rows * COLS * ROWS)),
        (SIDE,),
        [pl.BlockSpec(memory_space=pltpu.VMEM)] * 8,
        [
            pl.BlockSpec((2, rows, PAIR), lambda i, c: (i, 0, 0)),
            pl.BlockSpec((2, share, PAIR), lambda i, c: (0, i, 0)),
            whole(1, PAIR),
        ],
        [shape(COLS, rows, PAIR), shape(2, SIDE * share, PAIR), shape(1, PAIR)],
        scalars=1,
        flops=2 * 3 * 2 * SIDE * step * PAIR * PAIR,
        nbytes=4 * 4 * SIDE * step * PAIR,
    )(info, weights, gram, *blocks)


def swap_core(value):
    return lax.ppermute(value, "cols", TURN_CORE)


def along(value, shifts):
    return [lax.ppermute(value, "rows", pairs) for pairs in shifts]


def lower_kernel(info_ref, even_ref, odd_ref, low1_ref, lower_ref, pass_ref):
    lower_ref[...] = even_ref[:PAIR, BLOCK:] + odd_ref[...]
    pass_ref[...] = low1_ref[...]


def lower_before(info, even, odd, low1):
    out = [shape(PAIR, BLOCK), shape(*low1.shape)]
    return call_whole(lower_kernel, (info, even, odd, low1), out, nbytes=8 * (low1.size + PAIR * BLOCK))


def upper_kernel(info_ref, value_ref, out_ref):
    out_ref[...] = value_ref[:PAIR, :BLOCK]


def relayed_upper(info, even, before):
    upper = call_whole(upper_kernel, (info, even), [shape(PAIR, BLOCK)], before, nbytes=8 * PAIR * BLOCK)[0]
    return lax.ppermute(upper, "cols", EVEN_TO_ODD)


def body(sensitivity):
    x = sensitivity[0]
    rows = x.shape[0]
    column = lax.axis_index("cols")
    parity = column % 2
    basis_rows = x.shape[1] // ROWS // 2
    basis_at = (lax.axis_index("rows") * 2 + parity) * basis_rows
    info = jnp.stack([parity, column // 2, basis_at]).astype(jnp.int32)
    step = rows + basis_rows // SIDE

    packed = pack_main(info, x)
    main = [packed[0]] + [lax.ppermute(packed[k], "cols", CHIPS_ON[k]) for k in range(1, SIDE)]

    keep, send = first_grams(info, main)
    packed = pack_ahead(info, x, main[1:])
    ahead = [packed[0]] + [lax.ppermute(packed[k], "cols", CHIPS_ON[k]) for k in range(1, SIDE)]
    value = keep + swap_core(send)
    value = sum_parts(info, [value] + along(value, ALONG_X), [])
    weights, lower, gram = first_cayley(info, [value] + along(value, ALONG_Z), ahead[1:])

    own_blocks = main
    ahead_blocks = [value[None] for value in ahead]
    for sweep_round in range(ROUNDS - 1):
        last = sweep_round == ROUNDS - 2
        odd = lax.ppermute(lower, "cols", ODD_TO_ODD)
        even = lax.ppermute(weights, "cols", ODD_TO_EVEN)
        other = swap_core(weights)
        up = project(info, gram, weights)
        before = [up] + ([ahead_blocks[0]] if sweep_round else [])
        up0, up1, low1, cross = rotate_own(info, weights, other, own_blocks, before, rows, step)
        lower, passed = lower_before(info, even, odd, low1)
        low0, keep, send = rotate_ahead(info, lower, cross, up0, ahead_blocks, rows, step)
        value = keep + swap_core(send)
        value = value + sum(along(value, ALONG_X))
        own_blocks = [up0, low0, up1, low1]
        if last:
            other_blocks = [swap_core(block) for block in other_slot(info, own_blocks, [value])]
        else:
            up_m = rotate_up(info, [even, relayed_upper(info, even, [keep])], ahead_blocks, step)
            ahead_blocks = [up_m, lax.ppermute(passed, "cols", CHIPS_ON[1])]
        before = [] if last else [ahead_blocks[1]]
        weights, lower, gram = cayley(info, up, even, other, [value] + along(value, ALONG_Z), before, last)

    rotated, frame, column_scale = rotate_final(info, weights, gram, own_blocks + other_blocks, rows, step)
    return rotated, frame.reshape(2 * basis_rows, PAIR), column_scale.reshape(PAIR)


def solution(mesh):
    in_specs = (P("cols", "rows", None),)
    out_specs = (P(None, "rows", "cols"), P("rows", "cols"), P("cols"))
    return jax.shard_map(body, mesh=mesh, in_specs=in_specs, out_specs=out_specs, check_vma=False)
```

```python
import functools

import jax
import jax.numpy as jnp
from jax import lax
from jax.experimental import pallas as pl
from jax.experimental.pallas import tpu as pltpu
from jax.sharding import PartitionSpec as P

ROUNDS = 4
BLOCK = 128
PAIR = 256
SIDE = 4
ROWS = 16
COLS = 8
F32 = jnp.float32
BF16 = jnp.bfloat16
VMEM_LIMIT = 16 * 1024 * 1024

TURN_CORE = [(c, c ^ 1) for c in range(COLS)]
NEXT_SLOT = [(c, (c + 1) % COLS) for c in range(COLS)]
CHIPS_ON = [[(c, (c + 2 * k) % COLS) for c in range(COLS)] for k in range(SIDE)]
ODD_TO_EVEN = [(c, (c + 1) % COLS) for c in range(1, COLS, 2)]
ODD_TO_ODD = [(c, (c + 2) % COLS) for c in range(1, COLS, 2)]
EVEN_TO_ODD = [(c, c + 1) for c in range(0, COLS, 2)]
ALONG_X = [[(r, r - r % SIDE + (r + k) % SIDE) for r in range(ROWS)] for k in range(1, SIDE)]
ALONG_Z = [[(r, (r + SIDE * k) % ROWS) for r in range(ROWS)] for k in range(1, SIDE)]


def mm(left, right):
    return jnp.dot(left, right, precision=lax.Precision.HIGHEST, preferred_element_type=F32)


def mm_t(left, right):
    return lax.dot_general(
        left, right, (((0,), (0,)), ((), ())), precision=lax.Precision.HIGHEST, preferred_element_type=F32
    )


def parts_of(value):
    high = value.astype(BF16)
    return high, (value - high.astype(F32)).astype(BF16)


def dot(left, right, axis):
    return lax.dot_general(left, right, (((axis,), (0,)), ((), ())), preferred_element_type=F32)


def mm3(left, right, axis=1):
    high, low = parts_of(left)
    right_high, right_low = parts_of(right)
    width = right.shape[1]
    if width < PAIR:
        both = dot(high, jnp.concatenate([right_high, right_low], axis=1), axis)
        return both[:, :width] + (both[:, width:] + dot(low, right_high, axis))
    return dot(high, right_high, axis) + (dot(high, right_low, axis) + dot(low, right_high, axis))


def call(kernel, grid, in_specs, out_specs, out_shape, scalars=0, scratch=(), flops=0, nbytes=0):
    return pl.pallas_call(
        kernel,
        grid_spec=pltpu.PrefetchScalarGridSpec(
            num_scalar_prefetch=scalars,
            grid=grid,
            in_specs=in_specs,
            out_specs=out_specs,
            scratch_shapes=list(scratch),
        ),
        out_shape=out_shape,
        compiler_params=pltpu.CompilerParams(vmem_limit_bytes=VMEM_LIMIT),
        cost_estimate=pl.CostEstimate(flops=flops, bytes_accessed=nbytes, transcendentals=0),
    )


def call_whole(kernel, args, out_shape, before=(), scratch=(), flops=0, nbytes=0):
    inner = kernel
    if before:
        inner = lambda *refs: kernel(*refs[: len(args)], *refs[len(args) + len(before):])
    return pl.pallas_call(
        inner,
        in_specs=[pl.BlockSpec(memory_space=pltpu.SMEM)]
        + [pl.BlockSpec(memory_space=pltpu.VMEM)] * (len(args) - 1)
        + [pl.BlockSpec(memory_space=pl.ANY)] * len(before),
        out_specs=[pl.BlockSpec(memory_space=pltpu.VMEM)] * len(out_shape),
        out_shape=out_shape,
        scratch_shapes=list(scratch),
        compiler_params=pltpu.CompilerParams(vmem_limit_bytes=VMEM_LIMIT),
        cost_estimate=pl.CostEstimate(flops=flops, bytes_accessed=nbytes, transcendentals=0),
    )(*args, *before)


def shape(*dims):
    return jax.ShapeDtypeStruct(dims, F32)


def whole(*dims):
    return pl.BlockSpec(dims, lambda *_: (0,) * len(dims))


def pack_main_kernel(info_ref, *refs):
    for x_ref, out_ref in zip(refs[:SIDE], refs[SIDE:]):
        out_ref[0, 0] = x_ref[:, :BLOCK]
        out_ref[0, 1] = x_ref[:, BLOCK:]


def pack_main(info, x):
    rows = x.shape[0]

    def columns(k):
        return pl.BlockSpec((rows, PAIR), lambda j, c: (0, 2 * ((c[1] + k) % SIDE) + j))

    return call(
        pack_main_kernel,
        (2,),
        [columns(k) for k in range(SIDE)],
        [pl.BlockSpec((1, 2, rows, BLOCK), lambda j, c: (j, 0, 0, 0))] * SIDE,
        [shape(2, 2, rows, BLOCK)] * SIDE,
        scalars=1,
        nbytes=8 * SIDE * rows * 2 * PAIR,
    )(info, *[x] * SIDE)


def pack_ahead_kernel(info_ref, *refs):
    for x_ref, out_ref in zip(refs[:SIDE], refs[-SIDE:]):
        out_ref[0] = x_ref[:, :BLOCK]
        out_ref[1] = x_ref[:, BLOCK:]


def pack_ahead(info, x, before):
    rows = x.shape[0]

    def columns(k):
        return pl.BlockSpec((rows, PAIR), lambda i, c: (0, (2 * ((c[1] + k) % SIDE) + COLS - 1) % COLS))

    return call(
        pack_ahead_kernel,
        (1,),
        [columns(k) for k in range(SIDE)] + [pl.BlockSpec(memory_space=pl.ANY)] * len(before),
        [whole(2, rows, BLOCK)] * SIDE,
        [shape(2, rows, BLOCK)] * SIDE,
        scalars=1,
        nbytes=8 * SIDE * rows * PAIR,
    )(info, *[x] * SIDE, *before)


def gram_kernel(info_ref, *refs):
    keep_ref, send_ref = refs[-2:]
    first = info_ref[0] == 0
    grams = []
    for slot in range(2):
        squares = jnp.zeros((PAIR, PAIR), F32)
        mixed = jnp.zeros((PAIR, PAIR), F32)
        for ref in refs[:-2]:
            high, low = parts_of(jnp.concatenate([ref[slot, 0], ref[slot, 1]], axis=1))
            squares = squares + dot(high, high, 0)
            mixed = mixed + dot(high, low, 0)
        grams.append(squares + (mixed + mixed.T))
    rows = lax.broadcasted_iota(jnp.int32, (BLOCK, BLOCK), 0)
    columns = lax.broadcasted_iota(jnp.int32, (BLOCK, BLOCK), 1)
    for ref, gram in ((keep_ref, jnp.where(first, grams[0], grams[1])), (send_ref, jnp.where(first, grams[1], grams[0]))):
        low = gram[BLOCK:, BLOCK:]
        diagonal = jnp.sum(jnp.where(rows == columns, low, 0.0), axis=0, keepdims=True)
        ref[:BLOCK] = gram[:BLOCK, BLOCK:]
        ref[BLOCK:PAIR] = jnp.where(rows <= columns, gram[:BLOCK, :BLOCK], low)
        ref[PAIR:] = jnp.broadcast_to(diagonal, (8, BLOCK))


def unpacked(packed):
    rows = lax.broadcasted_iota(jnp.int32, (BLOCK, BLOCK), 0)
    columns = lax.broadcasted_iota(jnp.int32, (BLOCK, BLOCK), 1)
    triangles = packed[BLOCK:PAIR]
    turned = triangles.T
    up = jnp.where(rows <= columns, triangles, turned)
    low = jnp.where(rows > columns, triangles, jnp.where(rows < columns, turned, packed[PAIR : PAIR + 1]))
    return up, packed[:BLOCK], low


def first_grams(info, main):
    out = shape(PAIR + 8, BLOCK)
    return call_whole(
        gram_kernel, (info, *main), [out, out], flops=2 * 2 * 4 * main[0].size * PAIR, nbytes=16 * main[0].size
    )


def sum_kernel(info_ref, *refs):
    refs[-1][...] = (refs[0][...] + refs[1][...]) + (refs[2][...] + refs[3][...])


def sum_parts(info, parts, before):
    return call_whole(sum_kernel, (info, *parts), [shape(*parts[0].shape)], before, nbytes=20 * parts[0].size)[0]


def rotation_of(gram, x_ref, r_ref):
    rows = lax.broadcasted_iota(jnp.int32, (PAIR, PAIR), 0)
    columns = lax.broadcasted_iota(jnp.int32, (PAIR, PAIR), 1)
    eye = (rows == columns).astype(F32)
    on_diagonal = gram * eye
    across = jnp.sum(on_diagonal, axis=0, keepdims=True)
    down = jnp.sum(on_diagonal, axis=1, keepdims=True)
    spread = across - down
    totals = across + down
    skew = gram * spread / (2.0 * spread * spread + 0.5 * totals * totals)
    square = mm3(skew, skew)
    bound = jnp.max(jnp.sum(jnp.abs(square), axis=0))
    scale = 2.0 / (2.0 + bound)
    x_ref[...] = scale * (eye + skew)
    r_ref[...] = (1.0 - scale) * eye + scale * square

    def step(size):
        left = r_ref[...]
        x = x_ref[...]
        x_ref[...] = x + mm3(x, left)
        r_ref[...] = mm3(left, left)
        return size * size

    lax.while_loop(lambda size: size > 3e-4, step, bound / (2.0 + bound))
    x = x_ref[...]
    x = x + mm3(x, eye - x + mm3(skew, x))
    return 2.0 * x - eye


def cayley_kernel(fill, info_ref, *refs):
    weights_ref, lower_ref, gram_ref, x_ref, r_ref = refs[-5:]
    up, cross, low = fill(info_ref, *refs[:-5])
    gram_ref[:BLOCK, :BLOCK] = up
    gram_ref[:BLOCK, BLOCK:] = cross
    gram_ref[BLOCK:, :BLOCK] = cross.T
    gram_ref[BLOCK:, BLOCK:] = low
    weights = rotation_of(gram_ref[...], x_ref, r_ref)
    weights_ref[:PAIR] = weights
    lower_ref[...] = weights[:, BLOCK:]
    if weights_ref.shape[0] > PAIR:
        turned = mm3(weights[:, BLOCK:], mm3(gram_ref[...], weights[:, BLOCK:]), 0)
        weights_ref[PAIR:, :BLOCK] = turned[: BLOCK // 2]
        weights_ref[PAIR:, BLOCK:] = turned[BLOCK // 2 :]


def cayley_call(fill, args, before=(), last=False):
    return call_whole(
        functools.partial(cayley_kernel, fill),
        args,
        [shape(PAIR if last else PAIR + BLOCK // 2, PAIR), shape(PAIR, BLOCK), shape(PAIR, PAIR)],
        before,
        scratch=[pltpu.VMEM((PAIR, PAIR), F32)] * 2,
        flops=2 * 3 * 8 * PAIR**3,
        nbytes=16 * PAIR * PAIR,
    )


def total_of(part_refs):
    first, second, third, fourth = (ref[...] for ref in part_refs)
    return (first + second) + (third + fourth)


def first_cayley(info, parts, before):
    return cayley_call(lambda _, *part_refs: unpacked(total_of(part_refs)), (info, *parts), before)


def cayley(info, up, even, other, parts, before, last):
    def fill(info_ref, up_ref, even_ref, other_ref, *part_refs):
        folded = jnp.where(info_ref[0] == 0, even_ref[PAIR:], other_ref[PAIR:])
        low = jnp.concatenate([folded[:, :BLOCK], folded[:, BLOCK:]], axis=0)
        return up_ref[...], total_of(part_refs), low

    return cayley_call(fill, (info, up, even, other, *parts), before, last)


def project_kernel(info_ref, gram_ref, weights_ref, up_ref):
    weights = weights_ref[:PAIR, :BLOCK]
    up_ref[...] = mm3(weights, mm3(gram_ref[...], weights), 0)


def project(info, gram, weights):
    out = [shape(BLOCK, BLOCK)]
    return call_whole(project_kernel, (info, gram, weights), out, flops=2 * 3 * PAIR**3, nbytes=12 * PAIR * PAIR)[0]


def start_pair(info_ref, step, group, slot, up, low):
    share = step - up.shape[0]
    column = slot * PAIR - info_ref[2] - share * group
    rows = lax.broadcasted_iota(jnp.int32, (share, PAIR), 0)
    columns = lax.broadcasted_iota(jnp.int32, (share, PAIR), 1)
    basis = (rows == columns + column).astype(F32)
    return jnp.concatenate([jnp.concatenate([up, low], axis=1), basis], axis=0)


def groups_of(info_ref, step, refs, slots):
    if refs[0].shape[0] == SIDE:
        for group in range(SIDE):
            pairs = [(refs[2 * j][group], refs[2 * j + 1][group]) for j in range(len(slots))]
            yield group, [jnp.concatenate(pair, axis=1) for pair in pairs]
    else:
        for k, ref in enumerate(refs):
            group = lax.rem(info_ref[1] + SIDE - k, SIDE)
            yield group, [start_pair(info_ref, step, group, slot, ref[j, 0], ref[j, 1]) for j, slot in enumerate(slots)]


def own_kernel(rows, step, info_ref, own_ref, other_ref, *refs):
    up0_ref, up1_ref, low1_ref, cross_ref = refs[-4:]
    first = info_ref[0] == 0
    weights0 = jnp.where(first, own_ref[:PAIR], other_ref[:PAIR])
    weights1 = jnp.where(first, other_ref[:PAIR, :BLOCK], own_ref[:PAIR, :BLOCK])
    slot = 2 * info_ref[1]
    cross = jnp.zeros((BLOCK, BLOCK), F32)
    for group, (pair0, pair1) in groups_of(info_ref, step, refs[:-4], (slot, slot + 1)):
        turned = mm3(pair0, weights0)
        up1 = mm3(pair1, weights1)
        up0_ref[group] = turned[:, :BLOCK]
        low1_ref[group] = turned[:, BLOCK:]
        up1_ref[group] = up1
        cross = cross + mm3(up1[:rows], turned[:rows, BLOCK:], 0)
    cross_ref[...] = cross


def rotate_own(info, own, other, blocks, rows, step):
    return call_whole(
        functools.partial(own_kernel, rows, step),
        (info, own, other, *blocks),
        [shape(SIDE, step, BLOCK)] * 3 + [shape(BLOCK, BLOCK)],
        flops=2 * 3 * SIDE * step * 4 * BLOCK * PAIR,
        nbytes=4 * 7 * SIDE * step * BLOCK,
    )


def ahead_kernel(rows, step, info_ref, lower_ref, cross_ref, up0_ref, *refs):
    low0_ref, keep_ref, send_ref = refs[-3:]
    weights = lower_ref[...]
    slot = (2 * info_ref[1] + COLS - 1) % COLS
    total = jnp.zeros((BLOCK, BLOCK), F32)
    for group, (pair,) in groups_of(info_ref, step, refs[:-3], (slot,)):
        low0 = mm3(pair, weights)
        low0_ref[group] = low0
        total = total + mm3(up0_ref[group, :rows], low0[:rows], 0)
    first = info_ref[0] == 0
    keep_ref[...] = jnp.where(first, total, cross_ref[...])
    send_ref[...] = jnp.where(first, cross_ref[...], total)


def rotate_ahead(info, lower, cross, up0, blocks, rows, step):
    return call_whole(
        functools.partial(ahead_kernel, rows, step),
        (info, lower, cross, up0, *blocks),
        [shape(SIDE, step, BLOCK), shape(BLOCK, BLOCK), shape(BLOCK, BLOCK)],
        flops=2 * 3 * SIDE * step * 2 * BLOCK * PAIR,
        nbytes=4 * 4 * SIDE * step * BLOCK,
    )


def up_kernel(step, info_ref, even_ref, odd_ref, *refs):
    up_ref = refs[-1]
    weights = even_ref[:PAIR, :BLOCK] + odd_ref[...]
    slot = (2 * info_ref[1] + COLS - 1) % COLS
    for group, (pair,) in groups_of(info_ref, step, refs[:-1], (slot,)):
        up_ref[group] = mm3(pair, weights)


def rotate_up(info, ahead, blocks, step):
    return call_whole(
        functools.partial(up_kernel, step),
        (info, *ahead, *blocks),
        [shape(SIDE, step, BLOCK)],
        flops=2 * 3 * SIDE * step * BLOCK * PAIR,
        nbytes=4 * 3 * SIDE * step * BLOCK,
    )[0]


def other_slot_kernel(info_ref, up0_ref, low0_ref, up1_ref, low1_ref, up_ref, low_ref):
    first = info_ref[0] == 0
    up_ref[...] = jnp.where(first, up1_ref[...], up0_ref[...])
    low_ref[...] = jnp.where(first, low1_ref[...], low0_ref[...])


def other_slot(info, blocks, before):
    return call_whole(other_slot_kernel, (info, *blocks), [shape(*blocks[0].shape)] * 2, before, nbytes=24 * blocks[0].size)


def final_kernel(rows, total, info_ref, weights_ref, gram_ref, up0_ref, low0_ref, up1_ref, low1_ref, ru_ref, rl_ref,
                 out_ref, frame_ref, scale_ref):
    weights = weights_ref[...]
    first = info_ref[0] == 0
    i = pl.program_id(0)
    up = jnp.where(first, up0_ref[i], up1_ref[i])
    low = jnp.where(first, low0_ref[i], low1_ref[i])
    mine = mm3(jnp.concatenate([up, low], axis=1), weights)
    theirs = mm3(jnp.concatenate([ru_ref[i], rl_ref[i]], axis=1), weights)
    for k, turned in enumerate((jnp.where(first, mine, theirs), jnp.where(first, theirs, mine))):
        out_ref[k] = turned[:rows]
        frame_ref[k] = turned[rows:]

    @pl.when(i == 0)
    def _():
        squares = jnp.sum(weights * mm3(gram_ref[...], weights), axis=0, keepdims=True)
        scale_ref[...] = jnp.sqrt(squares / total)


def rotate_final(info, weights, gram, blocks, rows, step):
    share = step - rows
    return call(
        functools.partial(final_kernel, rows, float(rows * COLS * ROWS)),
        (SIDE,),
        [pl.BlockSpec(memory_space=pltpu.VMEM)] * 8,
        [
            pl.BlockSpec((2, rows, PAIR), lambda i, c: (i, 0, 0)),
            pl.BlockSpec((2, share, PAIR), lambda i, c: (0, i, 0)),
            whole(1, PAIR),
        ],
        [shape(COLS, rows, PAIR), shape(2, SIDE * share, PAIR), shape(1, PAIR)],
        scalars=1,
        flops=2 * 3 * 2 * SIDE * step * PAIR * PAIR,
        nbytes=4 * 4 * SIDE * step * PAIR,
    )(info, weights, gram, *blocks)


def swap_core(value):
    return lax.ppermute(value, "cols", TURN_CORE)


def along(value, shifts):
    return [lax.ppermute(value, "rows", pairs) for pairs in shifts]


def lower_kernel(info_ref, even_ref, odd_ref, low1_ref, lower_ref, pass_ref):
    lower_ref[...] = even_ref[:PAIR, BLOCK:] + odd_ref[...]
    pass_ref[...] = low1_ref[...]


def lower_before(info, even, odd, low1):
    out = [shape(PAIR, BLOCK), shape(*low1.shape)]
    return call_whole(lower_kernel, (info, even, odd, low1), out, nbytes=8 * (low1.size + PAIR * BLOCK))


def upper_kernel(info_ref, value_ref, out_ref):
    out_ref[...] = value_ref[:PAIR, :BLOCK]


def relayed_upper(info, even, before):
    upper = call_whole(upper_kernel, (info, even), [shape(PAIR, BLOCK)], before, nbytes=8 * PAIR * BLOCK)[0]
    return lax.ppermute(upper, "cols", EVEN_TO_ODD)


def body(sensitivity):
    x = sensitivity[0]
    rows = x.shape[0]
    column = lax.axis_index("cols")
    parity = column % 2
    basis_rows = x.shape[1] // ROWS // 2
    basis_at = (lax.axis_index("rows") * 2 + parity) * basis_rows
    info = jnp.stack([parity, column // 2, basis_at]).astype(jnp.int32)
    step = rows + basis_rows // SIDE

    packed = pack_main(info, x)
    main = [packed[0]] + [lax.ppermute(packed[k], "cols", CHIPS_ON[k]) for k in range(1, SIDE)]

    keep, send = first_grams(info, main)
    packed = pack_ahead(info, x, main[1:])
    ahead = [packed[0]] + [lax.ppermute(packed[k], "cols", CHIPS_ON[k]) for k in range(1, SIDE)]
    value = keep + swap_core(send)
    value = sum_parts(info, [value] + along(value, ALONG_X), [])
    weights, lower, gram = first_cayley(info, [value] + along(value, ALONG_Z), ahead[1:])

    own_blocks = main
    ahead_blocks = [value[None] for value in ahead]
    for sweep_round in range(ROUNDS - 1):
        last = sweep_round == ROUNDS - 2
        odd = lax.ppermute(lower, "cols", ODD_TO_ODD)
        even = lax.ppermute(weights, "cols", ODD_TO_EVEN)
        other = swap_core(weights)
        up = project(info, gram, weights)
        up0, up1, low1, cross = rotate_own(info, weights, other, own_blocks, rows, step)
        lower, passed = lower_before(info, even, odd, low1)
        low0, keep, send = rotate_ahead(info, lower, cross, up0, ahead_blocks, rows, step)
        value = keep + swap_core(send)
        value = value + sum(along(value, ALONG_X))
        own_blocks = [up0, low0, up1, low1]
        if last:
            other_blocks = [swap_core(block) for block in other_slot(info, own_blocks, [value])]
        else:
            up_m = rotate_up(info, [even, relayed_upper(info, even, [keep])], ahead_blocks, step)
            ahead_blocks = [up_m, lax.ppermute(passed, "cols", CHIPS_ON[1])]
        before = [] if last else ahead_blocks
        weights, lower, gram = cayley(info, up, even, other, [value] + along(value, ALONG_Z), before, last)

    rotated, frame, column_scale = rotate_final(info, weights, gram, own_blocks + other_blocks, rows, step)
    return rotated, frame.reshape(2 * basis_rows, PAIR), column_scale.reshape(PAIR)


def solution(mesh):
    in_specs = (P("cols", "rows", None),)
    out_specs = (P(None, "rows", "cols"), P("rows", "cols"), P("cols"))
    return jax.shard_map(body, mesh=mesh, in_specs=in_specs, out_specs=out_specs, check_vma=False)
```

```python
import functools

import jax
import jax.numpy as jnp
from jax import lax
from jax.experimental import pallas as pl
from jax.experimental.pallas import tpu as pltpu
from jax.sharding import PartitionSpec as P

ROUNDS = 4
BLOCK = 128
PAIR = 256
SIDE = 4
ROWS = 16
COLS = 8
F32 = jnp.float32
BF16 = jnp.bfloat16
AHEAD_COST = 180
VMEM_LIMIT = 16 * 1024 * 1024

TURN_CORE = [(c, c ^ 1) for c in range(COLS)]
NEXT_SLOT = [(c, (c + 1) % COLS) for c in range(COLS)]
CHIPS_ON = [[(c, (c + 2 * k) % COLS) for c in range(COLS)] for k in range(SIDE)]
ODD_TO_EVEN = [(c, (c + 1) % COLS) for c in range(1, COLS, 2)]
ODD_TO_ODD = [(c, (c + 2) % COLS) for c in range(1, COLS, 2)]
EVEN_TO_ODD = [(c, c + 1) for c in range(0, COLS, 2)]
ALONG_X = [[(r, r - r % SIDE + (r + k) % SIDE) for r in range(ROWS)] for k in range(1, SIDE)]
ALONG_Z = [[(r, (r + SIDE * k) % ROWS) for r in range(ROWS)] for k in range(1, SIDE)]


def mm(left, right):
    return jnp.dot(left, right, precision=lax.Precision.HIGHEST, preferred_element_type=F32)


def mm_t(left, right):
    return lax.dot_general(
        left, right, (((0,), (0,)), ((), ())), precision=lax.Precision.HIGHEST, preferred_element_type=F32
    )


def parts_of(value):
    high = value.astype(BF16)
    return high, (value - high.astype(F32)).astype(BF16)


def dot(left, right, axis):
    return lax.dot_general(left, right, (((axis,), (0,)), ((), ())), preferred_element_type=F32)


def mm3(left, right, axis=1):
    high, low = parts_of(left)
    right_high, right_low = parts_of(right)
    width = right.shape[1]
    if width < PAIR:
        both = dot(high, jnp.concatenate([right_high, right_low], axis=1), axis)
        return both[:, :width] + (both[:, width:] + dot(low, right_high, axis))
    return dot(high, right_high, axis) + (dot(high, right_low, axis) + dot(low, right_high, axis))


def call(kernel, grid, in_specs, out_specs, out_shape, scalars=0, scratch=(), flops=0, nbytes=0):
    return pl.pallas_call(
        kernel,
        grid_spec=pltpu.PrefetchScalarGridSpec(
            num_scalar_prefetch=scalars,
            grid=grid,
            in_specs=in_specs,
            out_specs=out_specs,
            scratch_shapes=list(scratch),
        ),
        out_shape=out_shape,
        compiler_params=pltpu.CompilerParams(vmem_limit_bytes=VMEM_LIMIT),
        cost_estimate=pl.CostEstimate(flops=flops, bytes_accessed=nbytes, transcendentals=0),
    )


def call_whole(kernel, args, out_shape, before=(), scratch=(), flops=0, nbytes=0):
    inner = kernel
    if before:
        inner = lambda *refs: kernel(*refs[: len(args)], *refs[len(args) + len(before):])
    return pl.pallas_call(
        inner,
        in_specs=[pl.BlockSpec(memory_space=pltpu.SMEM)]
        + [pl.BlockSpec(memory_space=pltpu.VMEM)] * (len(args) - 1)
        + [pl.BlockSpec(memory_space=pl.ANY)] * len(before),
        out_specs=[pl.BlockSpec(memory_space=pltpu.VMEM)] * len(out_shape),
        out_shape=out_shape,
        scratch_shapes=list(scratch),
        compiler_params=pltpu.CompilerParams(vmem_limit_bytes=VMEM_LIMIT),
        cost_estimate=pl.CostEstimate(flops=flops, bytes_accessed=nbytes, transcendentals=0),
    )(*args, *before)


def shape(*dims):
    return jax.ShapeDtypeStruct(dims, F32)


def whole(*dims):
    return pl.BlockSpec(dims, lambda *_: (0,) * len(dims))


def pack_main_kernel(info_ref, x_ref, *refs):
    outs, sems = refs[:SIDE], refs[SIDE]
    copies = []
    for k, out_ref in enumerate(outs):
        first = lax.rem(info_ref[1] + k, SIDE) * 2 * PAIR
        for j in range(4):
            at = pl.multiple_of(first + j * BLOCK, BLOCK)
            target = out_ref.at[j // 2, j % 2]
            copies.append(pltpu.make_async_copy(x_ref.at[:, pl.ds(at, BLOCK)], target, sems.at[4 * k + j]))
    for copy in copies:
        copy.start()
    for copy in copies:
        copy.wait()


def pack_main(info, x):
    rows = x.shape[0]
    return pl.pallas_call(
        pack_main_kernel,
        in_specs=[pl.BlockSpec(memory_space=pltpu.SMEM), pl.BlockSpec(memory_space=pl.ANY)],
        out_specs=[pl.BlockSpec(memory_space=pltpu.VMEM)] * SIDE,
        out_shape=[shape(2, 2, rows, BLOCK)] * SIDE,
        scratch_shapes=[pltpu.SemaphoreType.DMA((4 * SIDE,))],
        compiler_params=pltpu.CompilerParams(vmem_limit_bytes=VMEM_LIMIT),
        cost_estimate=pl.CostEstimate(flops=0, bytes_accessed=8 * SIDE * rows * 2 * PAIR, transcendentals=0),
    )(info, x)


def pack_ahead_kernel(info_ref, *refs):
    for x_ref, out_ref in zip(refs[:SIDE], refs[-SIDE:]):
        out_ref[0] = x_ref[:, :BLOCK]
        out_ref[1] = x_ref[:, BLOCK:]


def pack_ahead(info, x, before):
    rows = x.shape[0]

    def columns(k):
        return pl.BlockSpec((rows, PAIR), lambda i, c: (0, (2 * ((c[1] + k) % SIDE) + COLS - 1) % COLS))

    return call(
        pack_ahead_kernel,
        (1,),
        [columns(k) for k in range(SIDE)] + [pl.BlockSpec(memory_space=pl.ANY)] * len(before),
        [whole(2, rows, BLOCK)] * SIDE,
        [shape(2, rows, BLOCK)] * SIDE,
        scalars=1,
        nbytes=8 * SIDE * rows * PAIR,
    )(info, *[x] * SIDE, *before)


def gram_kernel(info_ref, *refs):
    keep_ref, send_ref = refs[-2:]
    first = info_ref[0] == 0
    grams = []
    for slot in range(2):
        squares = jnp.zeros((PAIR, PAIR), F32)
        mixed = jnp.zeros((PAIR, PAIR), F32)
        for ref in refs[:-2]:
            high, low = parts_of(jnp.concatenate([ref[slot, 0], ref[slot, 1]], axis=1))
            squares = squares + dot(high, high, 0)
            mixed = mixed + dot(high, low, 0)
        grams.append(squares + (mixed + mixed.T))
    rows = lax.broadcasted_iota(jnp.int32, (BLOCK, BLOCK), 0)
    columns = lax.broadcasted_iota(jnp.int32, (BLOCK, BLOCK), 1)
    for ref, gram in ((keep_ref, jnp.where(first, grams[0], grams[1])), (send_ref, jnp.where(first, grams[1], grams[0]))):
        low = gram[BLOCK:, BLOCK:]
        diagonal = jnp.sum(jnp.where(rows == columns, low, 0.0), axis=0, keepdims=True)
        ref[:BLOCK] = gram[:BLOCK, BLOCK:]
        ref[BLOCK:PAIR] = jnp.where(rows <= columns, gram[:BLOCK, :BLOCK], low)
        ref[PAIR:] = jnp.broadcast_to(diagonal, (8, BLOCK))


def unpacked(packed):
    rows = lax.broadcasted_iota(jnp.int32, (BLOCK, BLOCK), 0)
    columns = lax.broadcasted_iota(jnp.int32, (BLOCK, BLOCK), 1)
    triangles = packed[BLOCK:PAIR]
    turned = triangles.T
    up = jnp.where(rows <= columns, triangles, turned)
    low = jnp.where(rows > columns, triangles, jnp.where(rows < columns, turned, packed[PAIR : PAIR + 1]))
    return up, packed[:BLOCK], low


def first_grams(info, main):
    out = shape(PAIR + 8, BLOCK)
    return call_whole(
        gram_kernel, (info, *main), [out, out], flops=2 * 2 * 4 * main[0].size * PAIR, nbytes=16 * main[0].size
    )


def sum_kernel(info_ref, *refs):
    refs[-1][...] = (refs[0][...] + refs[1][...]) + (refs[2][...] + refs[3][...])


def sum_parts(info, parts, before):
    return call_whole(sum_kernel, (info, *parts), [shape(*parts[0].shape)], before, nbytes=20 * parts[0].size)[0]


def rotation_of(gram, x_ref, r_ref):
    rows = lax.broadcasted_iota(jnp.int32, (PAIR, PAIR), 0)
    columns = lax.broadcasted_iota(jnp.int32, (PAIR, PAIR), 1)
    eye = (rows == columns).astype(F32)
    on_diagonal = gram * eye
    across = jnp.sum(on_diagonal, axis=0, keepdims=True)
    down = jnp.sum(on_diagonal, axis=1, keepdims=True)
    spread = across - down
    totals = across + down
    skew = gram * spread / (2.0 * spread * spread + 0.5 * totals * totals)
    square = mm3(skew, skew)
    bound = jnp.max(jnp.sum(jnp.abs(square), axis=0))
    scale = 2.0 / (2.0 + bound)
    x_ref[...] = scale * (eye + skew)
    r_ref[...] = (1.0 - scale) * eye + scale * square

    def step(size):
        left = r_ref[...]
        x = x_ref[...]
        x_ref[...] = x + mm3(x, left)
        r_ref[...] = mm3(left, left)
        return size * size

    lax.while_loop(lambda size: size > 3e-4, step, bound / (2.0 + bound))
    x = x_ref[...]
    x = x + mm3(x, eye - x + mm3(skew, x))
    return 2.0 * x - eye


def cayley_kernel(fill, info_ref, *refs):
    weights_ref, lower_ref, gram_ref, x_ref, r_ref = refs[-5:]
    up, cross, low = fill(info_ref, *refs[:-5])
    gram_ref[:BLOCK, :BLOCK] = up
    gram_ref[:BLOCK, BLOCK:] = cross
    gram_ref[BLOCK:, :BLOCK] = cross.T
    gram_ref[BLOCK:, BLOCK:] = low
    weights = rotation_of(gram_ref[...], x_ref, r_ref)
    weights_ref[:PAIR] = weights
    lower_ref[...] = weights[:, BLOCK:]
    if weights_ref.shape[0] > PAIR:
        turned = mm3(weights[:, BLOCK:], mm3(gram_ref[...], weights[:, BLOCK:]), 0)
        weights_ref[PAIR:, :BLOCK] = turned[: BLOCK // 2]
        weights_ref[PAIR:, BLOCK:] = turned[BLOCK // 2 :]


def cayley_call(fill, args, before=(), last=False):
    return call_whole(
        functools.partial(cayley_kernel, fill),
        args,
        [shape(PAIR if last else PAIR + BLOCK // 2, PAIR), shape(PAIR, BLOCK), shape(PAIR, PAIR)],
        before,
        scratch=[pltpu.VMEM((PAIR, PAIR), F32)] * 2,
        flops=2 * 3 * 8 * PAIR**3,
        nbytes=16 * PAIR * PAIR,
    )


def total_of(part_refs):
    first, second, third, fourth = (ref[...] for ref in part_refs)
    return (first + second) + (third + fourth)


def first_cayley(info, parts, before):
    return cayley_call(lambda _, *part_refs: unpacked(total_of(part_refs)), (info, *parts), before)


def cayley(info, up, even, other, parts, before, last):
    def fill(info_ref, up_ref, even_ref, other_ref, *part_refs):
        folded = jnp.where(info_ref[0] == 0, even_ref[PAIR:], other_ref[PAIR:])
        low = jnp.concatenate([folded[:, :BLOCK], folded[:, BLOCK:]], axis=0)
        return up_ref[...], total_of(part_refs), low

    return cayley_call(fill, (info, up, even, other, *parts), before, last)


def project_kernel(info_ref, gram_ref, weights_ref, up_ref):
    weights = weights_ref[:PAIR, :BLOCK]
    up_ref[...] = mm3(weights, mm3(gram_ref[...], weights), 0)


def project(info, gram, weights):
    out = [shape(BLOCK, BLOCK)]
    return call_whole(project_kernel, (info, gram, weights), out, flops=2 * 3 * PAIR**3, nbytes=12 * PAIR * PAIR)[0]


def start_pair(info_ref, step, group, slot, up, low):
    share = step - up.shape[0]
    column = slot * PAIR - info_ref[2] - share * group
    rows = lax.broadcasted_iota(jnp.int32, (share, PAIR), 0)
    columns = lax.broadcasted_iota(jnp.int32, (share, PAIR), 1)
    basis = (rows == columns + column).astype(F32)
    return jnp.concatenate([jnp.concatenate([up, low], axis=1), basis], axis=0)


def groups_of(info_ref, step, refs, slots):
    if refs[0].shape[0] == SIDE:
        for group in range(SIDE):
            pairs = [(refs[2 * j][group], refs[2 * j + 1][group]) for j in range(len(slots))]
            yield group, [jnp.concatenate(pair, axis=1) for pair in pairs]
    else:
        for k, ref in enumerate(refs):
            group = lax.rem(info_ref[1] + SIDE - k, SIDE)
            yield group, [start_pair(info_ref, step, group, slot, ref[j, 0], ref[j, 1]) for j, slot in enumerate(slots)]


def own_kernel(rows, step, info_ref, own_ref, other_ref, *refs):
    up0_ref, up1_ref, low1_ref, cross_ref = refs[-4:]
    first = info_ref[0] == 0
    weights0 = jnp.where(first, own_ref[:PAIR], other_ref[:PAIR])
    weights1 = jnp.where(first, other_ref[:PAIR, :BLOCK], own_ref[:PAIR, :BLOCK])
    slot = 2 * info_ref[1]
    cross = jnp.zeros((BLOCK, BLOCK), F32)
    for group, (pair0, pair1) in groups_of(info_ref, step, refs[:-4], (slot, slot + 1)):
        turned = mm3(pair0, weights0)
        up1 = mm3(pair1, weights1)
        up0_ref[group] = turned[:, :BLOCK]
        low1_ref[group] = turned[:, BLOCK:]
        up1_ref[group] = up1
        cross = cross + mm3(up1[:rows], turned[:rows, BLOCK:], 0)
    cross_ref[...] = cross


def rotate_own(info, own, other, blocks, rows, step):
    return call_whole(
        functools.partial(own_kernel, rows, step),
        (info, own, other, *blocks),
        [shape(SIDE, step, BLOCK)] * 3 + [shape(BLOCK, BLOCK)],
        flops=2 * 3 * SIDE * step * 4 * BLOCK * PAIR,
        nbytes=4 * 7 * SIDE * step * BLOCK,
    )


def ahead_kernel(rows, step, info_ref, even_ref, odd_ref, cross_ref, up0_ref, *refs):
    low0_ref, keep_ref, send_ref = refs[-3:]
    weights = even_ref[:PAIR, BLOCK:] + odd_ref[...]
    slot = (2 * info_ref[1] + COLS - 1) % COLS
    total = jnp.zeros((BLOCK, BLOCK), F32)
    for group, (pair,) in groups_of(info_ref, step, refs[:-3], (slot,)):
        low0 = mm3(pair, weights)
        low0_ref[group] = low0
        total = total + mm3(up0_ref[group, :rows], low0[:rows], 0)
    first = info_ref[0] == 0
    keep_ref[...] = jnp.where(first, total, cross_ref[...])
    send_ref[...] = jnp.where(first, cross_ref[...], total)


def rotate_ahead(info, even, odd, cross, up0, blocks, rows, step):
    return call_whole(
        functools.partial(ahead_kernel, rows, step),
        (info, even, odd, cross, up0, *blocks),
        [shape(SIDE, step, BLOCK), shape(BLOCK, BLOCK), shape(BLOCK, BLOCK)],
        flops=AHEAD_COST * SIDE * step * BLOCK * PAIR,
        nbytes=4 * 4 * SIDE * step * BLOCK,
    )


def up_kernel(step, info_ref, even_ref, odd_ref, *refs):
    up_ref = refs[-1]
    weights = even_ref[:PAIR, :BLOCK] + odd_ref[...]
    slot = (2 * info_ref[1] + COLS - 1) % COLS
    for group, (pair,) in groups_of(info_ref, step, refs[:-1], (slot,)):
        up_ref[group] = mm3(pair, weights)


def rotate_up(info, ahead, blocks, step):
    return call_whole(
        functools.partial(up_kernel, step),
        (info, *ahead, *blocks),
        [shape(SIDE, step, BLOCK)],
        flops=2 * 3 * SIDE * step * BLOCK * PAIR,
        nbytes=4 * 3 * SIDE * step * BLOCK,
    )[0]


def other_slot_kernel(info_ref, up0_ref, low0_ref, up1_ref, low1_ref, up_ref, low_ref):
    first = info_ref[0] == 0
    up_ref[...] = jnp.where(first, up1_ref[...], up0_ref[...])
    low_ref[...] = jnp.where(first, low1_ref[...], low0_ref[...])


def other_slot(info, blocks, before):
    return call_whole(other_slot_kernel, (info, *blocks), [shape(*blocks[0].shape)] * 2, before, nbytes=24 * blocks[0].size)


def final_kernel(rows, total, info_ref, weights_ref, gram_ref, up0_ref, low0_ref, up1_ref, low1_ref, ru_ref, rl_ref,
                 out_ref, frame_ref, scale_ref):
    weights = weights_ref[...]
    first = info_ref[0] == 0
    i = pl.program_id(0)
    up = jnp.where(first, up0_ref[i], up1_ref[i])
    low = jnp.where(first, low0_ref[i], low1_ref[i])
    mine = mm3(jnp.concatenate([up, low], axis=1), weights)
    theirs = mm3(jnp.concatenate([ru_ref[i], rl_ref[i]], axis=1), weights)
    for k, turned in enumerate((jnp.where(first, mine, theirs), jnp.where(first, theirs, mine))):
        out_ref[k] = turned[:rows]
        frame_ref[k] = turned[rows:]

    @pl.when(i == 0)
    def _():
        squares = jnp.sum(weights * mm3(gram_ref[...], weights), axis=0, keepdims=True)
        scale_ref[...] = jnp.sqrt(squares / total)


def rotate_final(info, weights, gram, blocks, rows, step):
    share = step - rows
    return call(
        functools.partial(final_kernel, rows, float(rows * COLS * ROWS)),
        (SIDE,),
        [pl.BlockSpec(memory_space=pltpu.VMEM)] * 8,
        [
            pl.BlockSpec((2, rows, PAIR), lambda i, c: (i, 0, 0)),
            pl.BlockSpec((2, share, PAIR), lambda i, c: (0, i, 0)),
            whole(1, PAIR),
        ],
        [shape(COLS, rows, PAIR), shape(2, SIDE * share, PAIR), shape(1, PAIR)],
        scalars=1,
        flops=2 * 3 * 2 * SIDE * step * PAIR * PAIR,
        nbytes=4 * 4 * SIDE * step * PAIR,
    )(info, weights, gram, *blocks)


def swap_core(value):
    return lax.ppermute(value, "cols", TURN_CORE)


def along(value, shifts):
    return [lax.ppermute(value, "rows", pairs) for pairs in shifts]


def upper_kernel(info_ref, value_ref, out_ref):
    out_ref[...] = value_ref[:PAIR, :BLOCK]


def relayed_upper(info, even, before):
    upper = call_whole(upper_kernel, (info, even), [shape(PAIR, BLOCK)], before, nbytes=8 * PAIR * BLOCK)[0]
    return lax.ppermute(upper, "cols", EVEN_TO_ODD)


def body(sensitivity):
    x = sensitivity[0]
    rows = x.shape[0]
    column = lax.axis_index("cols")
    parity = column % 2
    basis_rows = x.shape[1] // ROWS // 2
    basis_at = (lax.axis_index("rows") * 2 + parity) * basis_rows
    info = jnp.stack([parity, column // 2, basis_at]).astype(jnp.int32)
    step = rows + basis_rows // SIDE

    packed = pack_main(info, x)
    main = [packed[0]] + [lax.ppermute(packed[k], "cols", CHIPS_ON[k]) for k in range(1, SIDE)]

    keep, send = first_grams(info, main)
    packed = pack_ahead(info, x, main[1:])
    ahead = [packed[0]] + [lax.ppermute(packed[k], "cols", CHIPS_ON[k]) for k in range(1, SIDE)]
    value = keep + swap_core(send)
    value = sum_parts(info, [value] + along(value, ALONG_X), [])
    weights, lower, gram = first_cayley(info, [value] + along(value, ALONG_Z), ahead[1:])

    own_blocks = main
    ahead_blocks = [value[None] for value in ahead]
    for sweep_round in range(ROUNDS - 1):
        last = sweep_round == ROUNDS - 2
        odd = lax.ppermute(lower, "cols", ODD_TO_ODD)
        even = lax.ppermute(weights, "cols", ODD_TO_EVEN)
        other = swap_core(weights)
        up = project(info, gram, weights)
        up0, up1, low1, cross = rotate_own(info, weights, other, own_blocks, rows, step)
        low0, keep, send = rotate_ahead(info, even, odd, cross, up0, ahead_blocks, rows, step)
        value = keep + swap_core(send)
        value = value + sum(along(value, ALONG_X))
        own_blocks = [up0, low0, up1, low1]
        if last:
            other_blocks = [swap_core(block) for block in other_slot(info, own_blocks, [value])]
        else:
            up_m = rotate_up(info, [even, relayed_upper(info, even, [keep])], ahead_blocks, step)
            ahead_blocks = [up_m, lax.ppermute(low1, "cols", CHIPS_ON[1])]
        before = [] if last else ahead_blocks
        weights, lower, gram = cayley(info, up, even, other, [value] + along(value, ALONG_Z), before, last)

    rotated, frame, column_scale = rotate_final(info, weights, gram, own_blocks + other_blocks, rows, step)
    return rotated, frame.reshape(2 * basis_rows, PAIR), column_scale.reshape(PAIR)


def solution(mesh):
    in_specs = (P("cols", "rows", None),)
    out_specs = (P(None, "rows", "cols"), P("rows", "cols"), P("cols"))
    return jax.shard_map(body, mesh=mesh, in_specs=in_specs, out_specs=out_specs, check_vma=False)
```

```python
import functools

import jax
import jax.numpy as jnp
from jax import lax
from jax.experimental import pallas as pl
from jax.experimental.pallas import tpu as pltpu
from jax.sharding import PartitionSpec as P

ROUNDS = 4
BLOCK = 128
PAIR = 256
SIDE = 4
ROWS = 16
COLS = 8
F32 = jnp.float32
BF16 = jnp.bfloat16
AHEAD_COST = 180
VMEM_LIMIT = 16 * 1024 * 1024

TURN_CORE = [(c, c ^ 1) for c in range(COLS)]
NEXT_SLOT = [(c, (c + 1) % COLS) for c in range(COLS)]
CHIPS_ON = [[(c, (c + 2 * k) % COLS) for c in range(COLS)] for k in range(SIDE)]
ODD_TO_EVEN = [(c, (c + 1) % COLS) for c in range(1, COLS, 2)]
ODD_TO_ODD = [(c, (c + 2) % COLS) for c in range(1, COLS, 2)]
EVEN_TO_ODD = [(c, c + 1) for c in range(0, COLS, 2)]
ALONG_X = [[(r, r - r % SIDE + (r + k) % SIDE) for r in range(ROWS)] for k in range(1, SIDE)]
ALONG_Z = [[(r, (r + SIDE * k) % ROWS) for r in range(ROWS)] for k in range(1, SIDE)]


def mm(left, right):
    return jnp.dot(left, right, precision=lax.Precision.HIGHEST, preferred_element_type=F32)


def mm_t(left, right):
    return lax.dot_general(
        left, right, (((0,), (0,)), ((), ())), precision=lax.Precision.HIGHEST, preferred_element_type=F32
    )


def parts_of(value):
    high = value.astype(BF16)
    return high, (value - high.astype(F32)).astype(BF16)


def dot(left, right, axis):
    return lax.dot_general(left, right, (((axis,), (0,)), ((), ())), preferred_element_type=F32)


def mm3(left, right, axis=1):
    high, low = parts_of(left)
    right_high, right_low = parts_of(right)
    width = right.shape[1]
    if width < PAIR:
        both = dot(high, jnp.concatenate([right_high, right_low], axis=1), axis)
        return both[:, :width] + (both[:, width:] + dot(low, right_high, axis))
    return dot(high, right_high, axis) + (dot(high, right_low, axis) + dot(low, right_high, axis))


def call(kernel, grid, in_specs, out_specs, out_shape, scalars=0, scratch=(), flops=0, nbytes=0):
    return pl.pallas_call(
        kernel,
        grid_spec=pltpu.PrefetchScalarGridSpec(
            num_scalar_prefetch=scalars,
            grid=grid,
            in_specs=in_specs,
            out_specs=out_specs,
            scratch_shapes=list(scratch),
        ),
        out_shape=out_shape,
        compiler_params=pltpu.CompilerParams(vmem_limit_bytes=VMEM_LIMIT),
        cost_estimate=pl.CostEstimate(flops=flops, bytes_accessed=nbytes, transcendentals=0),
    )


def call_whole(kernel, args, out_shape, before=(), scratch=(), flops=0, nbytes=0):
    inner = kernel
    if before:
        inner = lambda *refs: kernel(*refs[: len(args)], *refs[len(args) + len(before):])
    return pl.pallas_call(
        inner,
        in_specs=[pl.BlockSpec(memory_space=pltpu.SMEM)]
        + [pl.BlockSpec(memory_space=pltpu.VMEM)] * (len(args) - 1)
        + [pl.BlockSpec(memory_space=pl.ANY)] * len(before),
        out_specs=[pl.BlockSpec(memory_space=pltpu.VMEM)] * len(out_shape),
        out_shape=out_shape,
        scratch_shapes=list(scratch),
        compiler_params=pltpu.CompilerParams(vmem_limit_bytes=VMEM_LIMIT),
        cost_estimate=pl.CostEstimate(flops=flops, bytes_accessed=nbytes, transcendentals=0),
    )(*args, *before)


def shape(*dims):
    return jax.ShapeDtypeStruct(dims, F32)


def whole(*dims):
    return pl.BlockSpec(dims, lambda *_: (0,) * len(dims))


def pack_main_kernel(info_ref, x_ref, *refs):
    outs, sems = refs[:SIDE], refs[SIDE]
    copies = []
    for k, out_ref in enumerate(outs):
        first = lax.rem(info_ref[1] + k, SIDE) * 2 * PAIR
        for j in range(4):
            at = pl.multiple_of(first + j * BLOCK, BLOCK)
            target = out_ref.at[j // 2, j % 2]
            copies.append(pltpu.make_async_copy(x_ref.at[:, pl.ds(at, BLOCK)], target, sems.at[4 * k + j]))
    for copy in copies:
        copy.start()
    for copy in copies:
        copy.wait()


def pack_main(info, x):
    rows = x.shape[0]
    return pl.pallas_call(
        pack_main_kernel,
        in_specs=[pl.BlockSpec(memory_space=pltpu.SMEM), pl.BlockSpec(memory_space=pltpu.HBM)],
        out_specs=[pl.BlockSpec(memory_space=pltpu.VMEM)] * SIDE,
        out_shape=[shape(2, 2, rows, BLOCK)] * SIDE,
        scratch_shapes=[pltpu.SemaphoreType.DMA((4 * SIDE,))],
        compiler_params=pltpu.CompilerParams(vmem_limit_bytes=VMEM_LIMIT),
        cost_estimate=pl.CostEstimate(flops=0, bytes_accessed=8 * SIDE * rows * 2 * PAIR, transcendentals=0),
    )(info, pltpu.with_memory_space_constraint(x, pltpu.HBM))


def pack_ahead_kernel(info_ref, *refs):
    for x_ref, out_ref in zip(refs[:SIDE], refs[-SIDE:]):
        out_ref[0] = x_ref[:, :BLOCK]
        out_ref[1] = x_ref[:, BLOCK:]


def pack_ahead(info, x, before):
    rows = x.shape[0]

    def columns(k):
        return pl.BlockSpec((rows, PAIR), lambda i, c: (0, (2 * ((c[1] + k) % SIDE) + COLS - 1) % COLS))

    return call(
        pack_ahead_kernel,
        (1,),
        [columns(k) for k in range(SIDE)] + [pl.BlockSpec(memory_space=pl.ANY)] * len(before),
        [whole(2, rows, BLOCK)] * SIDE,
        [shape(2, rows, BLOCK)] * SIDE,
        scalars=1,
        nbytes=8 * SIDE * rows * PAIR,
    )(info, *[x] * SIDE, *before)


def gram_kernel(info_ref, *refs):
    keep_ref, send_ref = refs[-2:]
    first = info_ref[0] == 0
    grams = []
    for slot in range(2):
        squares = jnp.zeros((PAIR, PAIR), F32)
        mixed = jnp.zeros((PAIR, PAIR), F32)
        for ref in refs[:-2]:
            high, low = parts_of(jnp.concatenate([ref[slot, 0], ref[slot, 1]], axis=1))
            squares = squares + dot(high, high, 0)
            mixed = mixed + dot(high, low, 0)
        grams.append(squares + (mixed + mixed.T))
    rows = lax.broadcasted_iota(jnp.int32, (BLOCK, BLOCK), 0)
    columns = lax.broadcasted_iota(jnp.int32, (BLOCK, BLOCK), 1)
    for ref, gram in ((keep_ref, jnp.where(first, grams[0], grams[1])), (send_ref, jnp.where(first, grams[1], grams[0]))):
        low = gram[BLOCK:, BLOCK:]
        diagonal = jnp.sum(jnp.where(rows == columns, low, 0.0), axis=0, keepdims=True)
        ref[:BLOCK] = gram[:BLOCK, BLOCK:]
        ref[BLOCK:PAIR] = jnp.where(rows <= columns, gram[:BLOCK, :BLOCK], low)
        ref[PAIR:] = jnp.broadcast_to(diagonal, (8, BLOCK))


def unpacked(packed):
    rows = lax.broadcasted_iota(jnp.int32, (BLOCK, BLOCK), 0)
    columns = lax.broadcasted_iota(jnp.int32, (BLOCK, BLOCK), 1)
    triangles = packed[BLOCK:PAIR]
    turned = triangles.T
    up = jnp.where(rows <= columns, triangles, turned)
    low = jnp.where(rows > columns, triangles, jnp.where(rows < columns, turned, packed[PAIR : PAIR + 1]))
    return up, packed[:BLOCK], low


def first_grams(info, main):
    out = shape(PAIR + 8, BLOCK)
    return call_whole(
        gram_kernel, (info, *main), [out, out], flops=2 * 2 * 4 * main[0].size * PAIR, nbytes=16 * main[0].size
    )


def sum_kernel(info_ref, *refs):
    refs[-1][...] = (refs[0][...] + refs[1][...]) + (refs[2][...] + refs[3][...])


def sum_parts(info, parts):
    return call_whole(sum_kernel, (info, *parts), [shape(*parts[0].shape)], nbytes=20 * parts[0].size)[0]


def rotation_of(gram, x_ref, r_ref):
    rows = lax.broadcasted_iota(jnp.int32, (PAIR, PAIR), 0)
    columns = lax.broadcasted_iota(jnp.int32, (PAIR, PAIR), 1)
    eye = (rows == columns).astype(F32)
    on_diagonal = gram * eye
    across = jnp.sum(on_diagonal, axis=0, keepdims=True)
    down = jnp.sum(on_diagonal, axis=1, keepdims=True)
    spread = across - down
    totals = across + down
    skew = gram * spread / (2.0 * spread * spread + 0.5 * totals * totals)
    square = mm3(skew, skew)
    bound = jnp.max(jnp.sum(jnp.abs(square), axis=0))
    scale = 2.0 / (2.0 + bound)
    x_ref[...] = scale * (eye + skew)
    r_ref[...] = (1.0 - scale) * eye + scale * square

    def step(size):
        left = r_ref[...]
        x = x_ref[...]
        x_ref[...] = x + mm3(x, left)
        r_ref[...] = mm3(left, left)
        return size * size

    lax.while_loop(lambda size: size > 3e-4, step, bound / (2.0 + bound))
    x = x_ref[...]
    x = x + mm3(x, eye - x + mm3(skew, x))
    return 2.0 * x - eye


def cayley_kernel(fill, info_ref, *refs):
    weights_ref, lower_ref, gram_ref, x_ref, r_ref = refs[-5:]
    up, cross, low = fill(info_ref, *refs[:-5])
    gram_ref[:BLOCK, :BLOCK] = up
    gram_ref[:BLOCK, BLOCK:] = cross
    gram_ref[BLOCK:, :BLOCK] = cross.T
    gram_ref[BLOCK:, BLOCK:] = low
    weights = rotation_of(gram_ref[...], x_ref, r_ref)
    weights_ref[:PAIR] = weights
    lower_ref[...] = weights[:, BLOCK:]
    if weights_ref.shape[0] > PAIR:
        turned = mm3(weights[:, BLOCK:], mm3(gram_ref[...], weights[:, BLOCK:]), 0)
        weights_ref[PAIR:, :BLOCK] = turned[: BLOCK // 2]
        weights_ref[PAIR:, BLOCK:] = turned[BLOCK // 2 :]


def cayley_call(fill, args, before=(), last=False):
    return call_whole(
        functools.partial(cayley_kernel, fill),
        args,
        [shape(PAIR if last else PAIR + BLOCK // 2, PAIR), shape(PAIR, BLOCK), shape(PAIR, PAIR)],
        before,
        scratch=[pltpu.VMEM((PAIR, PAIR), F32)] * 2,
        flops=2 * 3 * 8 * PAIR**3,
        nbytes=16 * PAIR * PAIR,
    )


def total_of(part_refs):
    first, second, third, fourth = (ref[...] for ref in part_refs)
    return (first + second) + (third + fourth)


def first_cayley(info, parts, before):
    return cayley_call(lambda _, *part_refs: unpacked(total_of(part_refs)), (info, *parts), before)


def cayley(info, up, even, other, parts, before, last):
    def fill(info_ref, up_ref, even_ref, other_ref, *part_refs):
        folded = jnp.where(info_ref[0] == 0, even_ref[PAIR:], other_ref[PAIR:])
        low = jnp.concatenate([folded[:, :BLOCK], folded[:, BLOCK:]], axis=0)
        return up_ref[...], total_of(part_refs), low

    return cayley_call(fill, (info, up, even, other, *parts), before, last)


def project_kernel(info_ref, gram_ref, weights_ref, up_ref):
    weights = weights_ref[:PAIR, :BLOCK]
    up_ref[...] = mm3(weights, mm3(gram_ref[...], weights), 0)


def project(info, gram, weights):
    out = [shape(BLOCK, BLOCK)]
    return call_whole(project_kernel, (info, gram, weights), out, flops=2 * 3 * PAIR**3, nbytes=12 * PAIR * PAIR)[0]


def start_pair(info_ref, step, group, slot, up, low):
    share = step - up.shape[0]
    column = slot * PAIR - info_ref[2] - share * group
    rows = lax.broadcasted_iota(jnp.int32, (share, PAIR), 0)
    columns = lax.broadcasted_iota(jnp.int32, (share, PAIR), 1)
    basis = (rows == columns + column).astype(F32)
    return jnp.concatenate([jnp.concatenate([up, low], axis=1), basis], axis=0)


def groups_of(info_ref, step, refs, slots):
    if refs[0].shape[0] == SIDE:
        for group in range(SIDE):
            pairs = [(refs[2 * j][group], refs[2 * j + 1][group]) for j in range(len(slots))]
            yield group, [jnp.concatenate(pair, axis=1) for pair in pairs]
    else:
        for k, ref in enumerate(refs):
            group = lax.rem(info_ref[1] + SIDE - k, SIDE)
            yield group, [start_pair(info_ref, step, group, slot, ref[j, 0], ref[j, 1]) for j, slot in enumerate(slots)]


def own_kernel(rows, step, info_ref, own_ref, other_ref, *refs):
    up0_ref, up1_ref, low1_ref, cross_ref = refs[-4:]
    first = info_ref[0] == 0
    weights0 = jnp.where(first, own_ref[:PAIR], other_ref[:PAIR])
    weights1 = jnp.where(first, other_ref[:PAIR, :BLOCK], own_ref[:PAIR, :BLOCK])
    slot = 2 * info_ref[1]
    cross = jnp.zeros((BLOCK, BLOCK), F32)
    for group, (pair0, pair1) in groups_of(info_ref, step, refs[:-4], (slot, slot + 1)):
        turned = mm3(pair0, weights0)
        up1 = mm3(pair1, weights1)
        up0_ref[group] = turned[:, :BLOCK]
        low1_ref[group] = turned[:, BLOCK:]
        up1_ref[group] = up1
        cross = cross + mm3(up1[:rows], turned[:rows, BLOCK:], 0)
    cross_ref[...] = cross


def rotate_own(info, own, other, blocks, before, rows, step):
    return call_whole(
        functools.partial(own_kernel, rows, step),
        (info, own, other, *blocks),
        [shape(SIDE, step, BLOCK)] * 3 + [shape(BLOCK, BLOCK)],
        before,
        flops=2 * 3 * SIDE * step * 4 * BLOCK * PAIR,
        nbytes=4 * 7 * SIDE * step * BLOCK,
    )


def ahead_kernel(rows, step, info_ref, even_ref, odd_ref, cross_ref, up0_ref, *refs):
    low0_ref, keep_ref, send_ref = refs[-3:]
    weights = even_ref[:PAIR, BLOCK:] + odd_ref[...]
    slot = (2 * info_ref[1] + COLS - 1) % COLS
    total = jnp.zeros((BLOCK, BLOCK), F32)
    for group, (pair,) in groups_of(info_ref, step, refs[:-3], (slot,)):
        low0 = mm3(pair, weights)
        low0_ref[group] = low0
        total = total + mm3(up0_ref[group, :rows], low0[:rows], 0)
    first = info_ref[0] == 0
    keep_ref[...] = jnp.where(first, total, cross_ref[...])
    send_ref[...] = jnp.where(first, cross_ref[...], total)


def rotate_ahead(info, even, odd, cross, up0, blocks, rows, step):
    return call_whole(
        functools.partial(ahead_kernel, rows, step),
        (info, even, odd, cross, up0, *blocks),
        [shape(SIDE, step, BLOCK), shape(BLOCK, BLOCK), shape(BLOCK, BLOCK)],
        flops=AHEAD_COST * SIDE * step * BLOCK * PAIR,
        nbytes=4 * 4 * SIDE * step * BLOCK,
    )


def up_kernel(step, info_ref, even_ref, odd_ref, *refs):
    up_ref = refs[-1]
    weights = even_ref[:PAIR, :BLOCK] + odd_ref[...]
    slot = (2 * info_ref[1] + COLS - 1) % COLS
    for group, (pair,) in groups_of(info_ref, step, refs[:-1], (slot,)):
        up_ref[group] = mm3(pair, weights)


def rotate_up(info, ahead, blocks, step):
    return call_whole(
        functools.partial(up_kernel, step),
        (info, *ahead, *blocks),
        [shape(SIDE, step, BLOCK)],
        flops=2 * 3 * SIDE * step * BLOCK * PAIR,
        nbytes=4 * 3 * SIDE * step * BLOCK,
    )[0]


def other_slot_kernel(info_ref, up0_ref, low0_ref, up1_ref, low1_ref, up_ref, low_ref):
    first = info_ref[0] == 0
    up_ref[...] = jnp.where(first, up1_ref[...], up0_ref[...])
    low_ref[...] = jnp.where(first, low1_ref[...], low0_ref[...])


def other_slot(info, blocks, before):
    return call_whole(other_slot_kernel, (info, *blocks), [shape(*blocks[0].shape)] * 2, before, nbytes=24 * blocks[0].size)


def final_kernel(rows, total, info_ref, weights_ref, gram_ref, up0_ref, low0_ref, up1_ref, low1_ref, ru_ref, rl_ref,
                 out_ref, frame_ref, scale_ref):
    weights = weights_ref[...]
    first = info_ref[0] == 0
    i = pl.program_id(0)
    up = jnp.where(first, up0_ref[i], up1_ref[i])
    low = jnp.where(first, low0_ref[i], low1_ref[i])
    mine = mm3(jnp.concatenate([up, low], axis=1), weights)
    theirs = mm3(jnp.concatenate([ru_ref[i], rl_ref[i]], axis=1), weights)
    for k, turned in enumerate((jnp.where(first, mine, theirs), jnp.where(first, theirs, mine))):
        out_ref[k] = turned[:rows]
        frame_ref[k] = turned[rows:]

    @pl.when(i == 0)
    def _():
        squares = jnp.sum(weights * mm3(gram_ref[...], weights), axis=0, keepdims=True)
        scale_ref[...] = jnp.sqrt(squares / total)


def rotate_final(info, weights, gram, blocks, rows, step):
    share = step - rows
    return call(
        functools.partial(final_kernel, rows, float(rows * COLS * ROWS)),
        (SIDE,),
        [pl.BlockSpec(memory_space=pltpu.VMEM)] * 8,
        [
            pl.BlockSpec((2, rows, PAIR), lambda i, c: (i, 0, 0)),
            pl.BlockSpec((2, share, PAIR), lambda i, c: (0, i, 0)),
            whole(1, PAIR),
        ],
        [shape(COLS, rows, PAIR), shape(2, SIDE * share, PAIR), shape(1, PAIR)],
        scalars=1,
        flops=2 * 3 * 2 * SIDE * step * PAIR * PAIR,
        nbytes=4 * 4 * SIDE * step * PAIR,
    )(info, weights, gram, *blocks)


def swap_core(value):
    return lax.ppermute(value, "cols", TURN_CORE)


def along(value, shifts):
    return [lax.ppermute(value, "rows", pairs) for pairs in shifts]


def upper_kernel(info_ref, value_ref, out_ref):
    out_ref[...] = value_ref[:PAIR, :BLOCK]


def relayed_upper(info, even, before):
    upper = call_whole(upper_kernel, (info, even), [shape(PAIR, BLOCK)], before, nbytes=8 * PAIR * BLOCK)[0]
    return lax.ppermute(upper, "cols", EVEN_TO_ODD)


def body(sensitivity):
    x = sensitivity[0]
    rows = x.shape[0]
    column = lax.axis_index("cols")
    parity = column % 2
    basis_rows = x.shape[1] // ROWS // 2
    basis_at = (lax.axis_index("rows") * 2 + parity) * basis_rows
    info = jnp.stack([parity, column // 2, basis_at]).astype(jnp.int32)
    step = rows + basis_rows // SIDE

    packed = pack_main(info, x)
    main = [packed[0]] + [lax.ppermute(packed[k], "cols", CHIPS_ON[k]) for k in range(1, SIDE)]

    keep, send = first_grams(info, main)
    packed = pack_ahead(info, x, main[1:])
    ahead = [packed[0]] + [lax.ppermute(packed[k], "cols", CHIPS_ON[k]) for k in range(1, SIDE)]
    value = keep + swap_core(send)
    value = sum_parts(info, [value] + along(value, ALONG_X))
    weights, lower, gram = first_cayley(info, [value] + along(value, ALONG_Z), [ahead[1], ahead[3]])

    own_blocks = main
    ahead_blocks = [value[None] for value in ahead]
    for sweep_round in range(ROUNDS - 1):
        last = sweep_round == ROUNDS - 2
        odd = lax.ppermute(lower, "cols", ODD_TO_ODD)
        even = lax.ppermute(weights, "cols", ODD_TO_EVEN)
        other = swap_core(weights)
        up = project(info, gram, weights)
        before = [] if sweep_round else [ahead[2]]
        up0, up1, low1, cross = rotate_own(info, weights, other, own_blocks, before, rows, step)
        low0, keep, send = rotate_ahead(info, even, odd, cross, up0, ahead_blocks, rows, step)
        value = keep + swap_core(send)
        value = value + sum(along(value, ALONG_X))
        own_blocks = [up0, low0, up1, low1]
        if last:
            other_blocks = [swap_core(block) for block in other_slot(info, own_blocks, [value])]
        else:
            up_m = rotate_up(info, [even, relayed_upper(info, even, [keep])], ahead_blocks, step)
            ahead_blocks = [up_m, lax.ppermute(low1, "cols", CHIPS_ON[1])]
        before = [] if last else ahead_blocks
        weights, lower, gram = cayley(info, up, even, other, [value] + along(value, ALONG_Z), before, last)

    rotated, frame, column_scale = rotate_final(info, weights, gram, own_blocks + other_blocks, rows, step)
    return rotated, frame.reshape(2 * basis_rows, PAIR), column_scale.reshape(PAIR)


def solution(mesh):
    in_specs = (P("cols", "rows", None),)
    out_specs = (P(None, "rows", "cols"), P("rows", "cols"), P("cols"))
    return jax.shard_map(body, mesh=mesh, in_specs=in_specs, out_specs=out_specs, check_vma=False)
```
